32 devices in a mesh: prow: 4 (over y, x), pcol: 8 (over z, core).
Axes of the slice: x: 2, y: 2, z: 4, core: 2. Of those that a mesh axis runs over, the one named last changes fastest.
Arguments:
- matrix: float32 [4096, 2048], P('prow', 'pcol'), may hold values from -6 to 6
- l_panels: float32 [2, 4096, 256], P(None, ('prow', 'pcol')), may hold values from -0.375 to 0.375
- l_inverse: float32 [2, 256, 256], replicated, as said below
- pivots: int32 [2, 256], replicated, may hold values from 0 to 4095, as said below
Outputs:
- updated: float32 [4096, 2048], P('prow', 'pcol')
The draws below stay inside these ranges and needn't reach their ends.
Inputs may be any that keep to these rules, and one draw needn't show every extreme that they name: `pivots`: for each step s, entry k is either s * 256 + k or a row at or after (s + 1) * 256; the entries of one step are distinct. `l_inverse`: each block is unit lower triangular.
All inputs are finite; a program needn't handle non-finite values.
Results may differ from the reference program's by a relative error of at most 0.0001.
Values sent between devices are 32-bit elements; how exact they have to be, the bound alone decides.
No kernel may reach another device: no remote copies, remote signals or barrier semaphores. Data moves between devices by JAX's collectives and lax.ppermute only.
A program may use at most 64 MiB of HBM per device.

```python
import jax
import jax.numpy as jnp
from jax import lax

ROWS_DEV = 1024
NB = 256
STEPS = 2
M = 4096
N = 2048


def draw_l_inverse(key, part):
    values = jax.random.normal(key, (STEPS, NB, NB))
    lower = jnp.tril(values, -1) / jnp.sqrt(jnp.float32(NB))
    return (lower + jnp.eye(NB, dtype=jnp.float32)).astype(jnp.float32)


def draw_pivots(key, part):
    row_ids = jnp.arange(M, dtype=jnp.int32)
    owners = M // ROWS_DEV
    block_last = (row_ids + 1) % ROWS_DEV == 0
    result = []
    for step in range(STEPS):
        step_key = jax.random.fold_in(key, 11 + step)
        key_level, key_rank, key_order, key_keep = jax.random.split(step_key, 4)
        level = jax.random.randint(key_level, (owners,), 0, 4)
        owner_level = jnp.repeat(level, ROWS_DEV)
        rank = jax.random.permutation(key_rank, M).astype(jnp.int32)
        score = owner_level * M + rank
        score = jnp.where(block_last, 5 * M + row_ids, score)
        score = jnp.where(row_ids < (step + 1) * NB, -1, score)
        unused, chosen = lax.top_k(score, NB)
        chosen = chosen.astype(jnp.int32)
        order = jax.random.permutation(key_order, NB).astype(jnp.int32)
        place = jnp.argmax(order == NB - 1)
        first = order[0]
        order = order.at[place].set(first).at[0].set(NB - 1)
        chosen = chosen[order]
        forced = (chosen + 1) % ROWS_DEV == 0
        keep = jax.random.randint(key_keep, (NB,), 0, 4) == 0
        keep = keep & jnp.logical_not(forced)
        if step == 0:
            keep = keep.at[0].set(True)
        own_place = step * NB + jnp.arange(NB, dtype=jnp.int32)
        result.append(jnp.where(keep, own_place, chosen))
    return jnp.stack(result).astype(jnp.int32)


def block_levels(stream_key, shape, cuts, low, top_value):
    gain = 1.0
    for position, shards_of in cuts:
        steps = jax.random.uniform(jax.random.fold_in(jax.random.fold_in(stream_key, 6), position), (shards_of,), jnp.float32, low / len(cuts), top_value / len(cuts))
        gain = gain * jnp.repeat(jnp.exp(steps), shape[position] // shards_of).reshape((-1,) + (1,) * (len(shape) - 1 - position))
    return gain


def noise(stream_key, dims, width, reach, pieces=(), kind=jnp.bfloat16):
    values = width * jax.random.normal(stream_key, dims, jnp.float32)
    if pieces:
        values = values * block_levels(stream_key, dims, pieces, -0.22, 0.18)
    return jnp.clip(values, -reach, reach).astype(kind)


def setup_inputs(seed: int = 0) -> dict:
    streams_of = jax.random.split(jax.random.key(seed), 5)
    return {
        "matrix": noise(streams_of[0], (M, N), 1.0, 6.0, ((0, 4), (1, 8)), jnp.float32),
        "l_panels": noise(streams_of[1], (STEPS, M, NB), NB ** -0.5, 0.375, ((1, 32),), jnp.float32),
        "l_inverse": draw_l_inverse(jax.random.fold_in(streams_of[4], 71), 0),
        "pivots": draw_pivots(jax.random.fold_in(streams_of[4], 71), 0),
    }


def reference(matrix, l_panels, l_inverse, pivots):
    current = matrix
    row_ids = jnp.arange(M, dtype=jnp.int32)
    for step in range(STEPS):
        chosen = pivots[step]
        begin = step * NB
        picked = current[chosen]
        old_top = current[begin:begin + NB]
        current = current.at[chosen].set(old_top)
        upper = jnp.dot(l_inverse[step], picked, precision=lax.Precision.HIGHEST, preferred_element_type=jnp.float32)
        current = current.at[begin:begin + NB].set(upper)
        below = (row_ids >= begin + NB)[:, None]
        factor = jnp.where(below, l_panels[step], jnp.float32(0.0))
        current = current - jnp.dot(factor, upper, precision=lax.Precision.HIGHEST, preferred_element_type=jnp.float32)
    return current
```

```python
import functools

import jax
import jax.numpy as jnp
from jax import lax
from jax.experimental import pallas as pl
from jax.experimental.pallas import tpu as pltpu
from jax.sharding import PartitionSpec as P

VMEM = pl.BlockSpec(memory_space=pltpu.VMEM)
SMEM = pl.BlockSpec(memory_space=pltpu.SMEM)
GRANT = pltpu.CompilerParams(vmem_limit_bytes=40 * 1024 * 1024)
F32 = jnp.float32


def split(values):
    high = values.astype(jnp.bfloat16)
    low = (values - high.astype(F32)).astype(jnp.bfloat16)
    return high, low


def dot(left, right):
    product = functools.partial(jnp.dot, preferred_element_type=F32)
    return product(left[0], right[0]) + (product(left[0], right[1]) + product(left[1], right[0]))


def slot_rows(source, pivots, step, width, rows_dev, out):
    row = lax.axis_index("prow")
    first = row * rows_dev
    begin = step * width

    def body(k, carry):
        offset = pivots[step, k] - first
        owned = (offset >= 0) & (offset < rows_dev)
        place = jnp.where(owned, offset, jnp.where(row == 0, begin + k, 0))
        out[pl.ds(k, 1), :] = source[pl.ds(place, 1), :]
        return carry

    lax.fori_loop(0, width, body, 0, unroll=8)


def first_slots(rows_dev, width, matrix, pivots, out):
    slot_rows(matrix, pivots, 0, width, rows_dev, out)


def merge(schedule, stage, sent, received, owner, outs):
    row = lax.axis_index("prow")
    start = 0
    for half, bits in enumerate(schedule):
        bit = bits[stage]
        known = sum(bits[:stage])
        partner = row ^ bit
        rows = sent[half].shape[0]
        who = owner[start : start + rows, :]
        keep = ~known
        theirs = ((who ^ partner) & keep) == 0
        neither = ((who ^ row) & ~(known | bit)) != 0
        take = theirs | (neither & ((partner & keep) == 0))
        outs[half][...] = jnp.where(take, received[half][...], sent[half][...])
        start += rows


def merge_kernel(schedule, stage, *refs):
    merge(schedule, stage, refs[0:2], refs[2:4], refs[4], refs[5:7])


def swap_and_solve(schedule, step, width, rows_dev, inverse, pivots, sent, received, owner, picked, displaced, current):
    row = lax.axis_index("prow")
    first = row * rows_dev
    begin = step * width
    stages = len(schedule[0])
    start = 0
    for half, bits in enumerate(schedule):
        rows = sent[half].shape[0]
        part = slice(start, start + rows)
        bit = bits[-1]
        mine = ((owner[part, :] ^ row) & bit) == 0
        picked[part, :] = jnp.where(mine, sent[half][...], received[stages - 1][half][...])
        value = received[stages - 1][half][...]
        for stage in reversed(range(stages - 1)):
            reached = (row & ~sum(bits[: stage + 1])) == 0
            value = jnp.where(reached, received[stage][half][...], value)
        displaced[part, :] = value
        start += rows

    @pl.when(row != 0)
    def _():
        def body(k, carry):
            offset = pivots[step, k] - first

            @pl.when((offset >= 0) & (offset < rows_dev))
            def _():
                current[pl.ds(offset, 1), :] = displaced[pl.ds(k, 1), :]

            return carry

        lax.fori_loop(0, width, body, 0, unroll=8)

    upper = dot(split(inverse[step]), split(picked[...]))

    @pl.when(row == 0)
    def _():
        displaced[...] = current[begin : begin + width, :]

        def body(k, carry):
            offset = pivots[step, k]

            @pl.when(offset < rows_dev)
            def _():
                current[pl.ds(offset, 1), :] = displaced[pl.ds(k, 1), :]

            return carry

        lax.fori_loop(0, width, body, 0, unroll=8)
        current[begin : begin + width, :] = upper

    return upper


def update_kernel(schedule, step, steps, width, matrix, pivots, inverse, owner, *refs):
    rows_dev = matrix.shape[0]
    stages = len(schedule[0])
    refs = list(refs)
    sent = [refs.pop(0) for _ in schedule]
    received = [[refs.pop(0) for _ in schedule] for _ in range(stages)]
    last = step == steps - 1
    picked, displaced = refs[-2:]
    outs = refs[-3:-2] if last else refs[-4:-2]
    blocks = refs[: -3 if last else -4]
    current = outs[0]
    current[...] = matrix[...]
    upper = swap_and_solve(
        schedule, step, width, rows_dev, inverse, pivots, sent, received, owner, picked, displaced, current
    )
    upper = split(upper)
    row = lax.axis_index("prow")
    col = lax.axis_index("pcol")
    pairs = len(blocks) // 2
    limit = (step + 1) * width
    for distance in range(pairs):
        chip = lax.rem(col // 2 - distance + pairs, pairs)
        for side in range(2):
            core = (col % 2) if side == 0 else 1 - (col % 2)
            block = blocks[side * pairs + distance]
            rows = block.shape[0]
            start = pl.multiple_of((chip * 2 + core) * rows, rows)
            index = row * rows_dev + start + lax.broadcasted_iota(jnp.int32, block.shape, 0)
            factor = jnp.where(index >= limit, block[...], F32(0))
            current[pl.ds(start, rows), :] -= dot(split(factor), upper)
    if not last:
        slot_rows(current, pivots, step + 1, width, rows_dev, outs[1])


def gather_panel(block, count):
    onward = [(i, (i + 2) % count) for i in range(count)]
    across = [(i, i ^ 1) for i in range(count)]
    own = [block]
    for _ in range(count // 2 - 1):
        own.append(lax.ppermute(own[-1], "pcol", onward))
    return own + [lax.ppermute(piece, "pcol", across) for piece in own]


def per_device(mesh, matrix, l_panels, l_inverse, pivots):
    rows_dev, columns = matrix.shape
    steps, width = pivots.shape
    process_rows, process_columns = mesh.shape["prow"], mesh.shape["pcol"]
    bits = [1 << b for b in range(process_rows.bit_length() - 1)]
    schedule = (tuple(bits), tuple(reversed(bits)))
    half = width // 2
    shape = jax.ShapeDtypeStruct
    owner = jnp.broadcast_to((pivots // rows_dev)[:, :, None], (steps, width, columns))

    slots = pl.pallas_call(
        functools.partial(first_slots, rows_dev, width),
        out_shape=shape((width, columns), F32),
        in_specs=[VMEM, SMEM],
        out_specs=VMEM,
        compiler_params=GRANT,
        name="first_slots",
    )(matrix, pivots)
    panels = [gather_panel(l_panels[step], process_columns) for step in range(steps)]
    current = matrix
    for step in range(steps):
        sent = [slots[:half], slots[half:]]
        received = []
        for stage in range(len(bits)):
            if stage:
                sent = pl.pallas_call(
                    functools.partial(merge_kernel, schedule, stage - 1),
                    out_shape=[shape((half, columns), F32)] * 2,
                    in_specs=[VMEM] * 5,
                    out_specs=[VMEM] * 2,
                    compiler_params=GRANT,
                    name="merge",
                )(*sent, *received[-1], owner[step])
            received.append(
                [
                    lax.ppermute(sent[h], "prow", [(i, i ^ schedule[h][stage]) for i in range(process_rows)])
                    for h in range(2)
                ]
            )
        last = step == steps - 1
        outs = [shape((rows_dev, columns), F32)] + ([] if last else [shape((width, columns), F32)])
        operands = [matrix if step == 0 else current, pivots, l_inverse, owner[step], *sent]
        operands += [piece for pair in received for piece in pair] + panels[step]
        result = pl.pallas_call(
            functools.partial(update_kernel, schedule, step, steps, width),
            out_shape=outs,
            in_specs=[VMEM, SMEM] + [VMEM] * (len(operands) - 2),
            out_specs=[VMEM] * len(outs),
            scratch_shapes=[pltpu.VMEM((width, columns), F32), pltpu.VMEM((width, columns), F32)],
            compiler_params=GRANT,
            name="update",
        )(*operands)
        current = result[0]
        slots = None if last else result[1]
    return current


def solution(mesh):
    placed = (P("prow", "pcol"), P(None, ("prow", "pcol"), None), P(), P())
    return jax.shard_map(
        functools.partial(per_device, mesh), mesh=mesh, in_specs=placed, out_specs=P("prow", "pcol"), check_vma=False
    )
```

```python
import functools

import jax
import jax.numpy as jnp
from jax import lax
from jax.experimental import pallas as pl
from jax.experimental.pallas import tpu as pltpu
from jax.sharding import PartitionSpec as P

VMEM = pl.BlockSpec(memory_space=pltpu.VMEM)
HBM = pl.BlockSpec(memory_space=pltpu.HBM)
GRANT = pltpu.CompilerParams(vmem_limit_bytes=40 * 1024 * 1024)
F32 = jnp.float32
BF16 = jnp.bfloat16
NOWHERE = -(1 << 24)


def product(left, right):
    return jnp.dot(left, right, preferred_element_type=F32)


def split(values):
    high = values.astype(BF16)
    low = (values - high.astype(F32)).astype(BF16)
    return high, low


def dot(left, right):
    return product(left[0], right[0]) + (product(left[0], right[1]) + product(left[1], right[0]))


def pick(chosen, right):
    return product(chosen, right[0]) + product(chosen, right[1])


def one_hot(left, right):
    return jnp.where(left == right, F32(1), F32(0)).astype(BF16)


def iota(shape, dimension):
    return lax.broadcasted_iota(jnp.int32, shape, dimension)


def column_of(row):
    n = row.shape[1]
    spread = jnp.where(iota((n, n), 0) == iota((n, n), 1), row.astype(F32), F32(0))
    return jnp.sum(spread, axis=1, keepdims=True).astype(jnp.int32)


def local_rows(pivots, step, rows_dev):
    offset = pivots[step : step + 1, :] - lax.axis_index("prow") * rows_dev
    return jnp.where((offset >= 0) & (offset < rows_dev), offset, NOWHERE)


def slot_rows(pivots, step, rows_dev):
    offset = local_rows(pivots, step, rows_dev)
    width = offset.shape[1]
    top = jnp.where(lax.axis_index("prow") == 0, step * width + iota(offset.shape, 1), NOWHERE)
    return jnp.where(offset >= 0, offset, top)


def first_slots(matrix, pivots, out, held, chosen, sems):
    chunks = sems.shape[0] - 1
    rows_dev = held.shape[0]
    rows = rows_dev // chunks
    copies = [pltpu.make_async_copy(pivots, chosen, sems.at[chunks])]
    for c in range(chunks):
        part = pl.ds(c * rows, rows)
        copies.append(pltpu.make_async_copy(matrix.at[part, :], held.at[part, :], sems.at[c]))
    for copy in copies:
        copy.start()
    copies[0].wait()
    place = column_of(slot_rows(chosen, 0, rows_dev))
    total = None
    for c in range(chunks):
        copies[1 + c].wait()
        gather = one_hot(place, iota((place.shape[0], rows), 1) + c * rows)
        term = pick(gather, split(held[c * rows : (c + 1) * rows, :]))
        total = term if total is None else total + term
    out[...] = total


def prepare(matrix, pivots, base, ahead, places):
    rows_dev = matrix.shape[0]
    offset = local_rows(pivots, 0, rows_dev)
    width = offset.shape[1]
    place = column_of(slot_rows(pivots, 1, rows_dev))
    places[...] = jnp.broadcast_to(place, places.shape)
    total = None
    for start in range(0, rows_dev, width):
        hit = jnp.where(offset == iota((width, width), 0) + start, F32(1), F32(0))
        keep = jnp.sum(hit, axis=1, keepdims=True) == 0
        kept = jnp.where(keep, matrix[start : start + width, :], F32(0))
        base[start : start + width, :] = kept
        gather = one_hot(place, iota((width, width), 1) + start)
        term = pick(gather, split(kept))
        total = term if total is None else total + term
    ahead[...] = total


def stage_bits(bits, stage):
    odd = lax.rem(lax.axis_index("pcol"), 2) == 1
    bit = jnp.where(odd, bits[len(bits) - 1 - stage], bits[stage])
    known = jnp.where(odd, sum(bits[len(bits) - stage :]) if stage else 0, sum(bits[:stage]))
    return bit, known


def merge(bits, stage, sent, received, owner, out):
    row = lax.axis_index("prow")
    bit, known = stage_bits(bits, stage)
    partner = row ^ bit
    who = owner[...]
    keep = ~known
    theirs = ((who ^ partner) & keep) == 0
    neither = ((who ^ row) & ~(known | bit)) != 0
    take = theirs | (neither & ((partner & keep) == 0))
    out[...] = jnp.where(take, received[...], sent[...])


def picked_rows(bits, sent, received, owner):
    bit, _ = stage_bits(bits, len(bits) - 1)
    mine = ((owner[...] ^ lax.axis_index("prow")) & bit) == 0
    return jnp.where(mine, sent[...], received[-1][...])


def displaced_rows(bits, received, top):
    row = lax.axis_index("prow")
    value = received[-1][...]
    for stage in reversed(range(len(bits) - 1)):
        bit, known = stage_bits(bits, stage)
        value = jnp.where((row & ~(known | bit)) == 0, received[stage][...], value)
    return jnp.where(row == 0, top, value)


def block_start(position, blocks):
    pairs = len(blocks) // 2
    side, distance = divmod(position, pairs)
    col = lax.axis_index("pcol")
    chip = lax.rem(col // 2 - distance + pairs, pairs)
    core = lax.rem(col, 2) if side == 0 else 1 - lax.rem(col, 2)
    rows = blocks[position].shape[0]
    return pl.multiple_of((chip * 2 + core) * rows, rows)


def solve(bits, step, matrix, pivots, inverse, owner, ahead, places, sent, *refs):
    refs = list(refs)
    received = [refs.pop(0) for _ in bits]
    blocks, (upper_out, displaced_out, slots_out) = refs[:-3], refs[-3:]
    rows_dev = matrix.shape[0]
    picked = picked_rows(bits, sent, received, owner)
    width = picked.shape[0]
    upper = dot(split(inverse[step]), split(picked))
    upper_out[...] = upper
    displaced = displaced_rows(bits, received, matrix[step * width : (step + 1) * width, :])
    displaced_out[...] = displaced
    high = low = None
    for position, block in enumerate(blocks):
        rows = block.shape[0]
        local = places[:, :rows] - block_start(position, blocks)
        gather = one_hot(local, iota((width, rows), 1))
        block_high, block_low = split(block[...])
        term_high, term_low = product(gather, block_high), product(gather, block_low)
        high = term_high if high is None else high + term_high
        low = term_low if low is None else low + term_low
    moved = one_hot(places[...], local_rows(pivots, step, rows_dev))
    factor = (high.astype(BF16), low.astype(BF16))
    slots_out[...] = ahead[...] + (pick(moved, split(displaced)) - dot(factor, split(upper)))


def assemble(step, blocks, rows_dev, width, high, low):
    limit = (step + 1) * width - lax.axis_index("prow") * rows_dev
    for position, block in enumerate(blocks):
        rows = block.shape[0]
        start = block_start(position, blocks)
        below = start + iota(block.shape, 0) >= limit
        block_high, block_low = split(jnp.where(below, -block[...], F32(0)))
        high[pl.ds(start, rows), :] = block_high
        low[pl.ds(start, rows), :] = block_low


def update(step, base, pivots, upper_in, displaced_in, top, *refs):
    blocks, (out, top_out, high, low) = refs[:-4], refs[-4:]
    rows_dev = base.shape[0]
    width = upper_in.shape[0]
    assemble(step, blocks, rows_dev, width, high, low)
    offset = local_rows(pivots, step, rows_dev)
    later = local_rows(pivots, step + 1, rows_dev)
    upper = split(upper_in[...])
    displaced = split(displaced_in[...])
    for start in range(0, rows_dev, width):
        part = slice(start, start + width)
        rows = iota((width, width), 0) + start
        value = base[part, :] + (pick(one_hot(rows, offset), displaced) + dot((high[part, :], low[part, :]), upper))
        if start == step * width:
            value = jnp.where(lax.axis_index("prow") == 0, upper_in[...], value)
        if start == (step + 1) * width:
            top_out[...] = value
        hit = jnp.where(later == rows, F32(1), F32(0))
        out[part, :] = jnp.where(jnp.sum(hit, axis=1, keepdims=True) == 0, value, F32(0))


def finish(bits, step, base, pivots, inverse, owner, top, sent, *refs):
    refs = list(refs)
    received = [refs.pop(0) for _ in bits]
    blocks, (out, high, low, result, sems) = refs[:-5], refs[-5:]
    rows_dev = base.shape[0]
    picked = picked_rows(bits, sent, received, owner)
    width = picked.shape[0]
    upper_full = dot(split(inverse[step]), split(picked))
    assemble(step, blocks, rows_dev, width, high, low)
    offset = local_rows(pivots, step, rows_dev)
    upper = split(upper_full)
    displaced = split(displaced_rows(bits, received, top[...]))
    copies = []
    for start in range(0, rows_dev, width):
        part = slice(start, start + width)
        rows = iota((width, width), 0) + start
        value = base[part, :] + (pick(one_hot(rows, offset), displaced) + dot((high[part, :], low[part, :]), upper))
        if start == step * width:
            value = jnp.where(lax.axis_index("prow") == 0, upper_full, value)
        result[part, :] = value
        copies.append(
            pltpu.make_async_copy(result.at[pl.ds(start, width), :], out.at[pl.ds(start, width), :], sems.at[len(copies)])
        )
        copies[-1].start()
    for copy in copies:
        copy.wait()


def gather_panel(block, count):
    across = [(i, i ^ 1) for i in range(count)]
    own = [block]
    for distance in range(1, count // 2):
        own.append(lax.ppermute(block, "pcol", [(i, (i + 2 * distance) % count) for i in range(count)]))
    return own + [lax.ppermute(piece, "pcol", across) for piece in own]


def per_device(mesh, matrix, l_panels, l_inverse, pivots):
    rows_dev, columns = matrix.shape
    steps, width = pivots.shape
    process_rows, process_columns = mesh.shape["prow"], mesh.shape["pcol"]
    bits = [1 << b for b in range(process_rows.bit_length() - 1)]
    shape = jax.ShapeDtypeStruct
    square = shape((width, columns), F32)
    full = shape((rows_dev, columns), F32)

    def call(kernel, name, operands, outs, specs=None, out_specs=None, scratch=()):
        return pl.pallas_call(
            kernel,
            out_shape=outs,
            in_specs=specs or [VMEM] * len(operands),
            out_specs=out_specs or jax.tree.map(lambda _: VMEM, outs),
            scratch_shapes=scratch,
            compiler_params=GRANT,
            name=name,
        )(*operands)

    def exchange(sent, step):
        received = []
        for stage in range(len(bits)):
            if stage:
                sent = call(functools.partial(merge, bits, stage - 1), "merge", [sent, received[-1], owner[step]], square)
            pairs = []
            for i in range(process_rows):
                for j in range(process_columns):
                    bit = bits[len(bits) - 1 - stage] if j % 2 else bits[stage]
                    pairs.append((i * process_columns + j, (i ^ bit) * process_columns + j))
            received.append(lax.ppermute(sent, ("prow", "pcol"), pairs))
        return sent, received

    owner = jnp.broadcast_to((pivots // rows_dev)[:, :, None], (steps, width, columns))
    chunks = rows_dev // width
    halves = [pltpu.VMEM((rows_dev, l_panels.shape[2]), BF16)] * 2
    slots = call(
        first_slots,
        "first_slots",
        [matrix, pivots],
        square,
        specs=[HBM, HBM],
        scratch=[
            pltpu.VMEM((rows_dev, columns), F32),
            pltpu.VMEM((steps, width), jnp.int32),
            pltpu.SemaphoreType.DMA((chunks + 1,)),
        ],
    )
    sent, received = exchange(slots, 0)
    panels = [gather_panel(l_panels[step], process_columns) for step in range(steps)]
    base, ahead, places = call(
        prepare, "prepare", [matrix, pivots], [full, square, shape((width, width), jnp.int32)]
    )
    upper, displaced, slots = call(
        functools.partial(solve, bits, 0),
        "solve",
        [matrix, pivots, l_inverse, owner[0], ahead, places, sent, *received, *panels[0]],
        [square] * 3,
    )
    sent, received = exchange(slots, 1)
    base, top = call(
        functools.partial(update, 0),
        "update",
        [base, pivots, upper, displaced, matrix, *panels[0]],
        [full, square],
        scratch=halves,
    )
    return call(
        functools.partial(finish, bits, 1),
        "finish",
        [base, pivots, l_inverse, owner[1], top, sent, *received, *panels[1]],
        full,
        out_specs=HBM,
        scratch=halves + [pltpu.VMEM((rows_dev, columns), F32), pltpu.SemaphoreType.DMA((chunks,))],
    )


def solution(mesh):
    placed = (P("prow", "pcol"), P(None, ("prow", "pcol"), None), P(), P())
    return jax.shard_map(
        functools.partial(per_device, mesh), mesh=mesh, in_specs=placed, out_specs=P("prow", "pcol"), check_vma=False
    )
```

```python
import functools

import jax
import jax.numpy as jnp
from jax import lax
from jax.experimental import pallas as pl
from jax.experimental.pallas import tpu as pltpu
from jax.sharding import PartitionSpec as P

VMEM = pl.BlockSpec(memory_space=pltpu.VMEM)
ANY = pl.BlockSpec(memory_space=pl.ANY)
HBM = pl.BlockSpec(memory_space=pltpu.HBM)
GRANT = pltpu.CompilerParams(vmem_limit_bytes=40 * 1024 * 1024)
F32 = jnp.float32
BF16 = jnp.bfloat16
NOWHERE = -(1 << 24)


def product(left, right):
    return jnp.dot(left, right, preferred_element_type=F32)


def split(values):
    high = values.astype(BF16)
    low = (values - high.astype(F32)).astype(BF16)
    return high, low


def dot(left, right):
    return product(left[0], right[0]) + (product(left[0], right[1]) + product(left[1], right[0]))


def pick(chosen, right):
    return product(chosen, right[0]) + product(chosen, right[1])


def one_hot(left, right):
    return jnp.where(left == right, F32(1), F32(0)).astype(BF16)


def iota(shape, dimension):
    return lax.broadcasted_iota(jnp.int32, shape, dimension)


def column_of(row):
    n = row.shape[1]
    spread = jnp.where(iota((n, n), 0) == iota((n, n), 1), row.astype(F32), F32(0))
    return jnp.sum(spread, axis=1, keepdims=True).astype(jnp.int32)


def local_rows(pivots, step, rows_dev):
    offset = pivots[step : step + 1, :] - lax.axis_index("prow") * rows_dev
    return jnp.where((offset >= 0) & (offset < rows_dev), offset, NOWHERE)


def slot_rows(pivots, step, rows_dev):
    offset = local_rows(pivots, step, rows_dev)
    width = offset.shape[1]
    top = jnp.where(lax.axis_index("prow") == 0, step * width + iota(offset.shape, 1), NOWHERE)
    return jnp.where(offset >= 0, offset, top)


def first_slots(matrix, pivots, panels, out, panel, held, chosen, sems):
    chunks = sems.shape[0] - 2
    rows_dev = held.shape[0]
    rows = rows_dev // chunks
    copies = [pltpu.make_async_copy(pivots, chosen, sems.at[chunks])]
    for c in range(chunks):
        part = pl.ds(c * rows, rows)
        copies.append(pltpu.make_async_copy(matrix.at[part, :], held.at[part, :], sems.at[c]))
    copies.append(pltpu.make_async_copy(panels.at[0], panel, sems.at[chunks + 1]))
    for copy in copies:
        copy.start()
    copies[0].wait()
    place = column_of(slot_rows(chosen, 0, rows_dev))
    total = None
    for c in range(chunks):
        copies[1 + c].wait()
        gather = one_hot(place, iota((place.shape[0], rows), 1) + c * rows)
        term = pick(gather, split(held[c * rows : (c + 1) * rows, :]))
        total = term if total is None else total + term
    out[...] = total
    copies[-1].wait()


def prepare(matrix, pivots, panels, arrived, base, ahead, places, panel, sem):
    copy = pltpu.make_async_copy(panels.at[1], panel, sem)
    copy.start()
    rows_dev = matrix.shape[0]
    offset = local_rows(pivots, 0, rows_dev)
    width = offset.shape[1]
    place = column_of(slot_rows(pivots, 1, rows_dev))
    places[...] = jnp.broadcast_to(place, places.shape)
    total = None
    for start in range(0, rows_dev, width):
        hit = jnp.where(offset == iota((width, width), 0) + start, F32(1), F32(0))
        keep = jnp.sum(hit, axis=1, keepdims=True) == 0
        kept = jnp.where(keep, matrix[start : start + width, :], F32(0))
        base[start : start + width, :] = kept
        gather = one_hot(place, iota((width, width), 1) + start)
        term = pick(gather, split(kept))
        total = term if total is None else total + term
    ahead[...] = total
    copy.wait()


def stage_bits(bits, stage):
    odd = lax.rem(lax.axis_index("pcol"), 2) == 1
    bit = jnp.where(odd, bits[len(bits) - 1 - stage], bits[stage])
    known = jnp.where(odd, sum(bits[len(bits) - stage :]) if stage else 0, sum(bits[:stage]))
    return bit, known


def merge(bits, stage, sent, received, owner, out):
    row = lax.axis_index("prow")
    bit, known = stage_bits(bits, stage)
    partner = row ^ bit
    who = owner[...]
    keep = ~known
    theirs = ((who ^ partner) & keep) == 0
    neither = ((who ^ row) & ~(known | bit)) != 0
    take = theirs | (neither & ((partner & keep) == 0))
    out[...] = jnp.where(take, received[...], sent[...])


def picked_rows(bits, sent, received, owner):
    bit, _ = stage_bits(bits, len(bits) - 1)
    mine = ((owner[...] ^ lax.axis_index("prow")) & bit) == 0
    return jnp.where(mine, sent[...], received[-1][...])


def displaced_rows(bits, received, top):
    row = lax.axis_index("prow")
    value = received[-1][...]
    for stage in reversed(range(len(bits) - 1)):
        bit, known = stage_bits(bits, stage)
        value = jnp.where((row & ~(known | bit)) == 0, received[stage][...], value)
    return jnp.where(row == 0, top, value)


def block_start(position, blocks):
    pairs = len(blocks) // 2
    side, distance = divmod(position, pairs)
    col = lax.axis_index("pcol")
    chip = lax.rem(col // 2 - distance + pairs, pairs)
    core = lax.rem(col, 2) if side == 0 else 1 - lax.rem(col, 2)
    rows = blocks[position].shape[0]
    return pl.multiple_of((chip * 2 + core) * rows, rows)


def solve(bits, step, matrix, pivots, inverse, owner, ahead, places, sent, *refs):
    refs = list(refs)
    received = [refs.pop(0) for _ in bits]
    blocks, (upper_out, displaced_out, slots_out) = refs[:-3], refs[-3:]
    rows_dev = matrix.shape[0]
    picked = picked_rows(bits, sent, received, owner)
    width = picked.shape[0]
    upper = dot(split(inverse[step]), split(picked))
    upper_out[...] = upper
    displaced = displaced_rows(bits, received, matrix[step * width : (step + 1) * width, :])
    displaced_out[...] = displaced
    high = low = None
    for position, block in enumerate(blocks):
        rows = block.shape[0]
        local = places[:, :rows] - block_start(position, blocks)
        gather = one_hot(local, iota((width, rows), 1))
        block_high, block_low = split(block[...])
        term_high, term_low = product(gather, block_high), product(gather, block_low)
        high = term_high if high is None else high + term_high
        low = term_low if low is None else low + term_low
    moved = one_hot(places[...], local_rows(pivots, step, rows_dev))
    factor = (high.astype(BF16), low.astype(BF16))
    slots_out[...] = ahead[...] + (pick(moved, split(displaced)) - dot(factor, split(upper)))


def assemble(step, blocks, rows_dev, width, high, low):
    limit = (step + 1) * width - lax.axis_index("prow") * rows_dev
    for position, block in enumerate(blocks):
        rows = block.shape[0]
        start = block_start(position, blocks)
        below = start + iota(block.shape, 0) >= limit
        block_high, block_low = split(jnp.where(below, -block[...], F32(0)))
        high[pl.ds(start, rows), :] = block_high
        low[pl.ds(start, rows), :] = block_low


def update(step, base, pivots, upper_in, displaced_in, top, *refs):
    blocks, (out, top_out, high, low) = refs[:-4], refs[-4:]
    rows_dev = base.shape[0]
    width = upper_in.shape[0]
    assemble(step, blocks, rows_dev, width, high, low)
    offset = local_rows(pivots, step, rows_dev)
    later = local_rows(pivots, step + 1, rows_dev)
    upper = split(upper_in[...])
    displaced = split(displaced_in[...])
    for start in range(0, rows_dev, width):
        part = slice(start, start + width)
        rows = iota((width, width), 0) + start
        value = base[part, :] + (pick(one_hot(rows, offset), displaced) + dot((high[part, :], low[part, :]), upper))
        if start == step * width:
            value = jnp.where(lax.axis_index("prow") == 0, upper_in[...], value)
        if start == (step + 1) * width:
            top_out[...] = value
        hit = jnp.where(later == rows, F32(1), F32(0))
        out[part, :] = jnp.where(jnp.sum(hit, axis=1, keepdims=True) == 0, value, F32(0))


def finish(bits, step, base, pivots, inverse, owner, top, sent, *refs):
    refs = list(refs)
    received = [refs.pop(0) for _ in bits]
    blocks, (out, high, low, result, sems) = refs[:-5], refs[-5:]
    rows_dev = base.shape[0]
    picked = picked_rows(bits, sent, received, owner)
    width = picked.shape[0]
    upper_full = dot(split(inverse[step]), split(picked))
    assemble(step, blocks, rows_dev, width, high, low)
    offset = local_rows(pivots, step, rows_dev)
    upper = split(upper_full)
    displaced = split(displaced_rows(bits, received, top[...]))
    copies = []
    for start in range(0, rows_dev, width):
        part = slice(start, start + width)
        rows = iota((width, width), 0) + start
        value = base[part, :] + (pick(one_hot(rows, offset), displaced) + dot((high[part, :], low[part, :]), upper))
        if start == step * width:
            value = jnp.where(lax.axis_index("prow") == 0, upper_full, value)
        result[part, :] = value
        copies.append(
            pltpu.make_async_copy(result.at[pl.ds(start, width), :], out.at[pl.ds(start, width), :], sems.at[len(copies)])
        )
        copies[-1].start()
    for copy in copies:
        copy.wait()


def release(panel, before, out):
    out[...] = panel[...]


def gather_panel(block, later, count):
    across = [(i, i ^ 1) for i in range(count)]
    chips = count // 2
    own = [block]
    for distance in range(1, chips):
        sent = block if distance == chips // 2 else later
        own.append(lax.ppermute(sent, "pcol", [(i, (i + 2 * distance) % count) for i in range(count)]))
    return own + [lax.ppermute(piece, "pcol", across) for piece in own]


def per_device(mesh, matrix, l_panels, l_inverse, pivots):
    rows_dev, columns = matrix.shape
    steps, width = pivots.shape
    process_rows, process_columns = mesh.shape["prow"], mesh.shape["pcol"]
    bits = [1 << b for b in range(process_rows.bit_length() - 1)]
    shape = jax.ShapeDtypeStruct
    square = shape((width, columns), F32)
    full = shape((rows_dev, columns), F32)

    def call(kernel, name, operands, outs, specs=None, out_specs=None, scratch=()):
        return pl.pallas_call(
            kernel,
            out_shape=outs,
            in_specs=specs or [VMEM] * len(operands),
            out_specs=out_specs or jax.tree.map(lambda _: VMEM, outs),
            scratch_shapes=scratch,
            compiler_params=GRANT,
            name=name,
        )(*operands)

    def exchange(sent, step):
        received = []
        for stage in range(len(bits)):
            if stage:
                sent = call(functools.partial(merge, bits, stage - 1), "merge", [sent, received[-1], owner[step]], square)
            pairs = []
            for i in range(process_rows):
                for j in range(process_columns):
                    bit = bits[len(bits) - 1 - stage] if j % 2 else bits[stage]
                    pairs.append((i * process_columns + j, (i ^ bit) * process_columns + j))
            received.append(lax.ppermute(sent, ("prow", "pcol"), pairs))
        return sent, received

    owner = jnp.broadcast_to((pivots // rows_dev)[:, :, None], (steps, width, columns))
    chunks = rows_dev // width
    halves = [pltpu.VMEM((rows_dev, l_panels.shape[2]), BF16)] * 2
    panel_block = shape(l_panels.shape[1:], F32)
    slots, panel, matrix = call(
        first_slots,
        "first_slots",
        [pltpu.with_memory_space_constraint(x, pltpu.HBM) for x in (matrix, pivots, l_panels)],
        [square, panel_block, full],
        specs=[HBM] * 3,
        scratch=[pltpu.VMEM((steps, width), jnp.int32), pltpu.SemaphoreType.DMA((chunks + 2,))],
    )
    later = call(release, "release", [panel, slots], panel_block, specs=[VMEM, ANY])
    panels = [gather_panel(panel, later, process_columns)]
    sent, received = exchange(slots, 0)
    base, ahead, places, panel = call(
        prepare,
        "prepare",
        [matrix, pivots, l_panels, panels[0][process_columns // 4]],
        [full, square, shape((width, width), jnp.int32), panel_block],
        specs=[VMEM, VMEM, ANY, ANY],
        scratch=[pltpu.SemaphoreType.DMA],
    )
    panels.append(gather_panel(panel, panel, process_columns))
    upper, displaced, slots = call(
        functools.partial(solve, bits, 0),
        "solve",
        [matrix, pivots, l_inverse, owner[0], ahead, places, sent, *received, *panels[0]],
        [square] * 3,
    )
    sent, received = exchange(slots, 1)
    base, top = call(
        functools.partial(update, 0),
        "update",
        [base, pivots, upper, displaced, matrix, *panels[0]],
        [full, square],
        scratch=halves,
    )
    return call(
        functools.partial(finish, bits, 1),
        "finish",
        [base, pivots, l_inverse, owner[1], top, sent, *received, *panels[1]],
        full,
        out_specs=HBM,
        scratch=halves + [pltpu.VMEM((rows_dev, columns), F32), pltpu.SemaphoreType.DMA((chunks,))],
    )


def solution(mesh):
    placed = (P("prow", "pcol"), P(None, ("prow", "pcol"), None), P(), P())
    return jax.shard_map(
        functools.partial(per_device, mesh), mesh=mesh, in_specs=placed, out_specs=P("prow", "pcol"), check_vma=False
    )
```

```python
import functools

import jax
import jax.numpy as jnp
from jax import lax
from jax.experimental import pallas as pl
from jax.experimental.pallas import tpu as pltpu
from jax.sharding import PartitionSpec as P

VMEM = pl.BlockSpec(memory_space=pltpu.VMEM)
ANY = pl.BlockSpec(memory_space=pl.ANY)
HBM = pl.BlockSpec(memory_space=pltpu.HBM)
GRANT = pltpu.CompilerParams(vmem_limit_bytes=40 * 1024 * 1024)
F32 = jnp.float32
BF16 = jnp.bfloat16
NOWHERE = -(1 << 24)
COST = {"update": 4 << 20, "halve": 32 << 20}


def product(left, right):
    return jnp.dot(left, right, preferred_element_type=F32)


def split(values):
    high = values.astype(BF16)
    low = (values - high.astype(F32)).astype(BF16)
    return high, low


def dot(left, right):
    return product(left[0], right[0]) + (product(left[0], right[1]) + product(left[1], right[0]))


def pick(chosen, right):
    return product(chosen, right[0]) + product(chosen, right[1])


def one_hot(left, right):
    return jnp.where(left == right, F32(1), F32(0)).astype(BF16)


def iota(shape, dimension):
    return lax.broadcasted_iota(jnp.int32, shape, dimension)


def column_of(row):
    n = row.shape[1]
    spread = jnp.where(iota((n, n), 0) == iota((n, n), 1), row.astype(F32), F32(0))
    return jnp.sum(spread, axis=1, keepdims=True).astype(jnp.int32)


def local_rows(pivots, step, rows_dev):
    offset = pivots[step : step + 1, :] - lax.axis_index("prow") * rows_dev
    return jnp.where((offset >= 0) & (offset < rows_dev), offset, NOWHERE)


def slot_rows(pivots, step, rows_dev):
    offset = local_rows(pivots, step, rows_dev)
    width = offset.shape[1]
    top = jnp.where(lax.axis_index("prow") == 0, step * width + iota(offset.shape, 1), NOWHERE)
    return jnp.where(offset >= 0, offset, top)


def first_slots(matrix, pivots, panels, out, held, *refs):
    blocks, (chosen, sems) = refs[:-2], refs[-2:]
    chunks = sems.shape[0] - 1 - len(blocks)
    rows_dev = held.shape[0]
    rows = rows_dev // chunks
    copies = [pltpu.make_async_copy(pivots, chosen, sems.at[chunks])]
    for c in range(chunks):
        part = pl.ds(c * rows, rows)
        copies.append(pltpu.make_async_copy(matrix.at[part, :], held.at[part, :], sems.at[c]))
    for step, block in enumerate(blocks):
        copies.append(pltpu.make_async_copy(panels.at[step], block, sems.at[chunks + 1 + step]))
    for copy in copies:
        copy.start()
    copies[0].wait()
    place = column_of(slot_rows(chosen, 0, rows_dev))
    total = None
    for c in range(chunks):
        copies[1 + c].wait()
        gather = one_hot(place, iota((place.shape[0], rows), 1) + c * rows)
        term = pick(gather, split(held[c * rows : (c + 1) * rows, :]))
        total = term if total is None else total + term
    out[...] = total
    for copy in copies[1 + chunks :]:
        copy.wait()


def prepare(matrix, pivots, base, ahead, places):
    rows_dev = matrix.shape[0]
    offset = local_rows(pivots, 0, rows_dev)
    width = offset.shape[1]
    place = column_of(slot_rows(pivots, 1, rows_dev))
    places[...] = jnp.broadcast_to(place, places.shape)
    total = None
    for start in range(0, rows_dev, width):
        hit = jnp.where(offset == iota((width, width), 0) + start, F32(1), F32(0))
        keep = jnp.sum(hit, axis=1, keepdims=True) == 0
        kept = jnp.where(keep, matrix[start : start + width, :], F32(0))
        base[start : start + width, :] = kept
        gather = one_hot(place, iota((width, width), 1) + start)
        term = pick(gather, split(kept))
        total = term if total is None else total + term
    ahead[...] = total


def stage_bits(bits, stage):
    odd = lax.rem(lax.axis_index("pcol"), 2) == 1
    bit = jnp.where(odd, bits[len(bits) - 1 - stage], bits[stage])
    known = jnp.where(odd, sum(bits[len(bits) - stage :]) if stage else 0, sum(bits[:stage]))
    return bit, known


def merge(bits, stage, sent, received, owner, out):
    row = lax.axis_index("prow")
    bit, known = stage_bits(bits, stage)
    partner = row ^ bit
    who = owner[...]
    keep = ~known
    theirs = ((who ^ partner) & keep) == 0
    neither = ((who ^ row) & ~(known | bit)) != 0
    take = theirs | (neither & ((partner & keep) == 0))
    out[...] = jnp.where(take, received[...], sent[...])


def picked_rows(bits, sent, received, owner):
    bit, _ = stage_bits(bits, len(bits) - 1)
    mine = ((owner[...] ^ lax.axis_index("prow")) & bit) == 0
    return jnp.where(mine, sent[...], received[-1][...])


def displaced_rows(bits, received, top):
    row = lax.axis_index("prow")
    value = received[-1][...]
    for stage in reversed(range(len(bits) - 1)):
        bit, known = stage_bits(bits, stage)
        value = jnp.where((row & ~(known | bit)) == 0, received[stage][...], value)
    return jnp.where(row == 0, top, value)


def block_start(position, blocks):
    pairs = len(blocks) // 2
    side, distance = divmod(position, pairs)
    col = lax.axis_index("pcol")
    chip = lax.rem(col // 2 - distance + pairs, pairs)
    core = lax.rem(col, 2) if side == 0 else 1 - lax.rem(col, 2)
    rows = blocks[position].shape[0]
    return pl.multiple_of((chip * 2 + core) * rows, rows)


def solve(bits, step, matrix, pivots, inverse, owner, ahead, places, before, sent, *refs):
    refs = list(refs)
    received = [refs.pop(0) for _ in bits]
    blocks, (upper_out, displaced_out, slots_out) = refs[:-3], refs[-3:]
    rows_dev = matrix.shape[0]
    picked = picked_rows(bits, sent, received, owner)
    width = picked.shape[0]
    upper = dot(split(inverse[step]), split(picked))
    upper_out[...] = upper
    displaced = displaced_rows(bits, received, matrix[step * width : (step + 1) * width, :])
    displaced_out[...] = displaced
    high = low = None
    for position, block in enumerate(blocks):
        rows = block.shape[0]
        local = places[:, :rows] - block_start(position, blocks)
        gather = one_hot(local, iota((width, rows), 1))
        block_high, block_low = split(block[...])
        term_high, term_low = product(gather, block_high), product(gather, block_low)
        high = term_high if high is None else high + term_high
        low = term_low if low is None else low + term_low
    moved = one_hot(places[...], local_rows(pivots, step, rows_dev))
    factor = (high.astype(BF16), low.astype(BF16))
    slots_out[...] = ahead[...] + (pick(moved, split(displaced)) - dot(factor, split(upper)))


def assemble(step, blocks, rows_dev, width, high, low):
    limit = (step + 1) * width - lax.axis_index("prow") * rows_dev
    for position, block in enumerate(blocks):
        rows = block.shape[0]
        start = block_start(position, blocks)
        below = start + iota(block.shape, 0) >= limit
        block_high, block_low = split(jnp.where(below, -block[...], F32(0)))
        high[pl.ds(start, rows), :] = block_high
        low[pl.ds(start, rows), :] = block_low


def halve(step, rows_dev, width, *refs):
    assemble(step, refs[:-2], rows_dev, width, refs[-2], refs[-1])


def update(step, base, pivots, upper_in, displaced_in, top, *refs):
    blocks, (out, top_out, high, low) = refs[:-4], refs[-4:]
    rows_dev = base.shape[0]
    width = upper_in.shape[0]
    assemble(step, blocks, rows_dev, width, high, low)
    offset = local_rows(pivots, step, rows_dev)
    later = local_rows(pivots, step + 1, rows_dev)
    upper = split(upper_in[...])
    displaced = split(displaced_in[...])
    for start in range(0, rows_dev, width):
        part = slice(start, start + width)
        rows = iota((width, width), 0) + start
        value = base[part, :] + (pick(one_hot(rows, offset), displaced) + dot((high[part, :], low[part, :]), upper))
        if start == step * width:
            value = jnp.where(lax.axis_index("prow") == 0, upper_in[...], value)
        if start == (step + 1) * width:
            top_out[...] = value
        hit = jnp.where(later == rows, F32(1), F32(0))
        out[part, :] = jnp.where(jnp.sum(hit, axis=1, keepdims=True) == 0, value, F32(0))


def finish(bits, step, base, pivots, inverse, owner, top, high, low, sent, *refs):
    received, (out, result, sems) = refs[:-3], refs[-3:]
    rows_dev = base.shape[0]
    picked = picked_rows(bits, sent, received, owner)
    width = picked.shape[0]
    upper_full = dot(split(inverse[step]), split(picked))
    offset = local_rows(pivots, step, rows_dev)
    upper = split(upper_full)
    displaced = split(displaced_rows(bits, received, top[...]))
    copies = []
    for start in range(0, rows_dev, width):
        part = slice(start, start + width)
        rows = iota((width, width), 0) + start
        value = base[part, :] + (pick(one_hot(rows, offset), displaced) + dot((high[part, :], low[part, :]), upper))
        if start == step * width:
            value = jnp.where(lax.axis_index("prow") == 0, upper_full, value)
        result[part, :] = value
        copies.append(
            pltpu.make_async_copy(result.at[pl.ds(start, width), :], out.at[pl.ds(start, width), :], sems.at[len(copies)])
        )
        copies[-1].start()
    for copy in copies:
        copy.wait()


def release(panel, before, out):
    out[...] = panel[...]


def gather_panel(up, down, count):
    across = [(i, i ^ 1) for i in range(count)]
    chips = count // 2
    own = [up] * chips
    for distance in range(1, chips // 2 + 1):
        own[distance] = lax.ppermute(own[distance - 1], "pcol", [(i, (i + 2) % count) for i in range(count)])
    for distance in range(1, (chips - 1) // 2 + 1):
        sent = down if distance == 1 else own[chips - distance + 1]
        own[chips - distance] = lax.ppermute(sent, "pcol", [(i, (i - 2) % count) for i in range(count)])
    return own + [lax.ppermute(piece, "pcol", across) for piece in own]


def per_device(mesh, matrix, l_panels, l_inverse, pivots):
    rows_dev, columns = matrix.shape
    steps, width = pivots.shape
    process_rows, process_columns = mesh.shape["prow"], mesh.shape["pcol"]
    bits = [1 << b for b in range(process_rows.bit_length() - 1)]
    shape = jax.ShapeDtypeStruct
    square = shape((width, columns), F32)
    full = shape((rows_dev, columns), F32)

    def call(kernel, name, operands, outs, specs=None, out_specs=None, scratch=(), cost=None):
        return pl.pallas_call(
            kernel,
            out_shape=outs,
            in_specs=specs or [VMEM] * len(operands),
            out_specs=out_specs or jax.tree.map(lambda _: VMEM, outs),
            scratch_shapes=scratch,
            compiler_params=GRANT,
            cost_estimate=cost and pl.CostEstimate(flops=0, bytes_accessed=cost, transcendentals=0),
            name=name,
        )(*operands)

    def exchange(sent, step):
        received = []
        for stage in range(len(bits)):
            if stage:
                sent = call(functools.partial(merge, bits, stage - 1), "merge", [sent, received[-1], owner[step]], square)
            pairs = []
            for i in range(process_rows):
                for j in range(process_columns):
                    bit = bits[len(bits) - 1 - stage] if j % 2 else bits[stage]
                    pairs.append((i * process_columns + j, (i ^ bit) * process_columns + j))
            received.append(lax.ppermute(sent, ("prow", "pcol"), pairs))
        return sent, received

    owner = jnp.broadcast_to((pivots // rows_dev)[:, :, None], (steps, width, columns))
    chunks = rows_dev // width
    halves = [pltpu.VMEM((rows_dev, l_panels.shape[2]), BF16)] * 2
    block = shape(l_panels.shape[1:], F32)
    slots, matrix, *own = call(
        first_slots,
        "first_slots",
        [pltpu.with_memory_space_constraint(x, pltpu.HBM) for x in (matrix, pivots, l_panels)],
        [square, full] + [block] * steps,
        specs=[HBM] * 3,
        scratch=[pltpu.VMEM((steps, width), jnp.int32), pltpu.SemaphoreType.DMA((chunks + 1 + steps,))],
    )

    def after(panel, before):
        return call(release, "release", [panel, before], block, specs=[VMEM, ANY])

    panels = [gather_panel(own[0], after(own[0], slots), process_columns)]
    sent, received = exchange(slots, 0)
    base, ahead, places = call(
        prepare, "prepare", [matrix, pivots], [full, square, shape((width, width), jnp.int32)]
    )
    up = after(own[1], sent)
    first = lax.ppermute(up, "pcol", [(i, (i + 2) % process_columns) for i in range(process_columns)])
    operands = [matrix, pivots, l_inverse, owner[0], ahead, places, first, sent, *received, *panels[0]]
    specs = [VMEM] * len(operands)
    specs[6] = ANY
    upper, displaced, slots = call(functools.partial(solve, bits, 0), "solve", operands, [square] * 3, specs=specs)
    panels.append(gather_panel(up, after(own[1], slots), process_columns))
    sent, received = exchange(slots, 1)
    base, top = call(
        functools.partial(update, 0),
        "update",
        [base, pivots, upper, displaced, matrix, *panels[0]],
        [full, square],
        scratch=halves,
        cost=COST["update"],
    )
    high, low = call(
        functools.partial(halve, 1, rows_dev, width),
        "halve",
        panels[1],
        [shape((rows_dev, l_panels.shape[2]), BF16)] * 2,
        cost=COST["halve"],
    )
    return call(
        functools.partial(finish, bits, 1),
        "finish",
        [base, pivots, l_inverse, owner[1], top, high, low, sent, *received],
        full,
        out_specs=HBM,
        scratch=[pltpu.VMEM((rows_dev, columns), F32), pltpu.SemaphoreType.DMA((chunks,))],
    )


def solution(mesh):
    placed = (P("prow", "pcol"), P(None, ("prow", "pcol"), None), P(), P())
    return jax.shard_map(
        functools.partial(per_device, mesh), mesh=mesh, in_specs=placed, out_specs=P("prow", "pcol"), check_vma=False
    )
```

```python
import functools

import jax
import jax.numpy as jnp
from jax import lax
from jax.experimental import pallas as pl
from jax.experimental.pallas import tpu as pltpu
from jax.sharding import PartitionSpec as P

VMEM = pl.BlockSpec(memory_space=pltpu.VMEM)
ANY = pl.BlockSpec(memory_space=pl.ANY)
HBM = pl.BlockSpec(memory_space=pltpu.HBM)
GRANT = pltpu.CompilerParams(vmem_limit_bytes=40 * 1024 * 1024)
F32 = jnp.float32
BF16 = jnp.bfloat16
NOWHERE = -(1 << 24)


def product(left, right):
    return jnp.dot(left, right, preferred_element_type=F32)


def split(values):
    high = values.astype(BF16)
    low = (values - high.astype(F32)).astype(BF16)
    return high, low


def dot(left, right):
    return product(left[0], right[0]) + (product(left[0], right[1]) + product(left[1], right[0]))


def pick(chosen, right):
    return product(chosen, right[0]) + product(chosen, right[1])


def one_hot(left, right):
    return jnp.where(left == right, F32(1), F32(0)).astype(BF16)


def iota(shape, dimension):
    return lax.broadcasted_iota(jnp.int32, shape, dimension)


def column_of(row):
    n = row.shape[1]
    spread = jnp.where(iota((n, n), 0) == iota((n, n), 1), row.astype(F32), F32(0))
    return jnp.sum(spread, axis=1, keepdims=True).astype(jnp.int32)


def local_rows(pivots, step, rows_dev):
    offset = pivots[step : step + 1, :] - lax.axis_index("prow") * rows_dev
    return jnp.where((offset >= 0) & (offset < rows_dev), offset, NOWHERE)


def slot_rows(pivots, step, rows_dev):
    offset = local_rows(pivots, step, rows_dev)
    width = offset.shape[1]
    top = jnp.where(lax.axis_index("prow") == 0, step * width + iota(offset.shape, 1), NOWHERE)
    return jnp.where(offset >= 0, offset, top)


def first_slots(matrix, pivots, panels, out, held, *refs):
    blocks, (chosen, sems) = refs[:-2], refs[-2:]
    chunks = sems.shape[0] - 1 - len(blocks)
    rows_dev = held.shape[0]
    rows = rows_dev // chunks
    copies = [pltpu.make_async_copy(pivots, chosen, sems.at[chunks])]
    for c in range(chunks):
        part = pl.ds(c * rows, rows)
        copies.append(pltpu.make_async_copy(matrix.at[part, :], held.at[part, :], sems.at[c]))
    for step, block in enumerate(blocks):
        copies.append(pltpu.make_async_copy(panels.at[step], block, sems.at[chunks + 1 + step]))
    for copy in copies:
        copy.start()
    copies[0].wait()
    place = column_of(slot_rows(chosen, 0, rows_dev))
    total = None
    for c in range(chunks):
        copies[1 + c].wait()
        gather = one_hot(place, iota((place.shape[0], rows), 1) + c * rows)
        term = pick(gather, split(held[c * rows : (c + 1) * rows, :]))
        total = term if total is None else total + term
    out[...] = total
    for copy in copies[1 + chunks :]:
        copy.wait()


def prepare(matrix, pivots, base, ahead, places):
    rows_dev = matrix.shape[0]
    offset = local_rows(pivots, 0, rows_dev)
    width = offset.shape[1]
    place = column_of(slot_rows(pivots, 1, rows_dev))
    places[...] = jnp.broadcast_to(place, places.shape)
    total = None
    for start in range(0, rows_dev, width):
        hit = jnp.where(offset == iota((width, width), 0) + start, F32(1), F32(0))
        keep = jnp.sum(hit, axis=1, keepdims=True) == 0
        kept = jnp.where(keep, matrix[start : start + width, :], F32(0))
        base[start : start + width, :] = kept
        gather = one_hot(place, iota((width, width), 1) + start)
        term = pick(gather, split(kept))
        total = term if total is None else total + term
    ahead[...] = total


def stage_bits(bits, stage):
    odd = lax.rem(lax.axis_index("pcol"), 2) == 1
    bit = jnp.where(odd, bits[len(bits) - 1 - stage], bits[stage])
    known = jnp.where(odd, sum(bits[len(bits) - stage :]) if stage else 0, sum(bits[:stage]))
    return bit, known


def merge(bits, stage, sent, received, owner, *refs):
    row = lax.axis_index("prow")
    bit, known = stage_bits(bits, stage)
    partner = row ^ bit
    who = owner[...]
    keep = ~known
    theirs = ((who ^ partner) & keep) == 0
    neither = ((who ^ row) & ~(known | bit)) != 0
    take = theirs | (neither & ((partner & keep) == 0))
    refs[-1][...] = jnp.where(take, received[...], sent[...])


def picked_rows(bits, sent, received, owner):
    bit, _ = stage_bits(bits, len(bits) - 1)
    mine = ((owner[...] ^ lax.axis_index("prow")) & bit) == 0
    return jnp.where(mine, sent[...], received[-1][...])


def displaced_rows(bits, received, top):
    row = lax.axis_index("prow")
    value = received[-1][...]
    for stage in reversed(range(len(bits) - 1)):
        bit, known = stage_bits(bits, stage)
        value = jnp.where((row & ~(known | bit)) == 0, received[stage][...], value)
    return jnp.where(row == 0, top, value)


def place_of(chip, core, chips, rows):
    return pl.multiple_of((lax.rem(chip + chips, chips) * 2 + core) * rows, rows)


def ring_blocks(refs):
    chips = len(refs) // 2
    chip, core = lax.axis_index("pcol") // 2, lax.rem(lax.axis_index("pcol"), 2)
    found = []
    for position, ref in enumerate(refs):
        side, distance = divmod(position, chips)
        found.append((ref, place_of(chip - distance, 1 - core if side else core, chips, ref.shape[0])))
    return found


def pair_blocks(refs):
    chips, rows = len(refs) - 2, refs[0].shape[0]
    chip, core = lax.axis_index("pcol") // 2, lax.rem(lax.axis_index("pcol"), 2)
    found = []
    for position, ref in enumerate(refs[:4]):
        side, far = position % 2, position // 2
        found.append((ref, place_of(chip + far * (chips // 2), 1 - core if side else core, chips, rows)))
    hops = chips // 2 - 1
    for position, ref in enumerate(refs[4:]):
        side, distance = divmod(position, hops)
        along = (distance + 1) * (1 - 2 * core)
        for half in range(2):
            owner = core if side == half else 1 - core
            place = place_of(chip + along if side else chip - along, owner, chips, rows)
            found.append((ref.at[pl.ds(half * rows, rows), :], place))
    return found


def solve(bits, step, matrix, pivots, inverse, owner, ahead, places, sent, *refs):
    refs = list(refs)
    received = [refs.pop(0) for _ in bits]
    blocks, (upper_out, displaced_out, slots_out) = refs[:-3], refs[-3:]
    rows_dev = matrix.shape[0]
    picked = picked_rows(bits, sent, received, owner)
    width = picked.shape[0]
    upper = dot(split(inverse[step]), split(picked))
    upper_out[...] = upper
    displaced = displaced_rows(bits, received, matrix[step * width : (step + 1) * width, :])
    displaced_out[...] = displaced
    high = low = None
    for block, start in ring_blocks(blocks):
        rows = block.shape[0]
        local = places[:, :rows] - start
        gather = one_hot(local, iota((width, rows), 1))
        block_high, block_low = split(block[...])
        term_high, term_low = product(gather, block_high), product(gather, block_low)
        high = term_high if high is None else high + term_high
        low = term_low if low is None else low + term_low
    moved = one_hot(places[...], local_rows(pivots, step, rows_dev))
    factor = (high.astype(BF16), low.astype(BF16))
    slots_out[...] = ahead[...] + (pick(moved, split(displaced)) - dot(factor, split(upper)))


def assemble(step, blocks, rows_dev, width, high, low):
    limit = (step + 1) * width - lax.axis_index("prow") * rows_dev
    for block, start in blocks:
        rows = block.shape[0]
        below = start + iota(block.shape, 0) >= limit
        block_high, block_low = split(jnp.where(below, -block[...], F32(0)))
        high[pl.ds(start, rows), :] = block_high
        low[pl.ds(start, rows), :] = block_low


def halve(step, rows_dev, width, *refs):
    assemble(step, pair_blocks(refs[:-2]), rows_dev, width, refs[-2], refs[-1])


def update(step, base, pivots, upper_in, displaced_in, *refs):
    blocks, (out, top_out, high, low) = refs[:-4], refs[-4:]
    rows_dev = base.shape[0]
    width = upper_in.shape[0]
    assemble(step, ring_blocks(blocks), rows_dev, width, high, low)
    offset = local_rows(pivots, step, rows_dev)
    later = local_rows(pivots, step + 1, rows_dev)
    upper = split(upper_in[...])
    displaced = split(displaced_in[...])
    for start in range(0, rows_dev, width):
        part = slice(start, start + width)
        rows = iota((width, width), 0) + start
        value = base[part, :] + (pick(one_hot(rows, offset), displaced) + dot((high[part, :], low[part, :]), upper))
        if start == step * width:
            value = jnp.where(lax.axis_index("prow") == 0, upper_in[...], value)
        if start == (step + 1) * width:
            top_out[...] = value
        hit = jnp.where(later == rows, F32(1), F32(0))
        out[part, :] = jnp.where(jnp.sum(hit, axis=1, keepdims=True) == 0, value, F32(0))


def finish(bits, step, base, pivots, inverse, owner, top, high, low, sent, *refs):
    received, (out, result, sems) = refs[:-3], refs[-3:]
    rows_dev = base.shape[0]
    picked = picked_rows(bits, sent, received, owner)
    width = picked.shape[0]
    upper_full = dot(split(inverse[step]), split(picked))
    offset = local_rows(pivots, step, rows_dev)
    upper = split(upper_full)
    displaced = split(displaced_rows(bits, received, top[...]))
    copies = []
    for start in range(0, rows_dev, width):
        part = slice(start, start + width)
        rows = iota((width, width), 0) + start
        value = base[part, :] + (pick(one_hot(rows, offset), displaced) + dot((high[part, :], low[part, :]), upper))
        if start == step * width:
            value = jnp.where(lax.axis_index("prow") == 0, upper_full, value)
        result[part, :] = value
        copies.append(
            pltpu.make_async_copy(result.at[pl.ds(start, width), :], out.at[pl.ds(start, width), :], sems.at[len(copies)])
        )
        copies[-1].start()
    for copy in copies:
        copy.wait()


def pack(own, other, before, out):
    rows = own.shape[0]
    out[:rows, :] = own[...]
    out[rows:, :] = other[...]


def release(panel, before, out):
    out[...] = panel[...]


def shift(block, distance, count):
    return lax.ppermute(block, "pcol", [(i, (i + 2 * distance) % count) for i in range(count)])


def across(block, count):
    return lax.ppermute(block, "pcol", [(i, i ^ 1) for i in range(count)])


def forwarded(up, down, count):
    chips = count // 2
    own = [up] * chips
    for distance in range(1, chips // 2 + 1):
        own[distance] = shift(own[distance - 1], 1, count)
    for distance in range(1, (chips - 1) // 2 + 1):
        own[chips - distance] = shift(down if distance == 1 else own[chips - distance + 1], -1, count)
    return own + [across(piece, count) for piece in own]


def paired(own, other, pair, far, count):
    chips = count // 2
    onward = [(i, (i + (2 if i % 2 == 0 else -2)) % count) for i in range(count)]
    passed = [pair]
    for _ in range(chips // 2 - 1):
        passed.append(lax.ppermute(passed[-1], "pcol", onward))
    back = [across(piece, count) for piece in passed[1:]]
    return [own, other, far, across(far, count)] + passed[1:] + back


def per_device(mesh, matrix, l_panels, l_inverse, pivots):
    rows_dev, columns = matrix.shape
    steps, width = pivots.shape
    process_rows, process_columns = mesh.shape["prow"], mesh.shape["pcol"]
    bits = [1 << b for b in range(process_rows.bit_length() - 1)]
    shape = jax.ShapeDtypeStruct
    square = shape((width, columns), F32)
    full = shape((rows_dev, columns), F32)

    def call(kernel, name, operands, outs, specs=None, out_specs=None, scratch=()):
        return pl.pallas_call(
            kernel,
            out_shape=outs,
            in_specs=specs or [VMEM] * len(operands),
            out_specs=out_specs or jax.tree.map(lambda _: VMEM, outs),
            scratch_shapes=scratch,
            compiler_params=GRANT,
            name=name,
        )(*operands)

    def exchange(sent, step, before=()):
        received = []
        for stage in range(len(bits)):
            if stage:
                operands = [sent, received[-1], owner[step], *before]
                specs = [VMEM] * 3 + [ANY] * len(before)
                sent = call(functools.partial(merge, bits, stage - 1), "merge", operands, square, specs=specs)
            pairs = []
            for i in range(process_rows):
                for j in range(process_columns):
                    bit = bits[len(bits) - 1 - stage] if j % 2 else bits[stage]
                    pairs.append((i * process_columns + j, (i ^ bit) * process_columns + j))
            received.append(lax.ppermute(sent, ("prow", "pcol"), pairs))
        return sent, received

    owner = jnp.broadcast_to((pivots // rows_dev)[:, :, None], (steps, width, columns))
    chunks = rows_dev // width
    halves = [pltpu.VMEM((rows_dev, l_panels.shape[2]), BF16)] * 2
    block = shape(l_panels.shape[1:], F32)
    slots, matrix, *own = call(
        first_slots,
        "first_slots",
        [pltpu.with_memory_space_constraint(x, pltpu.HBM) for x in (matrix, pivots, l_panels)],
        [square, full] + [block] * steps,
        specs=[HBM] * 3,
        scratch=[pltpu.VMEM((steps, width), jnp.int32), pltpu.SemaphoreType.DMA((chunks + 1 + steps,))],
    )

    def after(panel, before):
        return call(release, "release", [panel, before], block, specs=[VMEM, ANY])

    panels = [forwarded(own[0], after(own[0], slots), process_columns)]
    base, ahead, places = call(
        prepare, "prepare", [matrix, pivots], [full, square, shape((width, width), jnp.int32)]
    )
    sent, received = exchange(slots, 0, [places])
    other = across(own[1], process_columns)
    two = shape((2 * block.shape[0], block.shape[1]), F32)
    pair = call(pack, "pack", [own[1], other, sent], two, specs=[VMEM, VMEM, ANY])
    operands = [matrix, pivots, l_inverse, owner[0], ahead, places, sent, *received, *panels[0]]
    upper, displaced, slots = call(functools.partial(solve, bits, 0), "solve", operands, [square] * 3)
    far = shift(after(own[1], slots), process_columns // 4, process_columns)
    panels.append(paired(own[1], other, pair, far, process_columns))
    base, top = call(
        functools.partial(update, 0),
        "update",
        [base, pivots, upper, displaced, *panels[0]],
        [full, square],
        scratch=halves,
    )
    sent, received = exchange(slots, 1)
    high, low = call(
        functools.partial(halve, 1, rows_dev, width),
        "halve",
        panels[1],
        [shape((rows_dev, l_panels.shape[2]), BF16)] * 2,
    )
    return call(
        functools.partial(finish, bits, 1),
        "finish",
        [base, pivots, l_inverse, owner[1], top, high, low, sent, *received],
        full,
        out_specs=HBM,
        scratch=[pltpu.VMEM((rows_dev, columns), F32), pltpu.SemaphoreType.DMA((chunks,))],
    )


def solution(mesh):
    placed = (P("prow", "pcol"), P(None, ("prow", "pcol"), None), P(), P())
    return jax.shard_map(
        functools.partial(per_device, mesh), mesh=mesh, in_specs=placed, out_specs=P("prow", "pcol"), check_vma=False
    )
```

```python
import functools

import jax
import jax.numpy as jnp
from jax import lax
from jax.experimental import pallas as pl
from jax.experimental.pallas import tpu as pltpu
from jax.sharding import PartitionSpec as P

VMEM = pl.BlockSpec(memory_space=pltpu.VMEM)
ANY = pl.BlockSpec(memory_space=pl.ANY)
HBM = pl.BlockSpec(memory_space=pltpu.HBM)
GRANT = pltpu.CompilerParams(vmem_limit_bytes=40 * 1024 * 1024)
F32 = jnp.float32
BF16 = jnp.bfloat16
NOWHERE = -(1 << 24)


def product(left, right):
    return jnp.dot(left, right, preferred_element_type=F32)


def split(values):
    high = values.astype(BF16)
    low = (values - high.astype(F32)).astype(BF16)
    return high, low


def dot(left, right):
    return product(left[0], right[0]) + (product(left[0], right[1]) + product(left[1], right[0]))


def pick(chosen, right):
    return product(chosen, right[0]) + product(chosen, right[1])


def one_hot(left, right):
    return jnp.where(left == right, F32(1), F32(0)).astype(BF16)


def iota(shape, dimension):
    return lax.broadcasted_iota(jnp.int32, shape, dimension)


def column_of(row):
    n = row.shape[1]
    spread = jnp.where(iota((n, n), 0) == iota((n, n), 1), row.astype(F32), F32(0))
    return jnp.sum(spread, axis=1, keepdims=True).astype(jnp.int32)


def local_rows(pivots, step, rows_dev):
    offset = pivots[step : step + 1, :] - lax.axis_index("prow") * rows_dev
    return jnp.where((offset >= 0) & (offset < rows_dev), offset, NOWHERE)


def slot_rows(pivots, step, rows_dev):
    offset = local_rows(pivots, step, rows_dev)
    width = offset.shape[1]
    top = jnp.where(lax.axis_index("prow") == 0, step * width + iota(offset.shape, 1), NOWHERE)
    return jnp.where(offset >= 0, offset, top)


def first_slots(matrix, pivots, panels, out, held, *refs):
    blocks, (chosen, sems) = refs[:-2], refs[-2:]
    chunks = sems.shape[0] - 1 - len(blocks)
    rows_dev = held.shape[0]
    rows = rows_dev // chunks
    copies = [pltpu.make_async_copy(pivots, chosen, sems.at[chunks])]
    for c in range(chunks):
        part = pl.ds(c * rows, rows)
        copies.append(pltpu.make_async_copy(matrix.at[part, :], held.at[part, :], sems.at[c]))
    for step, block in enumerate(blocks):
        copies.append(pltpu.make_async_copy(panels.at[step], block, sems.at[chunks + 1 + step]))
    for copy in copies:
        copy.start()
    copies[0].wait()
    place = column_of(slot_rows(chosen, 0, rows_dev))
    total = None
    for c in range(chunks):
        copies[1 + c].wait()
        gather = one_hot(place, iota((place.shape[0], rows), 1) + c * rows)
        term = pick(gather, split(held[c * rows : (c + 1) * rows, :]))
        total = term if total is None else total + term
    out[...] = total
    for copy in copies[1 + chunks :]:
        copy.wait()


def prepare(matrix, pivots, base, ahead, places):
    rows_dev = matrix.shape[0]
    offset = local_rows(pivots, 0, rows_dev)
    width = offset.shape[1]
    place = column_of(slot_rows(pivots, 1, rows_dev))
    places[...] = jnp.broadcast_to(place, places.shape)
    total = None
    for start in range(0, rows_dev, width):
        hit = jnp.where(offset == iota((width, width), 0) + start, F32(1), F32(0))
        keep = jnp.sum(hit, axis=1, keepdims=True) == 0
        kept = jnp.where(keep, matrix[start : start + width, :], F32(0))
        base[start : start + width, :] = kept
        gather = one_hot(place, iota((width, width), 1) + start)
        term = pick(gather, split(kept))
        total = term if total is None else total + term
    ahead[...] = total


def stage_bits(bits, stage):
    odd = lax.rem(lax.axis_index("pcol"), 2) == 1
    bit = jnp.where(odd, bits[len(bits) - 1 - stage], bits[stage])
    known = jnp.where(odd, sum(bits[len(bits) - stage :]) if stage else 0, sum(bits[:stage]))
    return bit, known


def merge(bits, stage, sent, received, owner, *refs):
    row = lax.axis_index("prow")
    bit, known = stage_bits(bits, stage)
    partner = row ^ bit
    who = owner[...]
    keep = ~known
    theirs = ((who ^ partner) & keep) == 0
    neither = ((who ^ row) & ~(known | bit)) != 0
    take = theirs | (neither & ((partner & keep) == 0))
    refs[-1][...] = jnp.where(take, received[...], sent[...])


def picked_rows(bits, sent, received, owner):
    bit, _ = stage_bits(bits, len(bits) - 1)
    mine = ((owner[...] ^ lax.axis_index("prow")) & bit) == 0
    return jnp.where(mine, sent[...], received[-1][...])


def displaced_rows(bits, received, top):
    row = lax.axis_index("prow")
    value = received[-1][...]
    for stage in reversed(range(len(bits) - 1)):
        bit, known = stage_bits(bits, stage)
        value = jnp.where((row & ~(known | bit)) == 0, received[stage][...], value)
    return jnp.where(row == 0, top, value)


def place_of(chip, core, chips, rows):
    return pl.multiple_of((lax.rem(chip + chips, chips) * 2 + core) * rows, rows)


def rows_of(ref, index, count=1):
    rows = ref.shape[0] // count
    return ref.at[pl.ds(index * rows, rows), :]


def ring_blocks(refs):
    chips, rows = (len(refs) + 1) // 2, refs[0].shape[0]
    mine, near, rest = refs[:chips], refs[chips], refs[chips + 1 :]
    chip, core = lax.axis_index("pcol") // 2, lax.rem(lax.axis_index("pcol"), 2)
    found = []
    for order, distance in enumerate(ring_order(chips)):
        found.append((mine[order], place_of(chip - distance, core, chips, rows)))
        if order < 2:
            ref = rows_of(near, order, 3)
        else:
            ref = rest[order - 2]
        found.append((ref, place_of(chip - distance, 1 - core, chips, rows)))
    return found


def pair_blocks(refs):
    own, near, far, far_back, *pairs = refs
    rows = own.shape[0]
    chips = len(pairs) + 2
    hops = len(pairs) // 2
    chip, core = lax.axis_index("pcol") // 2, lax.rem(lax.axis_index("pcol"), 2)
    opposite = chip + chips // 2
    found = [
        (own, place_of(chip, core, chips, rows)),
        (rows_of(near, 2, 3), place_of(chip, 1 - core, chips, rows)),
        (far, place_of(opposite, core, chips, rows)),
        (far_back, place_of(opposite, 1 - core, chips, rows)),
    ]
    for hop in range(hops):
        along = (hop + 1) * (1 - 2 * core)
        for half in range(2):
            owner = core if half == 0 else 1 - core
            found.append((rows_of(pairs[hop], half, 2), place_of(chip - along, owner, chips, rows)))
            found.append((rows_of(pairs[hops + hop], half, 2), place_of(chip + along, 1 - owner, chips, rows)))
    return found


def solve(bits, step, matrix, pivots, inverse, owner, ahead, places, sent, *refs):
    refs = list(refs)
    received = [refs.pop(0) for _ in bits]
    blocks, (upper_out, displaced_out, slots_out) = refs[:-3], refs[-3:]
    rows_dev = matrix.shape[0]
    picked = picked_rows(bits, sent, received, owner)
    width = picked.shape[0]
    upper = dot(split(inverse[step]), split(picked))
    upper_out[...] = upper
    displaced = displaced_rows(bits, received, matrix[step * width : (step + 1) * width, :])
    displaced_out[...] = displaced
    high = low = None
    for block, start in ring_blocks(blocks):
        rows = block.shape[0]
        local = places[:, :rows] - start
        gather = one_hot(local, iota((width, rows), 1))
        block_high, block_low = split(block[...])
        term_high, term_low = product(gather, block_high), product(gather, block_low)
        high = term_high if high is None else high + term_high
        low = term_low if low is None else low + term_low
    moved = one_hot(places[...], local_rows(pivots, step, rows_dev))
    factor = (high.astype(BF16), low.astype(BF16))
    slots_out[...] = ahead[...] + (pick(moved, split(displaced)) - dot(factor, split(upper)))


def assemble(step, blocks, rows_dev, width, high, low):
    limit = (step + 1) * width - lax.axis_index("prow") * rows_dev
    for block, start in blocks:
        rows = block.shape[0]
        below = start + iota(block.shape, 0) >= limit
        block_high, block_low = split(jnp.where(below, -block[...], F32(0)))
        high[pl.ds(start, rows), :] = block_high
        low[pl.ds(start, rows), :] = block_low


def halve(step, rows_dev, width, *refs):
    assemble(step, pair_blocks(refs[:-2]), rows_dev, width, refs[-2], refs[-1])


def update(step, base, pivots, upper_in, displaced_in, *refs):
    blocks, (out, top_out, high, low) = refs[:-4], refs[-4:]
    rows_dev = base.shape[0]
    width = upper_in.shape[0]
    assemble(step, ring_blocks(blocks), rows_dev, width, high, low)
    offset = local_rows(pivots, step, rows_dev)
    later = local_rows(pivots, step + 1, rows_dev)
    upper = split(upper_in[...])
    displaced = split(displaced_in[...])
    for start in range(0, rows_dev, width):
        part = slice(start, start + width)
        rows = iota((width, width), 0) + start
        value = base[part, :] + (pick(one_hot(rows, offset), displaced) + dot((high[part, :], low[part, :]), upper))
        if start == step * width:
            value = jnp.where(lax.axis_index("prow") == 0, upper_in[...], value)
        if start == (step + 1) * width:
            top_out[...] = value
        hit = jnp.where(later == rows, F32(1), F32(0))
        out[part, :] = jnp.where(jnp.sum(hit, axis=1, keepdims=True) == 0, value, F32(0))


def finish(bits, step, base, pivots, inverse, owner, top, high, low, sent, *refs):
    received, (out, result, sems) = refs[:-3], refs[-3:]
    rows_dev = base.shape[0]
    picked = picked_rows(bits, sent, received, owner)
    width = picked.shape[0]
    upper_full = dot(split(inverse[step]), split(picked))
    offset = local_rows(pivots, step, rows_dev)
    upper = split(upper_full)
    displaced = split(displaced_rows(bits, received, top[...]))
    copies = []
    for start in range(0, rows_dev, width):
        part = slice(start, start + width)
        rows = iota((width, width), 0) + start
        value = base[part, :] + (pick(one_hot(rows, offset), displaced) + dot((high[part, :], low[part, :]), upper))
        if start == step * width:
            value = jnp.where(lax.axis_index("prow") == 0, upper_full, value)
        result[part, :] = value
        copies.append(
            pltpu.make_async_copy(result.at[pl.ds(start, width), :], out.at[pl.ds(start, width), :], sems.at[len(copies)])
        )
        copies[-1].start()
    for copy in copies:
        copy.wait()


def stack(*refs):
    out = refs[-1]
    start = 0
    for ref in refs[:-1]:
        out[start : start + ref.shape[0], :] = ref[...]
        start += ref.shape[0]


def pack(own, near, before, out):
    rows = own.shape[0]
    out[:rows, :] = own[...]
    out[rows:, :] = near[2 * rows :, :]


def ring_order(chips):
    return [0] + list(range(1, chips // 2 + 1)) + list(range(chips - 1, chips // 2, -1))


def release(panel, before, out):
    out[...] = panel[...]


def shift(block, distance, count):
    return lax.ppermute(block, "pcol", [(i, (i + 2 * distance) % count) for i in range(count)])


def across(block, count):
    return lax.ppermute(block, "pcol", [(i, i ^ 1) for i in range(count)])


def forwarded(block, down, count):
    chips = count // 2
    own = [block]
    for distance in ring_order(chips)[1:]:
        if distance <= chips // 2:
            own.append(shift(own[-1], 1, count))
        else:
            own.append(shift(down if distance == chips - 1 else own[-1], -1, count))
    return own


def passed(pair, count):
    onward = [(i, (i + (2 if i % 2 == 0 else -2)) % count) for i in range(count)]
    pairs = [pair]
    for _ in range(count // 4 - 1):
        pairs.append(lax.ppermute(pairs[-1], "pcol", onward))
    return pairs[1:]


def per_device(mesh, matrix, l_panels, l_inverse, pivots):
    rows_dev, columns = matrix.shape
    steps, width = pivots.shape
    process_rows, process_columns = mesh.shape["prow"], mesh.shape["pcol"]
    bits = [1 << b for b in range(process_rows.bit_length() - 1)]
    shape = jax.ShapeDtypeStruct
    square = shape((width, columns), F32)
    full = shape((rows_dev, columns), F32)

    def call(kernel, name, operands, outs, specs=None, out_specs=None, scratch=()):
        return pl.pallas_call(
            kernel,
            out_shape=outs,
            in_specs=specs or [VMEM] * len(operands),
            out_specs=out_specs or jax.tree.map(lambda _: VMEM, outs),
            scratch_shapes=scratch,
            compiler_params=GRANT,
            name=name,
        )(*operands)

    def exchange(sent, step, before=()):
        received = []
        for stage in range(len(bits)):
            if stage:
                operands = [sent, received[-1], owner[step], *before]
                specs = [VMEM] * 3 + [ANY] * len(before)
                sent = call(functools.partial(merge, bits, stage - 1), "merge", operands, square, specs=specs)
            pairs = []
            for i in range(process_rows):
                for j in range(process_columns):
                    bit = bits[len(bits) - 1 - stage] if j % 2 else bits[stage]
                    pairs.append((i * process_columns + j, (i ^ bit) * process_columns + j))
            received.append(lax.ppermute(sent, ("prow", "pcol"), pairs))
        return sent, received

    owner = jnp.broadcast_to((pivots // rows_dev)[:, :, None], (steps, width, columns))
    chunks = rows_dev // width
    halves = [pltpu.VMEM((rows_dev, l_panels.shape[2]), BF16)] * 2
    block = shape(l_panels.shape[1:], F32)
    slots, matrix, *own = call(
        first_slots,
        "first_slots",
        [pltpu.with_memory_space_constraint(x, pltpu.HBM) for x in (matrix, pivots, l_panels)],
        [square, full] + [block] * steps,
        specs=[HBM] * 3,
        scratch=[pltpu.VMEM((steps, width), jnp.int32), pltpu.SemaphoreType.DMA((chunks + 1 + steps,))],
    )

    def after(panel, before):
        return call(release, "release", [panel, before], block, specs=[VMEM, ANY])

    def stacked(blocks):
        rows = sum(piece.shape[0] for piece in blocks)
        return call(stack, "stack", blocks, shape((rows, block.shape[1]), F32))

    base, ahead, places = call(
        prepare, "prepare", [matrix, pivots], [full, square, shape((width, width), jnp.int32)]
    )
    first = forwarded(own[0], after(own[0], places), process_columns)
    near = across(stacked([*first[:2], own[1]]), process_columns)
    first += [near] + [across(piece, process_columns) for piece in first[2:]]
    sent, received = exchange(slots, 0, [near])
    two = shape((2 * block.shape[0], block.shape[1]), F32)
    pair = call(pack, "pack", [own[1], near, sent], two, specs=[VMEM, VMEM, ANY])
    operands = [matrix, pivots, l_inverse, owner[0], ahead, places, sent, *received, *first]
    upper, displaced, slots = call(functools.partial(solve, bits, 0), "solve", operands, [square] * 3)
    far = shift(after(own[1], slots), process_columns // 4, process_columns)
    pairs = passed(pair, process_columns)
    second = [own[1], near, far, across(far, process_columns)]
    second += pairs + [across(piece, process_columns) for piece in pairs]
    base, top = call(
        functools.partial(update, 0),
        "update",
        [base, pivots, upper, displaced, *first],
        [full, square],
        scratch=halves,
    )
    sent, received = exchange(slots, 1)
    high, low = call(
        functools.partial(halve, 1, rows_dev, width),
        "halve",
        second,
        [shape((rows_dev, l_panels.shape[2]), BF16)] * 2,
    )
    return call(
        functools.partial(finish, bits, 1),
        "finish",
        [base, pivots, l_inverse, owner[1], top, high, low, sent, *received],
        full,
        out_specs=HBM,
        scratch=[pltpu.VMEM((rows_dev, columns), F32), pltpu.SemaphoreType.DMA((chunks,))],
    )


def solution(mesh):
    placed = (P("prow", "pcol"), P(None, ("prow", "pcol"), None), P(), P())
    return jax.shard_map(
        functools.partial(per_device, mesh), mesh=mesh, in_specs=placed, out_specs=P("prow", "pcol"), check_vma=False
    )
```

```python
import functools

import jax
import jax.numpy as jnp
from jax import lax
from jax.experimental import pallas as pl
from jax.experimental.pallas import tpu as pltpu
from jax.sharding import PartitionSpec as P

VMEM = pl.BlockSpec(memory_space=pltpu.VMEM)
ANY = pl.BlockSpec(memory_space=pl.ANY)
HBM = pl.BlockSpec(memory_space=pltpu.HBM)
GRANT = pltpu.CompilerParams(vmem_limit_bytes=40 * 1024 * 1024)
F32 = jnp.float32
BF16 = jnp.bfloat16
NOWHERE = -(1 << 24)


def product(left, right):
    return jnp.dot(left, right, preferred_element_type=F32)


def split(values):
    high = values.astype(BF16)
    low = (values - high.astype(F32)).astype(BF16)
    return high, low


def dot(left, right):
    return product(left[0], right[0]) + (product(left[0], right[1]) + product(left[1], right[0]))


def pick(chosen, right):
    return product(chosen, right[0]) + product(chosen, right[1])


def one_hot(left, right):
    return jnp.where(left == right, F32(1), F32(0)).astype(BF16)


def iota(shape, dimension):
    return lax.broadcasted_iota(jnp.int32, shape, dimension)


def column_of(row):
    n = row.shape[1]
    spread = jnp.where(iota((n, n), 0) == iota((n, n), 1), row.astype(F32), F32(0))
    return jnp.sum(spread, axis=1, keepdims=True).astype(jnp.int32)


def local_rows(pivots, step, rows_dev):
    offset = pivots[step : step + 1, :] - lax.axis_index("prow") * rows_dev
    return jnp.where((offset >= 0) & (offset < rows_dev), offset, NOWHERE)


def slot_rows(pivots, step, rows_dev):
    offset = local_rows(pivots, step, rows_dev)
    width = offset.shape[1]
    top = jnp.where(lax.axis_index("prow") == 0, step * width + iota(offset.shape, 1), NOWHERE)
    return jnp.where(offset >= 0, offset, top)


def first_slots(matrix, pivots, panels, out, held, *refs):
    blocks, (chosen, sems) = refs[:-2], refs[-2:]
    chunks = sems.shape[0] - 1 - len(blocks)
    rows_dev = held.shape[0]
    rows = rows_dev // chunks
    copies = [pltpu.make_async_copy(pivots, chosen, sems.at[chunks])]
    for c in range(chunks):
        part = pl.ds(c * rows, rows)
        copies.append(pltpu.make_async_copy(matrix.at[part, :], held.at[part, :], sems.at[c]))
    for step, block in enumerate(blocks):
        copies.append(pltpu.make_async_copy(panels.at[step], block, sems.at[chunks + 1 + step]))
    for copy in copies:
        copy.start()
    copies[0].wait()
    place = column_of(slot_rows(chosen, 0, rows_dev))
    total = None
    for c in range(chunks):
        copies[1 + c].wait()
        gather = one_hot(place, iota((place.shape[0], rows), 1) + c * rows)
        term = pick(gather, split(held[c * rows : (c + 1) * rows, :]))
        total = term if total is None else total + term
    out[...] = total
    for copy in copies[1 + chunks :]:
        copy.wait()


def prepare(matrix, pivots, base, ahead, places):
    rows_dev = matrix.shape[0]
    offset = local_rows(pivots, 0, rows_dev)
    width = offset.shape[1]
    place = column_of(slot_rows(pivots, 1, rows_dev))
    places[...] = jnp.broadcast_to(place, places.shape)
    total = None
    for start in range(0, rows_dev, width):
        hit = jnp.where(offset == iota((width, width), 0) + start, F32(1), F32(0))
        keep = jnp.sum(hit, axis=1, keepdims=True) == 0
        kept = jnp.where(keep, matrix[start : start + width, :], F32(0))
        base[start : start + width, :] = kept
        gather = one_hot(place, iota((width, width), 1) + start)
        term = pick(gather, split(kept))
        total = term if total is None else total + term
    ahead[...] = total


def stage_bits(bits, stage):
    odd = lax.rem(lax.axis_index("pcol"), 2) == 1
    bit = jnp.where(odd, bits[len(bits) - 1 - stage], bits[stage])
    known = jnp.where(odd, sum(bits[len(bits) - stage :]) if stage else 0, sum(bits[:stage]))
    return bit, known


def merge(bits, stage, sent, received, owner, *refs):
    row = lax.axis_index("prow")
    bit, known = stage_bits(bits, stage)
    partner = row ^ bit
    who = owner[...]
    keep = ~known
    theirs = ((who ^ partner) & keep) == 0
    neither = ((who ^ row) & ~(known | bit)) != 0
    take = theirs | (neither & ((partner & keep) == 0))
    refs[-1][...] = jnp.where(take, received[...], sent[...])


def picked_rows(bits, sent, received, owner):
    bit, _ = stage_bits(bits, len(bits) - 1)
    mine = ((owner[...] ^ lax.axis_index("prow")) & bit) == 0
    return jnp.where(mine, sent[...], received[-1][...])


def displaced_rows(bits, received, top):
    row = lax.axis_index("prow")
    value = received[-1][...]
    for stage in reversed(range(len(bits) - 1)):
        bit, known = stage_bits(bits, stage)
        value = jnp.where((row & ~(known | bit)) == 0, received[stage][...], value)
    return jnp.where(row == 0, top, value)


def place_of(chip, core, chips, rows):
    return pl.multiple_of((lax.rem(chip + chips, chips) * 2 + core) * rows, rows)


def rows_of(ref, index, count=1):
    rows = ref.shape[0] // count
    return ref.at[pl.ds(index * rows, rows), :]


def panel_blocks(step, steps, refs):
    own, near, far, far_back, *pairs = refs
    rows = own.shape[0]
    chips = len(pairs) + 2
    hops = len(pairs) // 2
    chip, core = lax.axis_index("pcol") // 2, lax.rem(lax.axis_index("pcol"), 2)
    opposite = chip + chips // 2
    found = [
        (own, place_of(chip, core, chips, rows)),
        (rows_of(near, step, steps), place_of(chip, 1 - core, chips, rows)),
        (far, place_of(opposite, core, chips, rows)),
        (far_back, place_of(opposite, 1 - core, chips, rows)),
    ]
    for hop in range(hops):
        along = (hop + 1) * (1 - 2 * core)
        for half in range(2):
            owner = core if half == 0 else 1 - core
            found.append((rows_of(pairs[hop], half, 2), place_of(chip - along, owner, chips, rows)))
            found.append((rows_of(pairs[hops + hop], half, 2), place_of(chip + along, 1 - owner, chips, rows)))
    return found


def solve(bits, step, matrix, pivots, inverse, owner, ahead, places, sent, *refs):
    refs = list(refs)
    received = [refs.pop(0) for _ in bits]
    blocks, (upper_out, displaced_out, slots_out) = refs[:-3], refs[-3:]
    rows_dev = matrix.shape[0]
    picked = picked_rows(bits, sent, received, owner)
    width = picked.shape[0]
    upper = dot(split(inverse[step]), split(picked))
    upper_out[...] = upper
    displaced = displaced_rows(bits, received, matrix[step * width : (step + 1) * width, :])
    displaced_out[...] = displaced
    high = low = None
    for block, start in panel_blocks(step, pivots.shape[0], blocks):
        rows = block.shape[0]
        local = places[:, :rows] - start
        gather = one_hot(local, iota((width, rows), 1))
        block_high, block_low = split(block[...])
        term_high, term_low = product(gather, block_high), product(gather, block_low)
        high = term_high if high is None else high + term_high
        low = term_low if low is None else low + term_low
    moved = one_hot(places[...], local_rows(pivots, step, rows_dev))
    factor = (high.astype(BF16), low.astype(BF16))
    slots_out[...] = ahead[...] + (pick(moved, split(displaced)) - dot(factor, split(upper)))


def assemble(step, blocks, rows_dev, width, high, low):
    limit = (step + 1) * width - lax.axis_index("prow") * rows_dev
    for block, start in blocks:
        rows = block.shape[0]
        below = start + iota(block.shape, 0) >= limit
        block_high, block_low = split(jnp.where(below, -block[...], F32(0)))
        high[pl.ds(start, rows), :] = block_high
        low[pl.ds(start, rows), :] = block_low


def halve(step, steps, rows_dev, width, *refs):
    assemble(step, panel_blocks(step, steps, refs[:-2]), rows_dev, width, refs[-2], refs[-1])


def update(step, base, pivots, upper_in, displaced_in, *refs):
    blocks, (out, top_out, high, low) = refs[:-4], refs[-4:]
    rows_dev = base.shape[0]
    width = upper_in.shape[0]
    assemble(step, panel_blocks(step, pivots.shape[0], blocks), rows_dev, width, high, low)
    offset = local_rows(pivots, step, rows_dev)
    later = local_rows(pivots, step + 1, rows_dev)
    upper = split(upper_in[...])
    displaced = split(displaced_in[...])
    for start in range(0, rows_dev, width):
        part = slice(start, start + width)
        rows = iota((width, width), 0) + start
        value = base[part, :] + (pick(one_hot(rows, offset), displaced) + dot((high[part, :], low[part, :]), upper))
        if start == step * width:
            value = jnp.where(lax.axis_index("prow") == 0, upper_in[...], value)
        if start == (step + 1) * width:
            top_out[...] = value
        hit = jnp.where(later == rows, F32(1), F32(0))
        out[part, :] = jnp.where(jnp.sum(hit, axis=1, keepdims=True) == 0, value, F32(0))


def finish(bits, step, base, pivots, inverse, owner, top, high, low, sent, *refs):
    received, (out, result, sems) = refs[:-3], refs[-3:]
    rows_dev = base.shape[0]
    picked = picked_rows(bits, sent, received, owner)
    width = picked.shape[0]
    upper_full = dot(split(inverse[step]), split(picked))
    offset = local_rows(pivots, step, rows_dev)
    upper = split(upper_full)
    displaced = split(displaced_rows(bits, received, top[...]))
    copies = []
    for start in range(0, rows_dev, width):
        part = slice(start, start + width)
        rows = iota((width, width), 0) + start
        value = base[part, :] + (pick(one_hot(rows, offset), displaced) + dot((high[part, :], low[part, :]), upper))
        if start == step * width:
            value = jnp.where(lax.axis_index("prow") == 0, upper_full, value)
        result[part, :] = value
        copies.append(
            pltpu.make_async_copy(result.at[pl.ds(start, width), :], out.at[pl.ds(start, width), :], sems.at[len(copies)])
        )
        copies[-1].start()
    for copy in copies:
        copy.wait()


def pack(step, own, near, before, out):
    rows = own.shape[0]
    out[:rows, :] = own[...]
    out[rows:, :] = near[step * rows : (step + 1) * rows, :]


def release(panel, before, out):
    out[...] = panel[...]


def shift(block, distance, count):
    return lax.ppermute(block, "pcol", [(i, (i + 2 * distance) % count) for i in range(count)])


def across(block, count):
    return lax.ppermute(block, "pcol", [(i, i ^ 1) for i in range(count)])


def passed(pair, count):
    onward = [(i, (i + (2 if i % 2 == 0 else -2)) % count) for i in range(count)]
    pairs = [pair]
    for _ in range(count // 4 - 1):
        pairs.append(lax.ppermute(pairs[-1], "pcol", onward))
    return pairs[1:]


def per_device(mesh, matrix, l_panels, l_inverse, pivots):
    rows_dev, columns = matrix.shape
    steps, width = pivots.shape
    process_rows, process_columns = mesh.shape["prow"], mesh.shape["pcol"]
    bits = [1 << b for b in range(process_rows.bit_length() - 1)]
    shape = jax.ShapeDtypeStruct
    square = shape((width, columns), F32)
    full = shape((rows_dev, columns), F32)

    def call(kernel, name, operands, outs, specs=None, out_specs=None, scratch=()):
        return pl.pallas_call(
            kernel,
            out_shape=outs,
            in_specs=specs or [VMEM] * len(operands),
            out_specs=out_specs or jax.tree.map(lambda _: VMEM, outs),
            scratch_shapes=scratch,
            compiler_params=GRANT,
            name=name,
        )(*operands)

    def exchange(sent, step, before=()):
        received = []
        for stage in range(len(bits)):
            if stage:
                operands = [sent, received[-1], owner[step], *before]
                specs = [VMEM] * 3 + [ANY] * len(before)
                sent = call(functools.partial(merge, bits, stage - 1), "merge", operands, square, specs=specs)
            pairs = []
            for i in range(process_rows):
                for j in range(process_columns):
                    bit = bits[len(bits) - 1 - stage] if j % 2 else bits[stage]
                    pairs.append((i * process_columns + j, (i ^ bit) * process_columns + j))
            received.append(lax.ppermute(sent, ("prow", "pcol"), pairs))
        return sent, received

    owner = jnp.broadcast_to((pivots // rows_dev)[:, :, None], (steps, width, columns))
    chunks = rows_dev // width
    halves = [pltpu.VMEM((rows_dev, l_panels.shape[2]), BF16)] * 2
    block = shape(l_panels.shape[1:], F32)
    slots, matrix, *own = call(
        first_slots,
        "first_slots",
        [pltpu.with_memory_space_constraint(x, pltpu.HBM) for x in (matrix, pivots, l_panels)],
        [square, full] + [block] * steps,
        specs=[HBM] * 3,
        scratch=[pltpu.VMEM((steps, width), jnp.int32), pltpu.SemaphoreType.DMA((chunks + 1 + steps,))],
    )

    def after(panel, before):
        return call(release, "release", [panel, before], block, specs=[VMEM, ANY])

    near = across(l_panels.reshape(-1, l_panels.shape[2]), process_columns)

    def gather(step, before_pair, before_far):
        two = shape((2 * block.shape[0], block.shape[1]), F32)
        specs = [VMEM, VMEM, ANY]
        pair = call(functools.partial(pack, step), "pack", [own[step], near, before_pair], two, specs=specs)
        far = shift(after(own[step], before_far), process_columns // 4, process_columns)
        pairs = passed(pair, process_columns)
        back = [across(piece, process_columns) for piece in pairs]
        return [own[step], near, far, across(far, process_columns), *pairs, *back]

    base, ahead, places = call(
        prepare, "prepare", [matrix, pivots], [full, square, shape((width, width), jnp.int32)]
    )
    later = call(release, "release", [slots, near], square, specs=[VMEM, ANY])
    first = gather(0, later, own[1])
    sent, received = exchange(later, 0, [places])
    operands = [matrix, pivots, l_inverse, owner[0], ahead, places, sent, *received, *first]
    upper, displaced, slots = call(functools.partial(solve, bits, 0), "solve", operands, [square] * 3)
    second = gather(1, sent, slots)
    base, top = call(
        functools.partial(update, 0),
        "update",
        [base, pivots, upper, displaced, *first],
        [full, square],
        scratch=halves,
    )
    sent, received = exchange(slots, 1)
    high, low = call(
        functools.partial(halve, 1, steps, rows_dev, width),
        "halve",
        second,
        [shape((rows_dev, l_panels.shape[2]), BF16)] * 2,
    )
    return call(
        functools.partial(finish, bits, 1),
        "finish",
        [base, pivots, l_inverse, owner[1], top, high, low, sent, *received],
        full,
        out_specs=HBM,
        scratch=[pltpu.VMEM((rows_dev, columns), F32), pltpu.SemaphoreType.DMA((chunks,))],
    )


def solution(mesh):
    placed = (P("prow", "pcol"), P(None, ("prow", "pcol"), None), P(), P())
    return jax.shard_map(
        functools.partial(per_device, mesh), mesh=mesh, in_specs=placed, out_specs=P("prow", "pcol"), check_vma=False
    )
```

```python
import functools

import jax
import jax.numpy as jnp
from jax import lax
from jax.experimental import pallas as pl
from jax.experimental.pallas import tpu as pltpu
from jax.sharding import PartitionSpec as P

VMEM = pl.BlockSpec(memory_space=pltpu.VMEM)
ANY = pl.BlockSpec(memory_space=pl.ANY)
HBM = pl.BlockSpec(memory_space=pltpu.HBM)
GRANT = pltpu.CompilerParams(vmem_limit_bytes=40 * 1024 * 1024)
F32 = jnp.float32
BF16 = jnp.bfloat16
NOWHERE = -(1 << 24)


def product(left, right):
    return jnp.dot(left, right, preferred_element_type=F32)


def split(values):
    high = values.astype(BF16)
    low = (values - high.astype(F32)).astype(BF16)
    return high, low


def dot(left, right):
    return product(left[0], right[0]) + (product(left[0], right[1]) + product(left[1], right[0]))


def pick(chosen, right):
    return product(chosen, right[0]) + product(chosen, right[1])


def one_hot(left, right):
    return jnp.where(left == right, F32(1), F32(0)).astype(BF16)


def iota(shape, dimension):
    return lax.broadcasted_iota(jnp.int32, shape, dimension)


def column_of(row):
    n = row.shape[1]
    spread = jnp.where(iota((n, n), 0) == iota((n, n), 1), row.astype(F32), F32(0))
    return jnp.sum(spread, axis=1, keepdims=True).astype(jnp.int32)


def local_rows(pivots, step, rows_dev):
    offset = pivots[step : step + 1, :] - lax.axis_index("prow") * rows_dev
    return jnp.where((offset >= 0) & (offset < rows_dev), offset, NOWHERE)


def slot_rows(pivots, step, rows_dev):
    offset = local_rows(pivots, step, rows_dev)
    width = offset.shape[1]
    top = jnp.where(lax.axis_index("prow") == 0, step * width + iota(offset.shape, 1), NOWHERE)
    return jnp.where(offset >= 0, offset, top)


def load(matrix, pivots, panels, held, chosen, *refs):
    blocks, sems = refs[:-1], refs[-1]
    sources = [panels.at[step] for step in range(len(blocks))] + [pivots, matrix]
    targets = [*blocks, chosen, held]
    copies = [pltpu.make_async_copy(*pair, sems.at[i]) for i, pair in enumerate(zip(sources, targets))]
    for copy in copies:
        copy.start()
    for copy in copies:
        copy.wait()


def first_slots(matrix, pivots, out):
    rows_dev = matrix.shape[0]
    place = column_of(slot_rows(pivots, 0, rows_dev))
    width = place.shape[0]
    total = None
    for start in range(0, rows_dev, width):
        gather = one_hot(place, iota((width, width), 1) + start)
        term = pick(gather, split(matrix[start : start + width, :]))
        total = term if total is None else total + term
    out[...] = total


def prepare(matrix, pivots, base, ahead, places):
    rows_dev = matrix.shape[0]
    offset = local_rows(pivots, 0, rows_dev)
    width = offset.shape[1]
    place = column_of(slot_rows(pivots, 1, rows_dev))
    places[...] = jnp.broadcast_to(place, places.shape)
    total = None
    for start in range(0, rows_dev, width):
        hit = jnp.where(offset == iota((width, width), 0) + start, F32(1), F32(0))
        keep = jnp.sum(hit, axis=1, keepdims=True) == 0
        kept = jnp.where(keep, matrix[start : start + width, :], F32(0))
        base[start : start + width, :] = kept
        gather = one_hot(place, iota((width, width), 1) + start)
        term = pick(gather, split(kept))
        total = term if total is None else total + term
    ahead[...] = total


def stage_bits(bits, stage):
    odd = lax.rem(lax.axis_index("pcol"), 2) == 1
    bit = jnp.where(odd, bits[len(bits) - 1 - stage], bits[stage])
    known = jnp.where(odd, sum(bits[len(bits) - stage :]) if stage else 0, sum(bits[:stage]))
    return bit, known


def merge(bits, stage, sent, received, owner, *refs):
    row = lax.axis_index("prow")
    bit, known = stage_bits(bits, stage)
    partner = row ^ bit
    who = owner[...]
    keep = ~known
    theirs = ((who ^ partner) & keep) == 0
    neither = ((who ^ row) & ~(known | bit)) != 0
    take = theirs | (neither & ((partner & keep) == 0))
    refs[-1][...] = jnp.where(take, received[...], sent[...])


def picked_rows(bits, sent, received, owner):
    bit, _ = stage_bits(bits, len(bits) - 1)
    mine = ((owner[...] ^ lax.axis_index("prow")) & bit) == 0
    return jnp.where(mine, sent[...], received[-1][...])


def displaced_rows(bits, received, top):
    row = lax.axis_index("prow")
    value = received[-1][...]
    for stage in reversed(range(len(bits) - 1)):
        bit, known = stage_bits(bits, stage)
        value = jnp.where((row & ~(known | bit)) == 0, received[stage][...], value)
    return jnp.where(row == 0, top, value)


def place_of(chip, core, chips, rows):
    return pl.multiple_of((lax.rem(chip + chips, chips) * 2 + core) * rows, rows)


def rows_of(ref, index, count=1):
    rows = ref.shape[0] // count
    return ref.at[pl.ds(index * rows, rows), :]


def ring_blocks(refs):
    chips = (len(refs) + 1) // 2
    mine, joint, rest = refs[:chips], refs[chips], refs[chips + 1 :]
    rows = mine[0].shape[0]
    others = [rows_of(joint, 0, 2), rows_of(joint, 1, 2), *rest]
    chip, core = lax.axis_index("pcol") // 2, lax.rem(lax.axis_index("pcol"), 2)
    found = []
    for order, distance in enumerate(ring_order(chips)):
        found.append((mine[order], place_of(chip - distance, core, chips, rows)))
        found.append((others[order], place_of(chip - distance, 1 - core, chips, rows)))
    return found


def pair_blocks(refs):
    own, near, far, far_back, *pairs = refs
    rows = own.shape[0]
    chips = len(pairs) + 2
    hops = len(pairs) // 2
    chip, core = lax.axis_index("pcol") // 2, lax.rem(lax.axis_index("pcol"), 2)
    opposite = chip + chips // 2
    found = [
        (own, place_of(chip, core, chips, rows)),
        (near, place_of(chip, 1 - core, chips, rows)),
        (far, place_of(opposite, core, chips, rows)),
        (far_back, place_of(opposite, 1 - core, chips, rows)),
    ]
    for hop in range(hops):
        along = (hop + 1) * (1 - 2 * core)
        for half in range(2):
            owner = core if half == 0 else 1 - core
            found.append((rows_of(pairs[hop], half, 2), place_of(chip - along, owner, chips, rows)))
            found.append((rows_of(pairs[hops + hop], half, 2), place_of(chip + along, 1 - owner, chips, rows)))
    return found


def solve(bits, step, matrix, pivots, inverse, owner, ahead, places, sent, *refs):
    refs = list(refs)
    received = [refs.pop(0) for _ in bits]
    blocks, (upper_out, displaced_out, slots_out) = refs[:-3], refs[-3:]
    rows_dev = matrix.shape[0]
    picked = picked_rows(bits, sent, received, owner)
    width = picked.shape[0]
    upper = dot(split(inverse[step]), split(picked))
    upper_out[...] = upper
    displaced = displaced_rows(bits, received, matrix[step * width : (step + 1) * width, :])
    displaced_out[...] = displaced
    high = low = None
    for block, start in ring_blocks(blocks):
        rows = block.shape[0]
        local = places[:, :rows] - start
        gather = one_hot(local, iota((width, rows), 1))
        block_high, block_low = split(block[...])
        term_high, term_low = product(gather, block_high), product(gather, block_low)
        high = term_high if high is None else high + term_high
        low = term_low if low is None else low + term_low
    moved = one_hot(places[...], local_rows(pivots, step, rows_dev))
    factor = (high.astype(BF16), low.astype(BF16))
    slots_out[...] = ahead[...] + (pick(moved, split(displaced)) - dot(factor, split(upper)))


def assemble(step, blocks, rows_dev, width, high, low):
    limit = (step + 1) * width - lax.axis_index("prow") * rows_dev
    for block, start in blocks:
        rows = block.shape[0]
        below = start + iota(block.shape, 0) >= limit
        block_high, block_low = split(jnp.where(below, -block[...], F32(0)))
        high[pl.ds(start, rows), :] = block_high
        low[pl.ds(start, rows), :] = block_low


def halve(step, rows_dev, width, *refs):
    assemble(step, pair_blocks(refs[:-2]), rows_dev, width, refs[-2], refs[-1])


def update(step, base, pivots, upper_in, displaced_in, *refs):
    blocks, (out, top_out, high, low) = refs[:-4], refs[-4:]
    rows_dev = base.shape[0]
    width = upper_in.shape[0]
    assemble(step, ring_blocks(blocks), rows_dev, width, high, low)
    offset = local_rows(pivots, step, rows_dev)
    later = local_rows(pivots, step + 1, rows_dev)
    upper = split(upper_in[...])
    displaced = split(displaced_in[...])
    for start in range(0, rows_dev, width):
        part = slice(start, start + width)
        rows = iota((width, width), 0) + start
        value = base[part, :] + (pick(one_hot(rows, offset), displaced) + dot((high[part, :], low[part, :]), upper))
        if start == step * width:
            value = jnp.where(lax.axis_index("prow") == 0, upper_in[...], value)
        if start == (step + 1) * width:
            top_out[...] = value
        hit = jnp.where(later == rows, F32(1), F32(0))
        out[part, :] = jnp.where(jnp.sum(hit, axis=1, keepdims=True) == 0, value, F32(0))


def finish(bits, step, base, pivots, inverse, owner, top, high, low, sent, *refs):
    received, (out, result, sems) = refs[:-3], refs[-3:]
    rows_dev = base.shape[0]
    picked = picked_rows(bits, sent, received, owner)
    width = picked.shape[0]
    upper_full = dot(split(inverse[step]), split(picked))
    offset = local_rows(pivots, step, rows_dev)
    upper = split(upper_full)
    displaced = split(displaced_rows(bits, received, top[...]))
    copies = []
    for start in range(0, rows_dev, width):
        part = slice(start, start + width)
        rows = iota((width, width), 0) + start
        value = base[part, :] + (pick(one_hot(rows, offset), displaced) + dot((high[part, :], low[part, :]), upper))
        if start == step * width:
            value = jnp.where(lax.axis_index("prow") == 0, upper_full, value)
        result[part, :] = value
        copies.append(
            pltpu.make_async_copy(result.at[pl.ds(start, width), :], out.at[pl.ds(start, width), :], sems.at[len(copies)])
        )
        copies[-1].start()
    for copy in copies:
        copy.wait()


def stack(one, other, out):
    rows = one.shape[0]
    out[:rows, :] = one[...]
    out[rows:, :] = other[...]


def pack(own, near, before, out):
    rows = own.shape[0]
    out[:rows, :] = own[...]
    out[rows:, :] = near[...]


def ring_order(chips):
    return [0] + list(range(1, chips // 2 + 1)) + list(range(chips - 1, chips // 2, -1))


def release(panel, before, out):
    out[...] = panel[...]


def shift(block, distance, count):
    return lax.ppermute(block, "pcol", [(i, (i + 2 * distance) % count) for i in range(count)])


def across(block, count):
    return lax.ppermute(block, "pcol", [(i, i ^ 1) for i in range(count)])


def forwarded(block, down, count):
    chips = count // 2
    own = [block]
    for distance in ring_order(chips)[1:]:
        if distance <= chips // 2:
            own.append(shift(own[-1], 1, count))
        else:
            own.append(shift(down if distance == chips - 1 else own[-1], -1, count))
    return own


def passed(pair, count):
    onward = [(i, (i + (2 if i % 2 == 0 else -2)) % count) for i in range(count)]
    pairs = [pair]
    for _ in range(count // 4 - 1):
        pairs.append(lax.ppermute(pairs[-1], "pcol", onward))
    return pairs[1:]


def per_device(mesh, matrix, l_panels, l_inverse, pivots):
    rows_dev, columns = matrix.shape
    steps, width = pivots.shape
    process_rows, process_columns = mesh.shape["prow"], mesh.shape["pcol"]
    bits = [1 << b for b in range(process_rows.bit_length() - 1)]
    shape = jax.ShapeDtypeStruct
    square = shape((width, columns), F32)
    full = shape((rows_dev, columns), F32)

    def call(kernel, name, operands, outs, specs=None, out_specs=None, scratch=()):
        return pl.pallas_call(
            kernel,
            out_shape=outs,
            in_specs=specs or [VMEM] * len(operands),
            out_specs=out_specs or jax.tree.map(lambda _: VMEM, outs),
            scratch_shapes=scratch,
            compiler_params=GRANT,
            name=name,
        )(*operands)

    def exchange(sent, step, before=()):
        received = []
        for stage in range(len(bits)):
            if stage:
                operands = [sent, received[-1], owner[step], *before]
                specs = [VMEM] * 3 + [ANY] * len(before)
                sent = call(functools.partial(merge, bits, stage - 1), "merge", operands, square, specs=specs)
            pairs = []
            for i in range(process_rows):
                for j in range(process_columns):
                    bit = bits[len(bits) - 1 - stage] if j % 2 else bits[stage]
                    pairs.append((i * process_columns + j, (i ^ bit) * process_columns + j))
            received.append(lax.ppermute(sent, ("prow", "pcol"), pairs))
        return sent, received

    chunks = rows_dev // width
    halves = [pltpu.VMEM((rows_dev, l_panels.shape[2]), BF16)] * 2
    block = shape(l_panels.shape[1:], F32)
    matrix, pivots, *own = call(
        load,
        "load",
        [pltpu.with_memory_space_constraint(x, pltpu.HBM) for x in (matrix, pivots, l_panels)],
        [full, shape(pivots.shape, pivots.dtype)] + [block] * steps,
        specs=[HBM] * 3,
        scratch=[pltpu.SemaphoreType.DMA((2 + steps,))],
    )
    slots = call(first_slots, "first_slots", [matrix, pivots], square)

    owner = jnp.broadcast_to((pivots // rows_dev)[:, :, None], (steps, width, columns))

    near = across(own[1], process_columns)

    def after(panel, before):
        return call(release, "release", [panel, before], block, specs=[VMEM, ANY])

    base, ahead, places = call(
        prepare, "prepare", [matrix, pivots], [full, square, shape((width, width), jnp.int32)]
    )
    first = forwarded(own[0], after(own[0], places), process_columns)
    joint = call(stack, "stack", first[:2], shape((2 * block.shape[0], block.shape[1]), F32))
    joint = across(joint, process_columns)
    first += [joint] + [across(piece, process_columns) for piece in first[2:]]
    sent, received = exchange(slots, 0, [joint])
    two = shape((2 * block.shape[0], block.shape[1]), F32)
    pair = call(pack, "pack", [own[1], near, sent], two, specs=[VMEM, VMEM, ANY])
    operands = [matrix, pivots, l_inverse, owner[0], ahead, places, sent, *received, *first]
    upper, displaced, slots = call(functools.partial(solve, bits, 0), "solve", operands, [square] * 3)
    far = shift(after(own[1], slots), process_columns // 4, process_columns)
    pairs = passed(pair, process_columns)
    second = [own[1], near, far, across(far, process_columns)]
    second += pairs + [across(piece, process_columns) for piece in pairs]
    base, top = call(
        functools.partial(update, 0),
        "update",
        [base, pivots, upper, displaced, *first],
        [full, square],
        scratch=halves,
    )
    sent, received = exchange(slots, 1)
    high, low = call(
        functools.partial(halve, 1, rows_dev, width),
        "halve",
        second,
        [shape((rows_dev, l_panels.shape[2]), BF16)] * 2,
    )
    return call(
        functools.partial(finish, bits, 1),
        "finish",
        [base, pivots, l_inverse, owner[1], top, high, low, sent, *received],
        full,
        out_specs=HBM,
        scratch=[pltpu.VMEM((rows_dev, columns), F32), pltpu.SemaphoreType.DMA((chunks,))],
    )


def solution(mesh):
    placed = (P("prow", "pcol"), P(None, ("prow", "pcol"), None), P(), P())
    return jax.shard_map(
        functools.partial(per_device, mesh), mesh=mesh, in_specs=placed, out_specs=P("prow", "pcol"), check_vma=False
    )
```

```python
import functools

import jax
import jax.numpy as jnp
from jax import lax
from jax.experimental import pallas as pl
from jax.experimental.pallas import tpu as pltpu
from jax.sharding import PartitionSpec as P

VMEM = pl.BlockSpec(memory_space=pltpu.VMEM)
ANY = pl.BlockSpec(memory_space=pl.ANY)
HBM = pl.BlockSpec(memory_space=pltpu.HBM)
GRANT = pltpu.CompilerParams(vmem_limit_bytes=40 * 1024 * 1024)
F32 = jnp.float32
BF16 = jnp.bfloat16
NOWHERE = -(1 << 24)
TAIL = 16
SPARE = 16


def product(left, right):
    return jnp.dot(left, right, preferred_element_type=F32)


def split(values):
    high = values.astype(BF16)
    low = (values - high.astype(F32)).astype(BF16)
    return high, low


def dot(left, right):
    return product(left[0], right[0]) + (product(left[0], right[1]) + product(left[1], right[0]))


def pick(chosen, right):
    return product(chosen, right[0]) + product(chosen, right[1])


def one_hot(left, right):
    return jnp.where(left == right, F32(1), F32(0)).astype(BF16)


def iota(shape, dimension):
    return lax.broadcasted_iota(jnp.int32, shape, dimension)


def column_of(row):
    n = row.shape[1]
    spread = jnp.where(iota((n, n), 0) == iota((n, n), 1), row.astype(F32), F32(0))
    return jnp.sum(spread, axis=1, keepdims=True).astype(jnp.int32)


def local_rows(pivots, step, rows_dev):
    offset = pivots[step : step + 1, :] - lax.axis_index("prow") * rows_dev
    return jnp.where((offset >= 0) & (offset < rows_dev), offset, NOWHERE)


def slot_rows(pivots, step, rows_dev):
    offset = local_rows(pivots, step, rows_dev)
    width = offset.shape[1]
    top = jnp.where(lax.axis_index("prow") == 0, step * width + iota(offset.shape, 1), NOWHERE)
    return jnp.where(offset >= 0, offset, top)


def load(matrix, pivots, panels, held, chosen, *refs):
    blocks, sems = refs[:-1], refs[-1]
    sources = [panels.at[step] for step in range(len(blocks))] + [pivots, matrix]
    targets = [*blocks, chosen, held]
    copies = [pltpu.make_async_copy(*pair, sems.at[i]) for i, pair in enumerate(zip(sources, targets))]
    for copy in copies:
        copy.start()
    for copy in copies:
        copy.wait()


def first_slots(matrix, pivots, out):
    rows_dev = matrix.shape[0]
    place = column_of(slot_rows(pivots, 0, rows_dev))
    width = place.shape[0]
    total = None
    for start in range(0, rows_dev, width):
        gather = one_hot(place, iota((width, width), 1) + start)
        term = pick(gather, split(matrix[start : start + width, :]))
        total = term if total is None else total + term
    out[...] = total


def prepare(matrix, pivots, base, ahead, places):
    rows_dev = matrix.shape[0]
    offset = local_rows(pivots, 0, rows_dev)
    width = offset.shape[1]
    place = column_of(slot_rows(pivots, 1, rows_dev))
    places[...] = jnp.broadcast_to(place, places.shape)
    total = None
    for start in range(0, rows_dev, width):
        hit = jnp.where(offset == iota((width, width), 0) + start, F32(1), F32(0))
        keep = jnp.sum(hit, axis=1, keepdims=True) == 0
        kept = jnp.where(keep, matrix[start : start + width, :], F32(0))
        base[start : start + width, :] = kept
        gather = one_hot(place, iota((width, width), 1) + start)
        term = pick(gather, split(kept))
        total = term if total is None else total + term
    ahead[...] = total


def stage_bits(bits, stage):
    odd = lax.rem(lax.axis_index("pcol"), 2) == 1
    bit = jnp.where(odd, bits[len(bits) - 1 - stage], bits[stage])
    known = jnp.where(odd, sum(bits[len(bits) - stage :]) if stage else 0, sum(bits[:stage]))
    return bit, known


def merge(bits, stage, sent, received, owner, *refs):
    row = lax.axis_index("prow")
    bit, known = stage_bits(bits, stage)
    partner = row ^ bit
    who = owner[...]
    keep = ~known
    theirs = ((who ^ partner) & keep) == 0
    neither = ((who ^ row) & ~(known | bit)) != 0
    take = theirs | (neither & ((partner & keep) == 0))
    refs[-1][...] = jnp.where(take, received[...], sent[...])


def picked_rows(bits, sent, received, owner):
    bit, _ = stage_bits(bits, len(bits) - 1)
    mine = ((owner[...] ^ lax.axis_index("prow")) & bit) == 0
    return jnp.where(mine, sent[...], received[-1][...])


def displaced_rows(bits, received, top):
    row = lax.axis_index("prow")
    value = received[-1][...]
    for stage in reversed(range(len(bits) - 1)):
        bit, known = stage_bits(bits, stage)
        value = jnp.where((row & ~(known | bit)) == 0, received[stage][...], value)
    return jnp.where(row == 0, top, value)


def place_of(chip, core, chips, rows):
    return pl.multiple_of((lax.rem(chip + chips, chips) * 2 + core) * rows, rows)


def rows_of(ref, index, count=1):
    rows = ref.shape[0] // count
    return ref.at[pl.ds(index * rows, rows), :]


def ring_blocks(refs):
    chips = (len(refs) + 1) // 2
    mine, joint, rest = refs[:chips], refs[chips], refs[chips + 1 :]
    rows = mine[0].shape[0]
    others = [rows_of(joint, 0, 2), rows_of(joint, 1, 2), *rest]
    chip, core = lax.axis_index("pcol") // 2, lax.rem(lax.axis_index("pcol"), 2)
    found = []
    for order, distance in enumerate(ring_order(chips)):
        found.append((mine[order], place_of(chip - distance, core, chips, rows)))
        found.append((others[order], place_of(chip - distance, 1 - core, chips, rows)))
    return found


def pair_blocks(refs):
    own, near, far, far_back, *rest = refs
    rows = own.shape[0]
    hops, tail = len(rest) // 2, tail_of(rows)
    pairs, back = rest[:hops], rest[hops:]
    chips = 2 * hops + 2
    chip, core = lax.axis_index("pcol") // 2, lax.rem(lax.axis_index("pcol"), 2)
    opposite = chip + chips // 2
    found = [
        (own, place_of(chip, core, chips, rows)),
        (near, place_of(chip, 1 - core, chips, rows)),
        (far, place_of(opposite, core, chips, rows)),
        (far_back.at[pl.ds(0, rows), :], place_of(opposite, 1 - core, chips, rows)),
    ]
    for hop in range(hops):
        along = (hop + 1) * (1 - 2 * core)
        for half in range(2):
            place = place_of(chip - along, core if half == 0 else 1 - core, chips, rows)
            found.append((pairs[hop].at[pl.ds(half * rows, rows), :], place))
            place = place_of(chip + along, 1 - core if half == 0 else core, chips, rows)
            held = rows - half * tail
            found.append((back[hop].at[pl.ds(half * rows, held), :], place))
        if tail:
            found.append((far_back.at[pl.ds(rows + hop * tail, tail), :], pl.multiple_of(place + held, tail)))
    return found


def solve(bits, step, matrix, pivots, inverse, owner, ahead, places, sent, *refs):
    refs = list(refs)
    received = [refs.pop(0) for _ in bits]
    blocks, (upper_out, displaced_out, slots_out) = refs[:-3], refs[-3:]
    rows_dev = matrix.shape[0]
    picked = picked_rows(bits, sent, received, owner)
    width = picked.shape[0]
    upper = dot(split(inverse[step]), split(picked))
    upper_out[...] = upper
    displaced = displaced_rows(bits, received, matrix[step * width : (step + 1) * width, :])
    displaced_out[...] = displaced
    high = low = None
    for block, start in ring_blocks(blocks):
        rows = block.shape[0]
        local = places[:, :rows] - start
        gather = one_hot(local, iota((width, rows), 1))
        block_high, block_low = split(block[...])
        term_high, term_low = product(gather, block_high), product(gather, block_low)
        high = term_high if high is None else high + term_high
        low = term_low if low is None else low + term_low
    moved = one_hot(places[...], local_rows(pivots, step, rows_dev))
    factor = (high.astype(BF16), low.astype(BF16))
    slots_out[...] = ahead[...] + (pick(moved, split(displaced)) - dot(factor, split(upper)))


def assemble(step, blocks, rows_dev, width, high, low):
    limit = (step + 1) * width - lax.axis_index("prow") * rows_dev
    for block, start in blocks:
        rows = block.shape[0]
        below = start + iota(block.shape, 0) >= limit
        block_high, block_low = split(jnp.where(below, -block[...], F32(0)))
        high[pl.ds(start, rows), :] = block_high
        low[pl.ds(start, rows), :] = block_low


def halve(step, rows_dev, width, *refs):
    assemble(step, pair_blocks(refs[:-2]), rows_dev, width, refs[-2], refs[-1])


def update(step, base, pivots, upper_in, displaced_in, *refs):
    blocks, (out, top_out, high, low) = refs[:-4], refs[-4:]
    rows_dev = base.shape[0]
    width = upper_in.shape[0]
    assemble(step, ring_blocks(blocks), rows_dev, width, high, low)
    offset = local_rows(pivots, step, rows_dev)
    later = local_rows(pivots, step + 1, rows_dev)
    upper = split(upper_in[...])
    displaced = split(displaced_in[...])
    for start in range(0, rows_dev, width):
        part = slice(start, start + width)
        rows = iota((width, width), 0) + start
        value = base[part, :] + (pick(one_hot(rows, offset), displaced) + dot((high[part, :], low[part, :]), upper))
        if start == step * width:
            value = jnp.where(lax.axis_index("prow") == 0, upper_in[...], value)
        if start == (step + 1) * width:
            top_out[...] = value
        hit = jnp.where(later == rows, F32(1), F32(0))
        out[part, :] = jnp.where(jnp.sum(hit, axis=1, keepdims=True) == 0, value, F32(0))


def finish(bits, step, base, pivots, inverse, owner, top, high, low, sent, *refs):
    received, (out, result, sems) = refs[:-3], refs[-3:]
    rows_dev = base.shape[0]
    picked = picked_rows(bits, sent, received, owner)
    width = picked.shape[0]
    upper_full = dot(split(inverse[step]), split(picked))
    offset = local_rows(pivots, step, rows_dev)
    upper = split(upper_full)
    displaced = split(displaced_rows(bits, received, top[...]))
    copies = []
    for start in range(0, rows_dev, width):
        part = slice(start, start + width)
        rows = iota((width, width), 0) + start
        value = base[part, :] + (pick(one_hot(rows, offset), displaced) + dot((high[part, :], low[part, :]), upper))
        if start == step * width:
            value = jnp.where(lax.axis_index("prow") == 0, upper_full, value)
        result[part, :] = value
        copies.append(
            pltpu.make_async_copy(result.at[pl.ds(start, width), :], out.at[pl.ds(start, width), :], sems.at[len(copies)])
        )
        copies[-1].start()
    for copy in copies:
        copy.wait()


def stack(one, other, out):
    rows = one.shape[0]
    out[:rows, :] = one[...]
    out[rows:, :] = other[...]


def pack(own, near, before, out):
    rows = own.shape[0]
    out[:rows, :] = own[...]
    out[rows : 2 * rows, :] = near[...]
    out[2 * rows :, :] = own[: out.shape[0] - 2 * rows, :]


def ring_order(chips):
    return [0] + list(range(1, chips // 2 + 1)) + list(range(chips - 1, chips // 2, -1))


def tail_of(rows):
    return TAIL if rows > TAIL else 0


def tails(far, *refs):
    pairs, out = refs[:-1], refs[-1]
    rows = far.shape[0]
    out[:rows, :] = far[...]
    for hop, pair in enumerate(pairs):
        start, tail = rows + hop * tail_of(rows), tail_of(rows)
        if tail:
            out[start : start + tail, :] = pair[2 * rows - tail : 2 * rows, :]


def release(panel, before, out):
    out[...] = panel[: out.shape[0], :]


def shift(block, distance, count):
    return lax.ppermute(block, "pcol", [(i, (i + 2 * distance) % count) for i in range(count)])


def across(block, count):
    return lax.ppermute(block, "pcol", [(i, i ^ 1) for i in range(count)])


def forwarded(block, down, count):
    chips = count // 2
    own = [block]
    for distance in ring_order(chips)[1:]:
        if distance <= chips // 2:
            own.append(shift(own[-1], 1, count))
        else:
            own.append(shift(down if distance == chips - 1 else own[-1], -1, count))
    return own


def passed(pair, count):
    onward = [(i, (i + (2 if i % 2 == 0 else -2)) % count) for i in range(count)]
    pairs = [pair]
    for _ in range(count // 4 - 1):
        pairs.append(lax.ppermute(pairs[-1], "pcol", onward))
    return pairs[1:]


def per_device(mesh, matrix, l_panels, l_inverse, pivots):
    rows_dev, columns = matrix.shape
    steps, width = pivots.shape
    process_rows, process_columns = mesh.shape["prow"], mesh.shape["pcol"]
    bits = [1 << b for b in range(process_rows.bit_length() - 1)]
    shape = jax.ShapeDtypeStruct
    square = shape((width, columns), F32)
    full = shape((rows_dev, columns), F32)

    def call(kernel, name, operands, outs, specs=None, out_specs=None, scratch=()):
        return pl.pallas_call(
            kernel,
            out_shape=outs,
            in_specs=specs or [VMEM] * len(operands),
            out_specs=out_specs or jax.tree.map(lambda _: VMEM, outs),
            scratch_shapes=scratch,
            compiler_params=GRANT,
            name=name,
        )(*operands)

    def exchange(sent, step, before=()):
        received = []
        for stage in range(len(bits)):
            if stage:
                operands = [sent, received[-1], owner[step], *before]
                specs = [VMEM] * 3 + [ANY] * len(before)
                sent = call(functools.partial(merge, bits, stage - 1), "merge", operands, square, specs=specs)
            pairs = []
            for i in range(process_rows):
                for j in range(process_columns):
                    bit = bits[len(bits) - 1 - stage] if j % 2 else bits[stage]
                    pairs.append((i * process_columns + j, (i ^ bit) * process_columns + j))
            received.append(lax.ppermute(sent, ("prow", "pcol"), pairs))
        return sent, received

    chunks = rows_dev // width
    halves = [pltpu.VMEM((rows_dev, l_panels.shape[2]), BF16)] * 2
    block = shape(l_panels.shape[1:], F32)
    matrix, pivots, *own = call(
        load,
        "load",
        [pltpu.with_memory_space_constraint(x, pltpu.HBM) for x in (matrix, pivots, l_panels)],
        [full, shape(pivots.shape, pivots.dtype)] + [block] * steps,
        specs=[HBM] * 3,
        scratch=[pltpu.SemaphoreType.DMA((2 + steps,))],
    )
    slots = call(first_slots, "first_slots", [matrix, pivots], square)

    owner = jnp.broadcast_to((pivots // rows_dev)[:, :, None], (steps, width, columns))

    near = across(own[1], process_columns)

    def after(panel, before, rows=block.shape[0]):
        return call(release, "release", [panel, before], shape((rows, block.shape[1]), F32), specs=[VMEM, ANY])

    base, ahead, places = call(
        prepare, "prepare", [matrix, pivots], [full, square, shape((width, width), jnp.int32)]
    )
    first = forwarded(own[0], after(own[0], places), process_columns)
    joint = call(stack, "stack", first[:2], shape((2 * block.shape[0], block.shape[1]), F32))
    joint = across(joint, process_columns)
    first += [joint] + [across(piece, process_columns) for piece in first[2:]]
    sent, received = exchange(slots, 0, [joint])
    two = shape((2 * block.shape[0] + SPARE, block.shape[1]), F32)
    pair = call(pack, "pack", [own[1], near, sent], two, specs=[VMEM, VMEM, ANY])
    operands = [matrix, pivots, l_inverse, owner[0], ahead, places, sent, *received, *first]
    upper, displaced, slots = call(functools.partial(solve, bits, 0), "solve", operands, [square] * 3)
    far = shift(after(own[1], slots), process_columns // 4, process_columns)
    pairs = passed(pair, process_columns)
    rows = block.shape[0]
    joint = call(tails, "tails", [far, *pairs], shape((rows + tail_of(rows) * len(pairs), block.shape[1]), F32))
    second = [own[1], near, far, across(joint, process_columns)]
    second += pairs + [across(after(piece, own[1], 2 * rows - tail_of(rows)), process_columns) for piece in pairs]
    base, top = call(
        functools.partial(update, 0),
        "update",
        [base, pivots, upper, displaced, *first],
        [full, square],
        scratch=halves,
    )
    sent, received = exchange(slots, 1)
    high, low = call(
        functools.partial(halve, 1, rows_dev, width),
        "halve",
        second,
        [shape((rows_dev, l_panels.shape[2]), BF16)] * 2,
    )
    return call(
        functools.partial(finish, bits, 1),
        "finish",
        [base, pivots, l_inverse, owner[1], top, high, low, sent, *received],
        full,
        out_specs=HBM,
        scratch=[pltpu.VMEM((rows_dev, columns), F32), pltpu.SemaphoreType.DMA((chunks,))],
    )


def solution(mesh):
    placed = (P("prow", "pcol"), P(None, ("prow", "pcol"), None), P(), P())
    return jax.shard_map(
        functools.partial(per_device, mesh), mesh=mesh, in_specs=placed, out_specs=P("prow", "pcol"), check_vma=False
    )
```

```python
import functools

import jax
import jax.numpy as jnp
from jax import lax
from jax.experimental import pallas as pl
from jax.experimental.pallas import tpu as pltpu
from jax.sharding import PartitionSpec as P

VMEM = pl.BlockSpec(memory_space=pltpu.VMEM)
ANY = pl.BlockSpec(memory_space=pl.ANY)
HBM = pl.BlockSpec(memory_space=pltpu.HBM)
GRANT = pltpu.CompilerParams(vmem_limit_bytes=40 * 1024 * 1024)
F32 = jnp.float32
BF16 = jnp.bfloat16
NOWHERE = -(1 << 24)
TAIL = 16
COST = {"holders": 3 * 10**9}
PARTS = 4
SPARE = 16


def product(left, right):
    return jnp.dot(left, right, preferred_element_type=F32)


def split(values):
    high = values.astype(BF16)
    low = (values - high.astype(F32)).astype(BF16)
    return high, low


def dot(left, right):
    return product(left[0], right[0]) + (product(left[0], right[1]) + product(left[1], right[0]))


def pick(chosen, right):
    return product(chosen, right[0]) + product(chosen, right[1])


def one_hot(left, right):
    return jnp.where(left == right, F32(1), F32(0)).astype(BF16)


def iota(shape, dimension):
    return lax.broadcasted_iota(jnp.int32, shape, dimension)


def column_of(row):
    n = row.shape[1]
    spread = jnp.where(iota((n, n), 0) == iota((n, n), 1), row.astype(F32), F32(0))
    return jnp.sum(spread, axis=1, keepdims=True).astype(jnp.int32)


def local_rows(pivots, step, rows_dev):
    offset = pivots[step : step + 1, :] - lax.axis_index("prow") * rows_dev
    return jnp.where((offset >= 0) & (offset < rows_dev), offset, NOWHERE)


def slot_rows(pivots, step, rows_dev):
    offset = local_rows(pivots, step, rows_dev)
    width = offset.shape[1]
    top = jnp.where(lax.axis_index("prow") == 0, step * width + iota(offset.shape, 1), NOWHERE)
    return jnp.where(offset >= 0, offset, top)


def load(matrix, pivots, panels, held, chosen, *refs):
    blocks, sems = refs[:-1], refs[-1]
    rows = held.shape[0] // PARTS
    parts = [pl.ds(part * rows, rows) for part in range(PARTS)]
    sources = [panels.at[step] for step in range(len(blocks))] + [pivots] + [matrix.at[part, :] for part in parts]
    targets = [*blocks, chosen] + [held.at[part, :] for part in parts]
    copies = [pltpu.make_async_copy(*pair, sems.at[i]) for i, pair in enumerate(zip(sources, targets))]
    for copy in copies:
        copy.start()
    for copy in copies:
        copy.wait()


def first_slots(matrix, pivots, out):
    rows_dev = matrix.shape[0]
    place = column_of(slot_rows(pivots, 0, rows_dev))
    width = place.shape[0]
    total = None
    for start in range(0, rows_dev, width):
        gather = one_hot(place, iota((width, width), 1) + start)
        term = pick(gather, split(matrix[start : start + width, :]))
        total = term if total is None else total + term
    out[...] = total


def holders(rows_dev, pivots, *owners):
    for step, owner in enumerate(owners):
        owner[...] = jnp.broadcast_to(column_of(pivots[step : step + 1, :]) // rows_dev, owner.shape)


def prepare(matrix, pivots, base, ahead, places):
    rows_dev = matrix.shape[0]
    offset = local_rows(pivots, 0, rows_dev)
    width = offset.shape[1]
    place = column_of(slot_rows(pivots, 1, rows_dev))
    places[...] = jnp.broadcast_to(place, places.shape)
    total = None
    for start in range(0, rows_dev, width):
        hit = jnp.where(offset == iota((width, width), 0) + start, F32(1), F32(0))
        keep = jnp.sum(hit, axis=1, keepdims=True) == 0
        kept = jnp.where(keep, matrix[start : start + width, :], F32(0))
        base[start : start + width, :] = kept
        gather = one_hot(place, iota((width, width), 1) + start)
        term = pick(gather, split(kept))
        total = term if total is None else total + term
    ahead[...] = total


def stage_bits(bits, stage):
    odd = lax.rem(lax.axis_index("pcol"), 2) == 1
    bit = jnp.where(odd, bits[len(bits) - 1 - stage], bits[stage])
    known = jnp.where(odd, sum(bits[len(bits) - stage :]) if stage else 0, sum(bits[:stage]))
    return bit, known


def merge(bits, stage, sent, received, owner, *refs):
    row = lax.axis_index("prow")
    bit, known = stage_bits(bits, stage)
    partner = row ^ bit
    who = owner[...]
    keep = ~known
    theirs = ((who ^ partner) & keep) == 0
    neither = ((who ^ row) & ~(known | bit)) != 0
    take = theirs | (neither & ((partner & keep) == 0))
    refs[-1][...] = jnp.where(take, received[...], sent[...])


def picked_rows(bits, sent, received, owner):
    bit, _ = stage_bits(bits, len(bits) - 1)
    mine = ((owner[...] ^ lax.axis_index("prow")) & bit) == 0
    return jnp.where(mine, sent[...], received[-1][...])


def displaced_rows(bits, received, top):
    row = lax.axis_index("prow")
    value = received[-1][...]
    for stage in reversed(range(len(bits) - 1)):
        bit, known = stage_bits(bits, stage)
        value = jnp.where((row & ~(known | bit)) == 0, received[stage][...], value)
    return jnp.where(row == 0, top, value)


def place_of(chip, core, chips, rows):
    return pl.multiple_of((lax.rem(chip + chips, chips) * 2 + core) * rows, rows)


def rows_of(ref, index, count=1):
    rows = ref.shape[0] // count
    return ref.at[pl.ds(index * rows, rows), :]


def ring_blocks(refs):
    chips = (len(refs) + 1) // 2
    mine, joint, rest = refs[:chips], refs[chips], refs[chips + 1 :]
    rows = next(ref for ref in [*mine, *rest] if ref is not None).shape[0]
    others = [joint if joint is None else rows_of(joint, half, 2) for half in range(2)] + list(rest)
    chip, core = lax.axis_index("pcol") // 2, lax.rem(lax.axis_index("pcol"), 2)
    found = []
    for order, distance in enumerate(ring_order(chips)):
        found.append((mine[order], place_of(chip - distance, core, chips, rows)))
        found.append((others[order], place_of(chip - distance, 1 - core, chips, rows)))
    return found


def pair_blocks(refs):
    own, near, far, far_back, *rest = refs
    rows = own.shape[0]
    hops, tail = len(rest) // 2, tail_of(rows)
    pairs, back = rest[:hops], rest[hops:]
    chips = 2 * hops + 2
    chip, core = lax.axis_index("pcol") // 2, lax.rem(lax.axis_index("pcol"), 2)
    opposite = chip + chips // 2
    found = [
        (own, place_of(chip, core, chips, rows)),
        (near, place_of(chip, 1 - core, chips, rows)),
        (far, place_of(opposite, core, chips, rows)),
        (far_back.at[pl.ds(0, rows), :], place_of(opposite, 1 - core, chips, rows)),
    ]
    for hop in range(hops):
        along = (hop + 1) * (1 - 2 * core)
        for half in range(2):
            place = place_of(chip - along, core if half == 0 else 1 - core, chips, rows)
            found.append((pairs[hop].at[pl.ds(half * rows, rows), :], place))
            place = place_of(chip + along, 1 - core if half == 0 else core, chips, rows)
            held = rows - half * tail
            found.append((back[hop].at[pl.ds(half * rows, held), :], place))
        if tail:
            found.append((far_back.at[pl.ds(rows + hop * tail, tail), :], pl.multiple_of(place + held, tail)))
    return found


def panel_rows(places, blocks):
    high = low = None
    for block, start in blocks:
        rows = block.shape[0]
        gather = one_hot(places[:, :rows] - start, iota((places.shape[0], rows), 1))
        block_high, block_low = split(block[...])
        term_high, term_low = product(gather, block_high), product(gather, block_low)
        high = term_high if high is None else high + term_high
        low = term_low if low is None else low + term_low
    return high, low


def late_blocks(chips):
    return [chips + chips // 2 - 1, 2 * chips - 2]


def collect(late, places, *refs):
    blocks, (high, low) = list(refs[:-2]), refs[-2:]
    for position in late:
        blocks.insert(position, None)
    found_high, found_low = panel_rows(places, [pair for pair in ring_blocks(blocks) if pair[0] is not None])
    high[...] = found_high.astype(BF16)
    low[...] = found_low.astype(BF16)


def solve(bits, step, late, matrix, pivots, inverse, owner, ahead, places, sent, *refs):
    refs = list(refs)
    received = [refs.pop(0) for _ in bits]
    high, low, *found, upper_out, displaced_out, slots = refs
    rows_dev = matrix.shape[0]
    picked = picked_rows(bits, sent, received, owner)
    width = picked.shape[0]
    upper = dot(split(inverse[step]), split(picked))
    upper_out[...] = upper
    displaced = displaced_rows(bits, received, matrix[step * width : (step + 1) * width, :])
    displaced_out[...] = displaced
    moved = one_hot(places[...], local_rows(pivots, step, rows_dev))
    blocks = [None] * (rows_dev // found[0].shape[0] - 1)
    for position, block in zip(late, found):
        blocks[position] = block
    rest_high, rest_low = panel_rows(places, [pair for pair in ring_blocks(blocks) if pair[0] is not None])
    factor = ((high[...].astype(F32) + rest_high).astype(BF16), (low[...].astype(F32) + rest_low).astype(BF16))
    slots[...] = ahead[...] + (pick(moved, split(displaced)) - dot(factor, split(upper)))


def assemble(step, blocks, rows_dev, width, high, low):
    limit = (step + 1) * width - lax.axis_index("prow") * rows_dev
    for block, start in blocks:
        rows = block.shape[0]
        below = start + iota(block.shape, 0) >= limit
        block_high, block_low = split(jnp.where(below, -block[...], F32(0)))
        high[pl.ds(start, rows), :] = block_high
        low[pl.ds(start, rows), :] = block_low


def halve(step, rows_dev, width, *refs):
    assemble(step, pair_blocks(refs[:-2]), rows_dev, width, refs[-2], refs[-1])


def update(step, base, pivots, upper_in, displaced_in, *refs):
    blocks, (out, top_out, high, low) = refs[:-4], refs[-4:]
    rows_dev = base.shape[0]
    width = upper_in.shape[0]
    assemble(step, ring_blocks(blocks), rows_dev, width, high, low)
    offset = local_rows(pivots, step, rows_dev)
    later = local_rows(pivots, step + 1, rows_dev)
    upper = split(upper_in[...])
    displaced = split(displaced_in[...])
    for start in range(0, rows_dev, width):
        part = slice(start, start + width)
        rows = iota((width, width), 0) + start
        value = base[part, :] + (pick(one_hot(rows, offset), displaced) + dot((high[part, :], low[part, :]), upper))
        if start == step * width:
            value = jnp.where(lax.axis_index("prow") == 0, upper_in[...], value)
        if start == (step + 1) * width:
            top_out[...] = value
        hit = jnp.where(later == rows, F32(1), F32(0))
        out[part, :] = jnp.where(jnp.sum(hit, axis=1, keepdims=True) == 0, value, F32(0))


def finish(bits, step, base, pivots, inverse, owner, top, high, low, sent, *refs):
    received, (out, result, sems) = refs[:-3], refs[-3:]
    rows_dev = base.shape[0]
    picked = picked_rows(bits, sent, received, owner)
    width = picked.shape[0]
    upper_full = dot(split(inverse[step]), split(picked))
    offset = local_rows(pivots, step, rows_dev)
    upper = split(upper_full)
    displaced = split(displaced_rows(bits, received, top[...]))
    copies = []
    for start in range(0, rows_dev, width):
        part = slice(start, start + width)
        rows = iota((width, width), 0) + start
        value = base[part, :] + (pick(one_hot(rows, offset), displaced) + dot((high[part, :], low[part, :]), upper))
        if start == step * width:
            value = jnp.where(lax.axis_index("prow") == 0, upper_full, value)
        result[part, :] = value
        copies.append(
            pltpu.make_async_copy(result.at[pl.ds(start, width), :], out.at[pl.ds(start, width), :], sems.at[len(copies)])
        )
        copies[-1].start()
    for copy in copies:
        copy.wait()


def stack(one, other, out):
    rows = one.shape[0]
    out[:rows, :] = one[...]
    out[rows:, :] = other[...]


def pack(own, near, before, out):
    rows = own.shape[0]
    out[:rows, :] = own[...]
    out[rows : 2 * rows, :] = near[...]
    out[2 * rows :, :] = own[: out.shape[0] - 2 * rows, :]


def ring_order(chips):
    return [0] + list(range(1, chips // 2 + 1)) + list(range(chips - 1, chips // 2, -1))


def tail_of(rows):
    return TAIL if rows > TAIL else 0


def tails(far, *refs):
    pairs, out = refs[:-1], refs[-1]
    rows = far.shape[0]
    out[:rows, :] = far[...]
    for hop, pair in enumerate(pairs):
        start, tail = rows + hop * tail_of(rows), tail_of(rows)
        if tail:
            out[start : start + tail, :] = pair[2 * rows - tail : 2 * rows, :]


def release(panel, before, out):
    out[...] = panel[: out.shape[0], :]


def shift(block, distance, count):
    return lax.ppermute(block, "pcol", [(i, (i + 2 * distance) % count) for i in range(count)])


def across(block, count):
    return lax.ppermute(block, "pcol", [(i, i ^ 1) for i in range(count)])


def forwarded(block, down, count):
    chips = count // 2
    own = [block]
    for distance in ring_order(chips)[1:]:
        if distance <= chips // 2:
            own.append(shift(own[-1], 1, count))
        else:
            own.append(shift(down if distance == chips - 1 else own[-1], -1, count))
    return own


def passed(pair, count):
    onward = [(i, (i + (2 if i % 2 == 0 else -2)) % count) for i in range(count)]
    pairs = [pair]
    for _ in range(count // 4 - 1):
        pairs.append(lax.ppermute(pairs[-1], "pcol", onward))
    return pairs[1:]


def per_device(mesh, matrix, l_panels, l_inverse, pivots):
    rows_dev, columns = matrix.shape
    steps, width = pivots.shape
    process_rows, process_columns = mesh.shape["prow"], mesh.shape["pcol"]
    bits = [1 << b for b in range(process_rows.bit_length() - 1)]
    shape = jax.ShapeDtypeStruct
    square = shape((width, columns), F32)
    full = shape((rows_dev, columns), F32)

    def call(kernel, name, operands, outs, specs=None, out_specs=None, scratch=()):
        return pl.pallas_call(
            kernel,
            out_shape=outs,
            in_specs=specs or [VMEM] * len(operands),
            out_specs=out_specs or jax.tree.map(lambda _: VMEM, outs),
            scratch_shapes=scratch,
            compiler_params=GRANT,
            cost_estimate=pl.CostEstimate(COST[name], 0, 0) if name in COST else None,
            name=name,
        )(*operands)

    def exchange(sent, step, before=()):
        received = []
        for stage in range(len(bits)):
            if stage:
                operands = [sent, received[-1], owner[step], *before]
                specs = [VMEM] * 3 + [ANY] * len(before)
                sent = call(functools.partial(merge, bits, stage - 1), "merge", operands, square, specs=specs)
            pairs = []
            for i in range(process_rows):
                for j in range(process_columns):
                    bit = bits[len(bits) - 1 - stage] if j % 2 else bits[stage]
                    pairs.append((i * process_columns + j, (i ^ bit) * process_columns + j))
            received.append(lax.ppermute(sent, ("prow", "pcol"), pairs))
        return sent, received

    chunks = rows_dev // width
    halves = [pltpu.VMEM((rows_dev, l_panels.shape[2]), BF16)] * 2
    block = shape(l_panels.shape[1:], F32)
    matrix, pivots, *own = call(
        load,
        "load",
        [pltpu.with_memory_space_constraint(x, pltpu.HBM) for x in (matrix, pivots, l_panels)],
        [full, shape(pivots.shape, pivots.dtype)] + [block] * steps,
        specs=[HBM] * 3,
        scratch=[pltpu.SemaphoreType.DMA((1 + steps + PARTS,))],
    )
    slots = call(first_slots, "first_slots", [matrix, pivots], square)

    near = across(own[1], process_columns)

    def after(panel, before, rows=block.shape[0]):
        return call(release, "release", [panel, before], shape((rows, block.shape[1]), F32), specs=[VMEM, ANY])

    indices = shape((width, columns), jnp.int32)
    owner = call(functools.partial(holders, rows_dev), "holders", [pivots], [indices] * steps)
    base, ahead, places = call(
        prepare, "prepare", [matrix, pivots], [full, square, shape((width, width), jnp.int32)]
    )
    first = forwarded(own[0], after(own[0], places), process_columns)
    joint = call(stack, "stack", first[:2], shape((2 * block.shape[0], block.shape[1]), F32))
    joint = across(joint, process_columns)
    first += [joint] + [across(piece, process_columns) for piece in first[2:]]
    sent, received = exchange(slots, 0, [joint])
    two = shape((2 * block.shape[0] + SPARE, block.shape[1]), F32)
    pair = call(pack, "pack", [own[1], near, sent], two, specs=[VMEM, VMEM, ANY])
    late = late_blocks(process_columns // 2)
    early = [piece for position, piece in enumerate(first) if position not in late]
    factor = call(functools.partial(collect, late), "collect", [places, *early], [shape((width, width), BF16)] * 2)
    operands = [matrix, pivots, l_inverse, owner[0], ahead, places, sent, *received, *factor, *[first[position] for position in late]]
    upper, displaced, slots = call(functools.partial(solve, bits, 0, late), "solve", operands, [square] * 3)
    far = shift(after(own[1], slots), process_columns // 4, process_columns)
    pairs = passed(pair, process_columns)
    rows = block.shape[0]
    joint = call(tails, "tails", [far, *pairs], shape((rows + tail_of(rows) * len(pairs), block.shape[1]), F32))
    second = [own[1], near, far, across(joint, process_columns)]
    second += pairs + [across(after(piece, own[1], 2 * rows - tail_of(rows)), process_columns) for piece in pairs]
    base, top = call(
        functools.partial(update, 0),
        "update",
        [base, pivots, upper, displaced, *first],
        [full, square],
        scratch=halves,
    )
    sent, received = exchange(slots, 1, [top])
    high, low = call(
        functools.partial(halve, 1, rows_dev, width),
        "halve",
        second,
        [shape((rows_dev, l_panels.shape[2]), BF16)] * 2,
    )
    return call(
        functools.partial(finish, bits, 1),
        "finish",
        [base, pivots, l_inverse, owner[1], top, high, low, sent, *received],
        full,
        out_specs=HBM,
        scratch=[pltpu.VMEM((rows_dev, columns), F32), pltpu.SemaphoreType.DMA((chunks,))],
    )


def solution(mesh):
    placed = (P("prow", "pcol"), P(None, ("prow", "pcol"), None), P(), P())
    return jax.shard_map(
        functools.partial(per_device, mesh), mesh=mesh, in_specs=placed, out_specs=P("prow", "pcol"), check_vma=False
    )
```

```python
import functools

import jax
import jax.numpy as jnp
from jax import lax
from jax.experimental import pallas as pl
from jax.experimental.pallas import tpu as pltpu
from jax.sharding import PartitionSpec as P

VMEM = pl.BlockSpec(memory_space=pltpu.VMEM)
ANY = pl.BlockSpec(memory_space=pl.ANY)
HBM = pl.BlockSpec(memory_space=pltpu.HBM)
GRANT = pltpu.CompilerParams(vmem_limit_bytes=40 * 1024 * 1024)
F32 = jnp.float32
BF16 = jnp.bfloat16
NOWHERE = -(1 << 24)
COST = {"holders": 3 * 10**9, "update": 5 * 10**9, "down_piece": 15 * 10**8}
PARTS = 4


def product(left, right):
    return jnp.dot(left, right, preferred_element_type=F32)


def split(values):
    high = values.astype(BF16)
    low = (values - high.astype(F32)).astype(BF16)
    return high, low


def dot(left, right):
    return product(left[0], right[0]) + (product(left[0], right[1]) + product(left[1], right[0]))


def pick(chosen, right):
    return product(chosen, right[0]) + product(chosen, right[1])


def one_hot(left, right):
    return jnp.where(left == right, F32(1), F32(0)).astype(BF16)


def iota(shape, dimension):
    return lax.broadcasted_iota(jnp.int32, shape, dimension)


def column_of(row):
    n = row.shape[1]
    spread = jnp.where(iota((n, n), 0) == iota((n, n), 1), row.astype(F32), F32(0))
    return jnp.sum(spread, axis=1, keepdims=True).astype(jnp.int32)


def local_rows(pivots, step, rows_dev):
    offset = pivots[step : step + 1, :] - lax.axis_index("prow") * rows_dev
    return jnp.where((offset >= 0) & (offset < rows_dev), offset, NOWHERE)


def slot_rows(pivots, step, rows_dev):
    offset = local_rows(pivots, step, rows_dev)
    width = offset.shape[1]
    top = jnp.where(lax.axis_index("prow") == 0, step * width + iota(offset.shape, 1), NOWHERE)
    return jnp.where(offset >= 0, offset, top)


def load(pivots, panels, chosen, *refs):
    blocks, sems = refs[:-1], refs[-1]
    sources = [panels.at[step] for step in range(len(blocks))] + [pivots]
    copies = [pltpu.make_async_copy(*pair, sems.at[i]) for i, pair in enumerate(zip(sources, [*blocks, chosen]))]
    for copy in copies:
        copy.start()
    for copy in copies:
        copy.wait()


def first_slots(pivots, matrix, out, held, sems):
    chunks, rows_dev = sems.shape[0], held.shape[0]
    rows = rows_dev // chunks
    parts = [pl.ds(part * rows, rows) for part in range(chunks)]
    copies = [pltpu.make_async_copy(matrix.at[part, :], held.at[part, :], sems.at[i]) for i, part in enumerate(parts)]
    for copy in copies:
        copy.start()
    place = column_of(slot_rows(pivots, 0, rows_dev))
    total = None
    for part, copy in enumerate(copies):
        copy.wait()
        gather = one_hot(place, iota((place.shape[0], rows), 1) + part * rows)
        term = pick(gather, split(held[part * rows : (part + 1) * rows, :]))
        total = term if total is None else total + term
    out[...] = total


def holders(rows_dev, pivots, *owners):
    for step, owner in enumerate(owners):
        owner[...] = jnp.broadcast_to(column_of(pivots[step : step + 1, :]) // rows_dev, owner.shape)


def prepare(matrix, pivots, base, ahead, places):
    rows_dev = matrix.shape[0]
    offset = local_rows(pivots, 0, rows_dev)
    width = offset.shape[1]
    place = column_of(slot_rows(pivots, 1, rows_dev))
    places[...] = jnp.broadcast_to(place, places.shape)
    total = None
    for start in range(0, rows_dev, width):
        hit = jnp.where(offset == iota((width, width), 0) + start, F32(1), F32(0))
        keep = jnp.sum(hit, axis=1, keepdims=True) == 0
        kept = jnp.where(keep, matrix[start : start + width, :], F32(0))
        base[start : start + width, :] = kept
        gather = one_hot(place, iota((width, width), 1) + start)
        term = pick(gather, split(kept))
        total = term if total is None else total + term
    ahead[...] = total


def stage_bits(bits, stage):
    odd = lax.rem(lax.axis_index("pcol"), 2) == 1
    bit = jnp.where(odd, bits[len(bits) - 1 - stage], bits[stage])
    known = jnp.where(odd, sum(bits[len(bits) - stage :]) if stage else 0, sum(bits[:stage]))
    return bit, known


def merge(bits, stage, sent, received, owner, *refs):
    row = lax.axis_index("prow")
    bit, known = stage_bits(bits, stage)
    partner = row ^ bit
    who = owner[...]
    keep = ~known
    theirs = ((who ^ partner) & keep) == 0
    neither = ((who ^ row) & ~(known | bit)) != 0
    take = theirs | (neither & ((partner & keep) == 0))
    refs[-1][...] = jnp.where(take, received[...], sent[...])


def picked_rows(bits, sent, received, owner):
    bit, _ = stage_bits(bits, len(bits) - 1)
    mine = ((owner[...] ^ lax.axis_index("prow")) & bit) == 0
    return jnp.where(mine, sent[...], received[-1][...])


def displaced_rows(bits, received, top):
    row = lax.axis_index("prow")
    value = received[-1][...]
    for stage in reversed(range(len(bits) - 1)):
        bit, known = stage_bits(bits, stage)
        value = jnp.where((row & ~(known | bit)) == 0, received[stage][...], value)
    return jnp.where(row == 0, top, value)


def place_of(chip, core, chips, rows):
    return pl.multiple_of((lax.rem(chip + chips, chips) * 2 + core) * rows, rows)


def rows_of(ref, index, count=1):
    rows = ref.shape[0] // count
    return ref.at[pl.ds(index * rows, rows), :]


def ring_blocks(refs):
    chips = (len(refs) + 1) // 2
    mine, joint, rest = refs[:chips], refs[chips], refs[chips + 1 :]
    rows = next(ref for ref in [*mine, *rest] if ref is not None).shape[0]
    others = [joint if joint is None else rows_of(joint, half, 2) for half in range(2)] + list(rest)
    chip, core = lax.axis_index("pcol") // 2, lax.rem(lax.axis_index("pcol"), 2)
    found = []
    for order, distance in enumerate(ring_order(chips)):
        found.append((mine[order], place_of(chip - distance, core, chips, rows)))
        found.append((others[order], place_of(chip - distance, 1 - core, chips, rows)))
    return found


def panel_rows(places, blocks):
    high = low = None
    for block, start in blocks:
        rows = block.shape[0]
        gather = one_hot(places[:, :rows] - start, iota((places.shape[0], rows), 1))
        block_high, block_low = split(block[...])
        term_high, term_low = product(gather, block_high), product(gather, block_low)
        high = term_high if high is None else high + term_high
        low = term_low if low is None else low + term_low
    return high, low


def late_blocks(chips):
    return [chips + chips // 2 - 1, 2 * chips - 2]


def collect(late, places, *refs):
    blocks, (high, low) = list(refs[:-2]), refs[-2:]
    for position in late:
        blocks.insert(position, None)
    found_high, found_low = panel_rows(places, [pair for pair in ring_blocks(blocks) if pair[0] is not None])
    high[...] = found_high.astype(BF16)
    low[...] = found_low.astype(BF16)


def solve(bits, step, late, matrix, pivots, inverse, owner, ahead, places, sent, *refs):
    refs = list(refs)
    received = [refs.pop(0) for _ in bits]
    high, low, *found, upper_out, displaced_out, slots = refs
    rows_dev = matrix.shape[0]
    picked = picked_rows(bits, sent, received, owner)
    width = picked.shape[0]
    upper = dot(split(inverse[step]), split(picked))
    upper_out[...] = upper
    displaced = displaced_rows(bits, received, matrix[step * width : (step + 1) * width, :])
    displaced_out[...] = displaced
    moved = one_hot(places[...], local_rows(pivots, step, rows_dev))
    blocks = [None] * (rows_dev // found[0].shape[0] - 1)
    for position, block in zip(late, found):
        blocks[position] = block
    rest_high, rest_low = panel_rows(places, [pair for pair in ring_blocks(blocks) if pair[0] is not None])
    factor = ((high[...].astype(F32) + rest_high).astype(BF16), (low[...].astype(F32) + rest_low).astype(BF16))
    slots[...] = ahead[...] + (pick(moved, split(displaced)) - dot(factor, split(upper)))


def assemble(step, blocks, rows_dev, width, high, low):
    limit = (step + 1) * width - lax.axis_index("prow") * rows_dev
    for block, start in blocks:
        rows = block.shape[0]
        below = start + iota(block.shape, 0) >= limit
        block_high, block_low = split(jnp.where(below, -block[...], F32(0)))
        high[pl.ds(start, rows), :] = block_high
        low[pl.ds(start, rows), :] = block_low


def halve(step, rows_dev, width, *refs):
    assemble(step, ring_blocks(refs[:-2]), rows_dev, width, refs[-2], refs[-1])


def update(step, base, pivots, upper_in, displaced_in, *refs):
    blocks, (out, top_out, high, low) = refs[:-4], refs[-4:]
    rows_dev = base.shape[0]
    width = upper_in.shape[0]
    assemble(step, ring_blocks(blocks), rows_dev, width, high, low)
    offset = local_rows(pivots, step, rows_dev)
    later = local_rows(pivots, step + 1, rows_dev)
    upper = split(upper_in[...])
    displaced = split(displaced_in[...])
    for start in range(0, rows_dev, width):
        part = slice(start, start + width)
        rows = iota((width, width), 0) + start
        value = base[part, :] + (pick(one_hot(rows, offset), displaced) + dot((high[part, :], low[part, :]), upper))
        if start == step * width:
            value = jnp.where(lax.axis_index("prow") == 0, upper_in[...], value)
        if start == (step + 1) * width:
            top_out[...] = value
        hit = jnp.where(later == rows, F32(1), F32(0))
        out[part, :] = jnp.where(jnp.sum(hit, axis=1, keepdims=True) == 0, value, F32(0))


def finish(bits, step, base, pivots, inverse, owner, top, high, low, sent, *refs):
    received, (out, result, sems) = refs[:-3], refs[-3:]
    rows_dev = base.shape[0]
    picked = picked_rows(bits, sent, received, owner)
    width = picked.shape[0]
    upper_full = dot(split(inverse[step]), split(picked))
    offset = local_rows(pivots, step, rows_dev)
    upper = split(upper_full)
    displaced = split(displaced_rows(bits, received, top[...]))
    copies = []
    for start in range(0, rows_dev, width):
        part = slice(start, start + width)
        rows = iota((width, width), 0) + start
        value = base[part, :] + (pick(one_hot(rows, offset), displaced) + dot((high[part, :], low[part, :]), upper))
        if start == step * width:
            value = jnp.where(lax.axis_index("prow") == 0, upper_full, value)
        result[part, :] = value
        copies.append(
            pltpu.make_async_copy(result.at[pl.ds(start, width), :], out.at[pl.ds(start, width), :], sems.at[len(copies)])
        )
        copies[-1].start()
    for copy in copies:
        copy.wait()


def stack(one, other, out):
    rows = one.shape[0]
    out[:rows, :] = one[...]
    out[rows:, :] = other[...]


def ring_order(chips):
    return [0] + list(range(1, chips // 2 + 1)) + list(range(chips - 1, chips // 2, -1))


def release(panel, before, out):
    out[...] = panel[...]


def shift(block, distance, count):
    return lax.ppermute(block, "pcol", [(i, (i + 2 * distance) % count) for i in range(count)])


def across(block, count):
    return lax.ppermute(block, "pcol", [(i, i ^ 1) for i in range(count)])


def forwarded(block, up, down, count, held=lambda piece: piece):
    chips = count // 2
    own = [block]
    for distance in ring_order(chips)[1:]:
        if distance <= chips // 2:
            own.append(held(shift(up, 1, count)) if distance == 1 else shift(own[-1], 1, count))
        else:
            own.append(shift(down if distance == chips - 1 else own[-1], -1, count))
    return own


def per_device(mesh, matrix, l_panels, l_inverse, pivots):
    rows_dev, columns = matrix.shape
    steps, width = pivots.shape
    process_rows, process_columns = mesh.shape["prow"], mesh.shape["pcol"]
    bits = [1 << b for b in range(process_rows.bit_length() - 1)]
    shape = jax.ShapeDtypeStruct
    square = shape((width, columns), F32)
    full = shape((rows_dev, columns), F32)

    def call(kernel, name, operands, outs, specs=None, out_specs=None, scratch=()):
        return pl.pallas_call(
            kernel,
            out_shape=outs,
            in_specs=specs or [VMEM] * len(operands),
            out_specs=out_specs or jax.tree.map(lambda _: VMEM, outs),
            scratch_shapes=scratch,
            compiler_params=GRANT,
            cost_estimate=pl.CostEstimate(COST[name], 0, 0) if name in COST else None,
            name=name,
        )(*operands)

    def exchange(sent, step, before=()):
        received = []
        for stage in range(len(bits)):
            if stage:
                operands = [sent, received[-1], owner[step], *before]
                specs = [VMEM] * 3 + [ANY] * len(before)
                sent = call(functools.partial(merge, bits, stage - 1), "merge", operands, square, specs=specs)
            pairs = []
            for i in range(process_rows):
                for j in range(process_columns):
                    bit = bits[len(bits) - 1 - stage] if j % 2 else bits[stage]
                    pairs.append((i * process_columns + j, (i ^ bit) * process_columns + j))
            received.append(lax.ppermute(sent, ("prow", "pcol"), pairs))
        return sent, received

    chunks = rows_dev // width
    halves = [pltpu.VMEM((rows_dev, l_panels.shape[2]), BF16)] * 2
    block = shape(l_panels.shape[1:], F32)
    chosen, *own = call(
        load,
        "load",
        [pltpu.with_memory_space_constraint(x, pltpu.HBM) for x in (pivots, l_panels)],
        [shape(pivots.shape, pivots.dtype)] + [block] * steps,
        specs=[HBM] * 2,
        scratch=[pltpu.SemaphoreType.DMA((1 + steps,))],
    )
    pivots = chosen
    slots, matrix = call(
        first_slots,
        "first_slots",
        [pivots, pltpu.with_memory_space_constraint(matrix, pltpu.HBM)],
        [square, full],
        specs=[VMEM, HBM],
        scratch=[pltpu.SemaphoreType.DMA((PARTS,))],
    )

    def after(panel, before, name):
        return call(release, name, [panel, before], block, specs=[VMEM, ANY])

    def with_other_core(mine, name):
        joint = call(stack, name, mine[:2], shape((2 * block.shape[0], block.shape[1]), F32))
        return mine + [across(piece, process_columns) for piece in [joint, *mine[2:]]]

    indices = shape((width, columns), jnp.int32)
    owner = call(functools.partial(holders, rows_dev), "holders", [pivots], [indices] * steps)
    base, ahead, places = call(
        prepare, "prepare", [matrix, pivots], [full, square, shape((width, width), jnp.int32)]
    )
    first = with_other_core(forwarded(own[0], own[0], after(own[0], places, "down_first"), process_columns), "stack_first")
    sent, received = exchange(slots, 0, [first[process_columns // 2]])
    late = late_blocks(process_columns // 2)
    early = [piece for position, piece in enumerate(first) if position not in late]
    factor = call(functools.partial(collect, late), "collect", [places, *early], [shape((width, width), BF16)] * 2)
    operands = [matrix, pivots, l_inverse, owner[0], ahead, places, sent, *received, *factor, *[first[position] for position in late]]
    upper, displaced, slots = call(functools.partial(solve, bits, 0, late), "solve", operands, [square] * 3)
    base, top = call(
        functools.partial(update, 0),
        "update",
        [base, pivots, upper, displaced, *first],
        [full, square],
        scratch=halves,
    )
    up = after(own[1], sent, "up_second")
    down = after(own[1], slots, "down_second")
    second = forwarded(own[1], up, down, process_columns, lambda piece: after(piece, top, "onward"))
    second[-1] = after(second[-1], slots, "down_piece")
    second = with_other_core(second, "stack_second")
    sent, received = exchange(slots, 1, [top])
    high, low = call(
        functools.partial(halve, 1, rows_dev, width),
        "halve",
        second,
        [shape((rows_dev, l_panels.shape[2]), BF16)] * 2,
    )
    return call(
        functools.partial(finish, bits, 1),
        "finish",
        [base, pivots, l_inverse, owner[1], top, high, low, sent, *received],
        full,
        out_specs=HBM,
        scratch=[pltpu.VMEM((rows_dev, columns), F32), pltpu.SemaphoreType.DMA((chunks,))],
    )


def solution(mesh):
    placed = (P("prow", "pcol"), P(None, ("prow", "pcol"), None), P(), P())
    return jax.shard_map(
        functools.partial(per_device, mesh), mesh=mesh, in_specs=placed, out_specs=P("prow", "pcol"), check_vma=False
    )
```

```python
import functools

import jax
import jax.numpy as jnp
from jax import lax
from jax.experimental import pallas as pl
from jax.experimental.pallas import tpu as pltpu
from jax.sharding import PartitionSpec as P

VMEM = pl.BlockSpec(memory_space=pltpu.VMEM)
ANY = pl.BlockSpec(memory_space=pl.ANY)
HBM = pl.BlockSpec(memory_space=pltpu.HBM)
GRANT = pltpu.CompilerParams(vmem_limit_bytes=40 * 1024 * 1024)
F32 = jnp.float32
BF16 = jnp.bfloat16
NOWHERE = -(1 << 24)
COST = {
    "holders": 3000 * 10**6,
    "update": 5000 * 10**6,
    "pair_piece": 2000 * 10**6,
    "stack": 5000 * 10**6,
    "far_piece": 3000 * 10**6,
    "far_block": 5000 * 10**6,
    "prepare": 600 * 10**6,
    "down_block": 300 * 10**6,
    "collect": 1 * 10**6,
}
PARTS = 4


def product(left, right):
    return jnp.dot(left, right, preferred_element_type=F32)


def split(values):
    high = values.astype(BF16)
    low = (values - high.astype(F32)).astype(BF16)
    return high, low


def dot(left, right):
    return product(left[0], right[0]) + (product(left[0], right[1]) + product(left[1], right[0]))


def pick(chosen, right):
    return product(chosen, right[0]) + product(chosen, right[1])


def one_hot(left, right):
    return jnp.where(left == right, F32(1), F32(0)).astype(BF16)


def iota(shape, dimension):
    return lax.broadcasted_iota(jnp.int32, shape, dimension)


def column_of(row):
    n = row.shape[1]
    spread = jnp.where(iota((n, n), 0) == iota((n, n), 1), row.astype(F32), F32(0))
    return jnp.sum(spread, axis=1, keepdims=True).astype(jnp.int32)


def local_rows(pivots, step, rows_dev):
    offset = pivots[step : step + 1, :] - lax.axis_index("prow") * rows_dev
    return jnp.where((offset >= 0) & (offset < rows_dev), offset, NOWHERE)


def slot_rows(pivots, step, rows_dev):
    offset = local_rows(pivots, step, rows_dev)
    width = offset.shape[1]
    top = jnp.where(lax.axis_index("prow") == 0, step * width + iota(offset.shape, 1), NOWHERE)
    return jnp.where(offset >= 0, offset, top)


def load(matrix, pivots, panels, held, chosen, *refs):
    blocks, sems = refs[:-1], refs[-1]
    rows = held.shape[0] // PARTS
    parts = [pl.ds(part * rows, rows) for part in range(PARTS)]
    sources = [panels.at[step] for step in range(len(blocks))] + [pivots] + [matrix.at[part, :] for part in parts]
    targets = [*blocks, chosen] + [held.at[part, :] for part in parts]
    copies = [pltpu.make_async_copy(*pair, sems.at[i]) for i, pair in enumerate(zip(sources, targets))]
    for copy in copies:
        copy.start()
    for copy in copies:
        copy.wait()


def first_slots(matrix, pivots, out):
    rows_dev = matrix.shape[0]
    place = column_of(slot_rows(pivots, 0, rows_dev))
    width = place.shape[0]
    total = None
    for start in range(0, rows_dev, width):
        gather = one_hot(place, iota((width, width), 1) + start)
        term = pick(gather, split(matrix[start : start + width, :]))
        total = term if total is None else total + term
    out[...] = total


def holders(rows_dev, pivots, *owners):
    for step, owner in enumerate(owners):
        owner[...] = jnp.broadcast_to(column_of(pivots[step : step + 1, :]) // rows_dev, owner.shape)


def prepare(matrix, pivots, base, ahead, places):
    rows_dev = matrix.shape[0]
    offset = local_rows(pivots, 0, rows_dev)
    width = offset.shape[1]
    place = column_of(slot_rows(pivots, 1, rows_dev))
    places[...] = jnp.broadcast_to(place, places.shape)
    total = None
    for start in range(0, rows_dev, width):
        hit = jnp.where(offset == iota((width, width), 0) + start, F32(1), F32(0))
        keep = jnp.sum(hit, axis=1, keepdims=True) == 0
        kept = jnp.where(keep, matrix[start : start + width, :], F32(0))
        base[start : start + width, :] = kept
        gather = one_hot(place, iota((width, width), 1) + start)
        term = pick(gather, split(kept))
        total = term if total is None else total + term
    ahead[...] = total


def stage_bits(bits, stage):
    odd = lax.rem(lax.axis_index("pcol"), 2) == 1
    bit = jnp.where(odd, bits[len(bits) - 1 - stage], bits[stage])
    known = jnp.where(odd, sum(bits[len(bits) - stage :]) if stage else 0, sum(bits[:stage]))
    return bit, known


def merge(bits, stage, sent, received, owner, *refs):
    row = lax.axis_index("prow")
    bit, known = stage_bits(bits, stage)
    partner = row ^ bit
    who = owner[...]
    keep = ~known
    theirs = ((who ^ partner) & keep) == 0
    neither = ((who ^ row) & ~(known | bit)) != 0
    take = theirs | (neither & ((partner & keep) == 0))
    refs[-1][...] = jnp.where(take, received[...], sent[...])


def picked_rows(bits, sent, received, owner):
    bit, _ = stage_bits(bits, len(bits) - 1)
    mine = ((owner[...] ^ lax.axis_index("prow")) & bit) == 0
    return jnp.where(mine, sent[...], received[-1][...])


def displaced_rows(bits, received, top):
    row = lax.axis_index("prow")
    value = received[-1][...]
    for stage in reversed(range(len(bits) - 1)):
        bit, known = stage_bits(bits, stage)
        value = jnp.where((row & ~(known | bit)) == 0, received[stage][...], value)
    return jnp.where(row == 0, top, value)


def place_of(chip, core, chips, rows):
    return pl.multiple_of((lax.rem(chip + chips, chips) * 2 + core) * rows, rows)


def rows_of(ref, index, count=1):
    rows = ref.shape[0] // count
    return ref.at[pl.ds(index * rows, rows), :]


def ring_blocks(refs):
    chips = (len(refs) + 1) // 2
    mine, joint, rest = refs[:chips], refs[chips], refs[chips + 1 :]
    rows = next(ref for ref in [*mine, *rest] if ref is not None).shape[0]
    others = [joint if joint is None else rows_of(joint, half, 2) for half in range(2)] + list(rest)
    chip, core = lax.axis_index("pcol") // 2, lax.rem(lax.axis_index("pcol"), 2)
    found = []
    for order, distance in enumerate(ring_order(chips)):
        found.append((mine[order], place_of(chip - distance, core, chips, rows)))
        found.append((others[order], place_of(chip - distance, 1 - core, chips, rows)))
    return found


def pair_blocks(refs):
    own, near, far, far_back, *rest = refs
    rows = own.shape[0]
    hops = len(rest) // 2
    chips = 2 * hops + 2
    chip, core = lax.axis_index("pcol") // 2, lax.rem(lax.axis_index("pcol"), 2)
    opposite = chip + chips // 2
    found = [
        (own, place_of(chip, core, chips, rows)),
        (near, place_of(chip, 1 - core, chips, rows)),
        (far, place_of(opposite, core, chips, rows)),
        (far_back, place_of(opposite, 1 - core, chips, rows)),
    ]
    for hop in range(hops):
        along = (hop + 1) * (1 - 2 * core)
        for half in range(2):
            owner = core if half == 0 else 1 - core
            found.append((rows_of(rest[hop], half, 2), place_of(chip - along, owner, chips, rows)))
            found.append((rows_of(rest[hops + hop], half, 2), place_of(chip + along, 1 - owner, chips, rows)))
    return found


def panel_rows(places, blocks):
    high = low = None
    for block, start in blocks:
        rows = block.shape[0]
        gather = one_hot(places[:, :rows] - start, iota((places.shape[0], rows), 1))
        block_high, block_low = split(block[...])
        term_high, term_low = product(gather, block_high), product(gather, block_low)
        high = term_high if high is None else high + term_high
        low = term_low if low is None else low + term_low
    return high, low


def late_blocks(chips):
    return [chips + chips // 2 - 1, 2 * chips - 2]


def collect(late, places, *refs):
    blocks, (high, low) = list(refs[:-2]), refs[-2:]
    for position in late:
        blocks.insert(position, None)
    found_high, found_low = panel_rows(places, [pair for pair in ring_blocks(blocks) if pair[0] is not None])
    high[...] = found_high.astype(BF16)
    low[...] = found_low.astype(BF16)


def solve(bits, step, late, matrix, pivots, inverse, owner, ahead, places, sent, *refs):
    refs = list(refs)
    received = [refs.pop(0) for _ in bits]
    high, low, *found, upper_out, displaced_out, slots = refs
    rows_dev = matrix.shape[0]
    picked = picked_rows(bits, sent, received, owner)
    width = picked.shape[0]
    upper = dot(split(inverse[step]), split(picked))
    upper_out[...] = upper
    displaced = displaced_rows(bits, received, matrix[step * width : (step + 1) * width, :])
    displaced_out[...] = displaced
    moved = one_hot(places[...], local_rows(pivots, step, rows_dev))
    blocks = [None] * (rows_dev // found[0].shape[0] - 1)
    for position, block in zip(late, found):
        blocks[position] = block
    rest_high, rest_low = panel_rows(places, [pair for pair in ring_blocks(blocks) if pair[0] is not None])
    factor = ((high[...].astype(F32) + rest_high).astype(BF16), (low[...].astype(F32) + rest_low).astype(BF16))
    slots[...] = ahead[...] + (pick(moved, split(displaced)) - dot(factor, split(upper)))


def assemble(step, blocks, rows_dev, width, high, low):
    limit = (step + 1) * width - lax.axis_index("prow") * rows_dev
    for block, start in blocks:
        rows = block.shape[0]
        below = start + iota(block.shape, 0) >= limit
        block_high, block_low = split(jnp.where(below, -block[...], F32(0)))
        high[pl.ds(start, rows), :] = block_high
        low[pl.ds(start, rows), :] = block_low


def halve(step, rows_dev, width, *refs):
    assemble(step, pair_blocks(refs[:-2]), rows_dev, width, refs[-2], refs[-1])


def update(step, base, pivots, upper_in, displaced_in, *refs):
    blocks, (out, top_out, high, low) = refs[:-4], refs[-4:]
    rows_dev = base.shape[0]
    width = upper_in.shape[0]
    assemble(step, ring_blocks(blocks), rows_dev, width, high, low)
    offset = local_rows(pivots, step, rows_dev)
    later = local_rows(pivots, step + 1, rows_dev)
    upper = split(upper_in[...])
    displaced = split(displaced_in[...])
    for start in range(0, rows_dev, width):
        part = slice(start, start + width)
        rows = iota((width, width), 0) + start
        value = base[part, :] + (pick(one_hot(rows, offset), displaced) + dot((high[part, :], low[part, :]), upper))
        if start == step * width:
            value = jnp.where(lax.axis_index("prow") == 0, upper_in[...], value)
        if start == (step + 1) * width:
            top_out[...] = value
        hit = jnp.where(later == rows, F32(1), F32(0))
        out[part, :] = jnp.where(jnp.sum(hit, axis=1, keepdims=True) == 0, value, F32(0))


def finish(bits, step, base, pivots, inverse, owner, top, high, low, sent, *refs):
    received, (out, result, sems) = refs[:-3], refs[-3:]
    rows_dev = base.shape[0]
    picked = picked_rows(bits, sent, received, owner)
    width = picked.shape[0]
    upper_full = dot(split(inverse[step]), split(picked))
    offset = local_rows(pivots, step, rows_dev)
    upper = split(upper_full)
    displaced = split(displaced_rows(bits, received, top[...]))
    copies = []
    part = rows_dev // sems.shape[0]
    for start in range(0, rows_dev, part):
        rows = slice(start, start + part)
        gather = one_hot(iota((part, width), 0) + start, offset)
        value = base[rows, :] + (pick(gather, displaced) + dot((high[rows, :], low[rows, :]), upper))
        inside = start - step * width
        if 0 <= inside < width:
            value = jnp.where(lax.axis_index("prow") == 0, upper_full[inside : inside + part, :], value)
        result[rows, :] = value
        place = pl.ds(start, part)
        copies.append(pltpu.make_async_copy(result.at[place, :], out.at[place, :], sems.at[len(copies)]))
        copies[-1].start()
    for copy in copies:
        copy.wait()


def stack(one, other, out):
    rows = one.shape[0]
    out[:rows, :] = one[...]
    out[rows:, :] = other[...]


def pack(own, near, before, out):
    rows = own.shape[0]
    out[:rows, :] = own[...]
    out[rows:, :] = near[...]


def ring_order(chips):
    return [0] + list(range(1, chips // 2 + 1)) + list(range(chips - 1, chips // 2, -1))


def release(panel, before, out):
    out[...] = panel[...]


def shift(block, distance, count):
    return lax.ppermute(block, "pcol", [(i, (i + 2 * distance) % count) for i in range(count)])


def across(block, count):
    return lax.ppermute(block, "pcol", [(i, i ^ 1) for i in range(count)])


def forwarded(block, down, count):
    chips = count // 2
    own = [block]
    for distance in ring_order(chips)[1:]:
        if distance <= chips // 2:
            own.append(shift(own[-1], 1, count))
        else:
            own.append(shift(down if distance == chips - 1 else own[-1], -1, count))
    return own


def passed(pair, count):
    onward = [(i, (i + (2 if i % 2 == 0 else -2)) % count) for i in range(count)]
    pairs = [pair]
    for _ in range(count // 4 - 1):
        pairs.append(lax.ppermute(pairs[-1], "pcol", onward))
    return pairs[1:]


def per_device(mesh, matrix, l_panels, l_inverse, pivots):
    rows_dev, columns = matrix.shape
    steps, width = pivots.shape
    process_rows, process_columns = mesh.shape["prow"], mesh.shape["pcol"]
    bits = [1 << b for b in range(process_rows.bit_length() - 1)]
    shape = jax.ShapeDtypeStruct
    square = shape((width, columns), F32)
    full = shape((rows_dev, columns), F32)

    def call(kernel, name, operands, outs, specs=None, out_specs=None, scratch=()):
        return pl.pallas_call(
            kernel,
            out_shape=outs,
            in_specs=specs or [VMEM] * len(operands),
            out_specs=out_specs or jax.tree.map(lambda _: VMEM, outs),
            scratch_shapes=scratch,
            compiler_params=GRANT,
            cost_estimate=pl.CostEstimate(COST[name], 0, 0) if name in COST else None,
            name=name,
        )(*operands)

    def exchange(sent, step, before=()):
        received = []
        for stage in range(len(bits)):
            if stage:
                operands = [sent, received[-1], owner[step], *before]
                specs = [VMEM] * 3 + [ANY] * len(before)
                sent = call(functools.partial(merge, bits, stage - 1), "merge", operands, square, specs=specs)
            pairs = []
            for i in range(process_rows):
                for j in range(process_columns):
                    bit = bits[len(bits) - 1 - stage] if j % 2 else bits[stage]
                    pairs.append((i * process_columns + j, (i ^ bit) * process_columns + j))
            received.append(lax.ppermute(sent, ("prow", "pcol"), pairs))
        return sent, received

    chunks = rows_dev // width
    halves = [pltpu.VMEM((rows_dev, l_panels.shape[2]), BF16)] * 2
    block = shape(l_panels.shape[1:], F32)
    matrix, pivots, *own = call(
        load,
        "load",
        [pltpu.with_memory_space_constraint(x, pltpu.HBM) for x in (matrix, pivots, l_panels)],
        [full, shape(pivots.shape, pivots.dtype)] + [block] * steps,
        specs=[HBM] * 3,
        scratch=[pltpu.SemaphoreType.DMA((1 + steps + PARTS,))],
    )
    slots = call(first_slots, "first_slots", [matrix, pivots], square)

    near = across(own[1], process_columns)

    def after(panel, before, name="release"):
        return call(release, name, [panel, before], shape(panel.shape, F32), specs=[VMEM, ANY])

    indices = shape((width, columns), jnp.int32)
    owner = call(functools.partial(holders, rows_dev), "holders", [pivots], [indices] * steps)
    base, ahead, places = call(
        prepare, "prepare", [matrix, pivots], [full, square, shape((width, width), jnp.int32)]
    )
    first = forwarded(own[0], after(own[0], places, "down_block"), process_columns)
    joint = call(stack, "stack", first[:2], shape((2 * block.shape[0], block.shape[1]), F32))
    joint = across(joint, process_columns)
    first += [joint] + [across(piece, process_columns) for piece in first[2:]]
    sent, received = exchange(slots, 0, [joint])
    two = shape((2 * block.shape[0], block.shape[1]), F32)
    pair = call(pack, "pack", [own[1], near, sent], two, specs=[VMEM, VMEM, ANY])
    late = late_blocks(process_columns // 2)
    early = [piece for position, piece in enumerate(first) if position not in late]
    factor = call(functools.partial(collect, late), "collect", [places, *early], [shape((width, width), BF16)] * 2)
    operands = [matrix, pivots, l_inverse, owner[0], ahead, places, sent, *received, *factor, *[first[position] for position in late]]
    upper, displaced, slots = call(functools.partial(solve, bits, 0, late), "solve", operands, [square] * 3)
    far = shift(after(own[1], slots, "far_block"), process_columns // 4, process_columns)
    pairs = passed(pair, process_columns)
    base, top = call(
        functools.partial(update, 0),
        "update",
        [base, pivots, upper, displaced, *first],
        [full, square],
        scratch=halves,
    )
    sent, received = exchange(slots, 1, [top])
    second = [own[1], near, far, across(after(far, own[1], "far_piece"), process_columns)]
    second += pairs + [across(after(piece, sent, "pair_piece"), process_columns) for piece in pairs]
    high, low = call(
        functools.partial(halve, 1, rows_dev, width),
        "halve",
        second,
        [shape((rows_dev, l_panels.shape[2]), BF16)] * 2,
    )
    return call(
        functools.partial(finish, bits, 1),
        "finish",
        [base, pivots, l_inverse, owner[1], top, high, low, sent, *received],
        full,
        out_specs=HBM,
        scratch=[pltpu.VMEM((rows_dev, columns), F32), pltpu.SemaphoreType.DMA((2 * chunks,))],
    )


def solution(mesh):
    placed = (P("prow", "pcol"), P(None, ("prow", "pcol"), None), P(), P())
    return jax.shard_map(
        functools.partial(per_device, mesh), mesh=mesh, in_specs=placed, out_specs=P("prow", "pcol"), check_vma=False
    )
```

```python
import functools

import jax
import jax.numpy as jnp
from jax import lax
from jax.experimental import pallas as pl
from jax.experimental.pallas import tpu as pltpu
from jax.sharding import PartitionSpec as P

VMEM = pl.BlockSpec(memory_space=pltpu.VMEM)
ANY = pl.BlockSpec(memory_space=pl.ANY)
HBM = pl.BlockSpec(memory_space=pltpu.HBM)
GRANT = pltpu.CompilerParams(vmem_limit_bytes=40 * 1024 * 1024)
F32 = jnp.float32
BF16 = jnp.bfloat16
NOWHERE = -(1 << 24)
COST = {
    "prepare": 1000 * 10**6,
    "down_block": 300 * 10**6,
    "far_block": 5000 * 10**6,
    "collect": 1500 * 10**6,
    "holders": 3000 * 10**6,
    "update": 5000 * 10**6,
    "pair_piece": 1000 * 10**6,
    "stack": 8000 * 10**6,
    "far_piece": 3000 * 10**6,
}
PARTS = 4


def product(left, right):
    return jnp.dot(left, right, preferred_element_type=F32)


def split(values):
    high = values.astype(BF16)
    low = (values - high.astype(F32)).astype(BF16)
    return high, low


def dot(left, right):
    return product(left[0], right[0]) + (product(left[0], right[1]) + product(left[1], right[0]))


def pick(chosen, right):
    return product(chosen, right[0]) + product(chosen, right[1])


def one_hot(left, right):
    return jnp.where(left == right, F32(1), F32(0)).astype(BF16)


def iota(shape, dimension):
    return lax.broadcasted_iota(jnp.int32, shape, dimension)


def column_of(row):
    n = row.shape[1]
    spread = jnp.where(iota((n, n), 0) == iota((n, n), 1), row.astype(F32), F32(0))
    return jnp.sum(spread, axis=1, keepdims=True).astype(jnp.int32)


def local_rows(pivots, step, rows_dev):
    offset = pivots[step : step + 1, :] - lax.axis_index("prow") * rows_dev
    return jnp.where((offset >= 0) & (offset < rows_dev), offset, NOWHERE)


def slot_rows(pivots, step, rows_dev):
    offset = local_rows(pivots, step, rows_dev)
    width = offset.shape[1]
    top = jnp.where(lax.axis_index("prow") == 0, step * width + iota(offset.shape, 1), NOWHERE)
    return jnp.where(offset >= 0, offset, top)


def load(matrix, pivots, panels, held, chosen, *refs):
    blocks, sems = refs[:-1], refs[-1]
    rows = held.shape[0] // PARTS
    parts = [pl.ds(part * rows, rows) for part in range(PARTS)]
    sources = [panels.at[step] for step in range(len(blocks))] + [pivots] + [matrix.at[part, :] for part in parts]
    targets = [*blocks, chosen] + [held.at[part, :] for part in parts]
    copies = [pltpu.make_async_copy(*pair, sems.at[i]) for i, pair in enumerate(zip(sources, targets))]
    for copy in copies:
        copy.start()
    for copy in copies:
        copy.wait()


def first_slots(matrix, pivots, out):
    rows_dev = matrix.shape[0]
    place = column_of(slot_rows(pivots, 0, rows_dev))
    width = place.shape[0]
    total = None
    for start in range(0, rows_dev, width):
        gather = one_hot(place, iota((width, width), 1) + start)
        term = pick(gather, split(matrix[start : start + width, :]))
        total = term if total is None else total + term
    out[...] = total


def holders(rows_dev, pivots, *owners):
    for step, owner in enumerate(owners):
        owner[...] = jnp.broadcast_to(column_of(pivots[step : step + 1, :]) // rows_dev, owner.shape)


def prepare(matrix, pivots, base, ahead, places):
    rows_dev = matrix.shape[0]
    offset = local_rows(pivots, 0, rows_dev)
    width = offset.shape[1]
    place = column_of(slot_rows(pivots, 1, rows_dev))
    places[...] = jnp.broadcast_to(place, places.shape)
    total = None
    for start in range(0, rows_dev, width):
        hit = jnp.where(offset == iota((width, width), 0) + start, F32(1), F32(0))
        keep = jnp.sum(hit, axis=1, keepdims=True) == 0
        kept = jnp.where(keep, matrix[start : start + width, :], F32(0))
        base[start : start + width, :] = kept
        gather = one_hot(place, iota((width, width), 1) + start)
        term = pick(gather, split(kept))
        total = term if total is None else total + term
    ahead[...] = total


def stage_bits(bits, stage):
    odd = lax.rem(lax.axis_index("pcol"), 2) == 1
    bit = jnp.where(odd, bits[len(bits) - 1 - stage], bits[stage])
    known = jnp.where(odd, sum(bits[len(bits) - stage :]) if stage else 0, sum(bits[:stage]))
    return bit, known


def merge(bits, stage, sent, received, owner, *refs):
    row = lax.axis_index("prow")
    bit, known = stage_bits(bits, stage)
    partner = row ^ bit
    who = owner[...]
    keep = ~known
    theirs = ((who ^ partner) & keep) == 0
    neither = ((who ^ row) & ~(known | bit)) != 0
    take = theirs | (neither & ((partner & keep) == 0))
    refs[-1][...] = jnp.where(take, received[...], sent[...])


def picked_rows(bits, sent, received, owner):
    bit, _ = stage_bits(bits, len(bits) - 1)
    mine = ((owner[...] ^ lax.axis_index("prow")) & bit) == 0
    return jnp.where(mine, sent[...], received[-1][...])


def displaced_rows(bits, received, top):
    row = lax.axis_index("prow")
    value = received[-1][...]
    for stage in reversed(range(len(bits) - 1)):
        bit, known = stage_bits(bits, stage)
        value = jnp.where((row & ~(known | bit)) == 0, received[stage][...], value)
    return jnp.where(row == 0, top, value)


def place_of(chip, core, chips, rows):
    return pl.multiple_of((lax.rem(chip + chips, chips) * 2 + core) * rows, rows)


def rows_of(ref, index, count=1):
    rows = ref.shape[0] // count
    return ref.at[pl.ds(index * rows, rows), :]


def ring_blocks(refs):
    chips = (len(refs) + 1) // 2
    mine, joint, rest = refs[:chips], refs[chips], refs[chips + 1 :]
    rows = next(ref for ref in [*mine, *rest] if ref is not None).shape[0]
    others = [joint if joint is None else rows_of(joint, half, 2) for half in range(2)] + list(rest)
    chip, core = lax.axis_index("pcol") // 2, lax.rem(lax.axis_index("pcol"), 2)
    found = []
    for order, distance in enumerate(ring_order(chips)):
        found.append((mine[order], place_of(chip - distance, core, chips, rows)))
        found.append((others[order], place_of(chip - distance, 1 - core, chips, rows)))
    return found


def pair_blocks(refs):
    own, near, far, far_back, *rest = refs
    rows = own.shape[0]
    hops = len(rest) // 2
    chips = 2 * hops + 2
    chip, core = lax.axis_index("pcol") // 2, lax.rem(lax.axis_index("pcol"), 2)
    opposite = chip + chips // 2
    found = [
        (own, place_of(chip, core, chips, rows)),
        (near, place_of(chip, 1 - core, chips, rows)),
        (far, place_of(opposite, core, chips, rows)),
        (far_back, place_of(opposite, 1 - core, chips, rows)),
    ]
    for hop in range(hops):
        along = (hop + 1) * (1 - 2 * core)
        for half in range(2):
            owner = core if half == 0 else 1 - core
            found.append((rows_of(rest[hop], half, 2), place_of(chip - along, owner, chips, rows)))
            found.append((rows_of(rest[hops + hop], half, 2), place_of(chip + along, 1 - owner, chips, rows)))
    return found


def panel_rows(places, blocks):
    high = low = None
    for block, start in blocks:
        rows = block.shape[0]
        gather = one_hot(places[:, :rows] - start, iota((places.shape[0], rows), 1))
        block_high, block_low = split(block[...])
        term_high, term_low = product(gather, block_high), product(gather, block_low)
        high = term_high if high is None else high + term_high
        low = term_low if low is None else low + term_low
    return high, low


def late_blocks(chips):
    return [chips + chips // 2 - 1, 2 * chips - 2]


def collect(late, places, *refs):
    blocks, (high, low) = list(refs[:-2]), refs[-2:]
    for position in late:
        blocks.insert(position, None)
    found_high, found_low = panel_rows(places, [pair for pair in ring_blocks(blocks) if pair[0] is not None])
    high[...] = found_high.astype(BF16)
    low[...] = found_low.astype(BF16)


def solve(bits, step, late, matrix, pivots, inverse, owner, ahead, places, sent, *refs):
    refs = list(refs)
    received = [refs.pop(0) for _ in bits]
    high, low, *found, upper_out, displaced_out, slots = refs
    rows_dev = matrix.shape[0]
    picked = picked_rows(bits, sent, received, owner)
    width = picked.shape[0]
    upper = dot(split(inverse[step]), split(picked))
    upper_out[...] = upper
    displaced = displaced_rows(bits, received, matrix[step * width : (step + 1) * width, :])
    displaced_out[...] = displaced
    moved = one_hot(places[...], local_rows(pivots, step, rows_dev))
    blocks = [None] * (rows_dev // found[0].shape[0] - 1)
    for position, block in zip(late, found):
        blocks[position] = block
    rest_high, rest_low = panel_rows(places, [pair for pair in ring_blocks(blocks) if pair[0] is not None])
    factor = ((high[...].astype(F32) + rest_high).astype(BF16), (low[...].astype(F32) + rest_low).astype(BF16))
    slots[...] = ahead[...] + (pick(moved, split(displaced)) - dot(factor, split(upper)))


def assemble(step, blocks, rows_dev, width, high, low):
    limit = (step + 1) * width - lax.axis_index("prow") * rows_dev
    for block, start in blocks:
        rows = block.shape[0]
        below = start + iota(block.shape, 0) >= limit
        block_high, block_low = split(jnp.where(below, -block[...], F32(0)))
        high[pl.ds(start, rows), :] = block_high
        low[pl.ds(start, rows), :] = block_low


def halve(step, rows_dev, width, *refs):
    assemble(step, pair_blocks(refs[:-2]), rows_dev, width, refs[-2], refs[-1])


def update(step, base, pivots, upper_in, displaced_in, *refs):
    blocks, (out, top_out, high, low) = refs[:-4], refs[-4:]
    rows_dev = base.shape[0]
    width = upper_in.shape[0]
    assemble(step, ring_blocks(blocks), rows_dev, width, high, low)
    offset = local_rows(pivots, step, rows_dev)
    later = local_rows(pivots, step + 1, rows_dev)
    upper = split(upper_in[...])
    displaced = split(displaced_in[...])
    for start in range(0, rows_dev, width):
        part = slice(start, start + width)
        rows = iota((width, width), 0) + start
        value = base[part, :] + (pick(one_hot(rows, offset), displaced) + dot((high[part, :], low[part, :]), upper))
        if start == step * width:
            value = jnp.where(lax.axis_index("prow") == 0, upper_in[...], value)
        if start == (step + 1) * width:
            top_out[...] = value
        hit = jnp.where(later == rows, F32(1), F32(0))
        out[part, :] = jnp.where(jnp.sum(hit, axis=1, keepdims=True) == 0, value, F32(0))


def finish(bits, step, base, pivots, inverse, owner, top, high, low, sent, *refs):
    received, (out, result, sems) = refs[:-3], refs[-3:]
    rows_dev = base.shape[0]
    picked = picked_rows(bits, sent, received, owner)
    width = picked.shape[0]
    upper_full = dot(split(inverse[step]), split(picked))
    offset = local_rows(pivots, step, rows_dev)
    upper = split(upper_full)
    displaced = split(displaced_rows(bits, received, top[...]))
    copies = []
    part = rows_dev // sems.shape[0]
    for start in range(0, rows_dev, part):
        rows = slice(start, start + part)
        gather = one_hot(iota((part, width), 0) + start, offset)
        value = base[rows, :] + (pick(gather, displaced) + dot((high[rows, :], low[rows, :]), upper))
        inside = start - step * width
        if 0 <= inside < width:
            value = jnp.where(lax.axis_index("prow") == 0, upper_full[inside : inside + part, :], value)
        result[rows, :] = value
        place = pl.ds(start, part)
        copies.append(pltpu.make_async_copy(result.at[place, :], out.at[place, :], sems.at[len(copies)]))
        copies[-1].start()
    for copy in copies:
        copy.wait()


def stack(one, other, out):
    rows = one.shape[0]
    out[:rows, :] = one[...]
    out[rows:, :] = other[...]


def pack(own, near, before, out):
    rows = own.shape[0]
    out[:rows, :] = own[...]
    out[rows:, :] = near[...]


def ring_order(chips):
    return [0] + list(range(1, chips // 2 + 1)) + list(range(chips - 1, chips // 2, -1))


def release(panel, before, out):
    out[...] = panel[...]


def shift(block, distance, count):
    return lax.ppermute(block, "pcol", [(i, (i + 2 * distance) % count) for i in range(count)])


def across(block, count):
    return lax.ppermute(block, "pcol", [(i, i ^ 1) for i in range(count)])


def forwarded(block, down, count):
    chips = count // 2
    own = [block]
    for distance in ring_order(chips)[1:]:
        if distance <= chips // 2:
            own.append(shift(own[-1], 1, count))
        else:
            own.append(shift(down if distance == chips - 1 else own[-1], -1, count))
    return own


def passed(pair, count):
    onward = [(i, (i + (2 if i % 2 == 0 else -2)) % count) for i in range(count)]
    pairs = [pair]
    for _ in range(count // 4 - 1):
        pairs.append(lax.ppermute(pairs[-1], "pcol", onward))
    return pairs[1:]


def per_device(mesh, matrix, l_panels, l_inverse, pivots):
    rows_dev, columns = matrix.shape
    steps, width = pivots.shape
    process_rows, process_columns = mesh.shape["prow"], mesh.shape["pcol"]
    bits = [1 << b for b in range(process_rows.bit_length() - 1)]
    shape = jax.ShapeDtypeStruct
    square = shape((width, columns), F32)
    full = shape((rows_dev, columns), F32)

    def call(kernel, name, operands, outs, specs=None, out_specs=None, scratch=()):
        return pl.pallas_call(
            kernel,
            out_shape=outs,
            in_specs=specs or [VMEM] * len(operands),
            out_specs=out_specs or jax.tree.map(lambda _: VMEM, outs),
            scratch_shapes=scratch,
            compiler_params=GRANT,
            cost_estimate=pl.CostEstimate(COST[name], 0, 0) if name in COST else None,
            name=name,
        )(*operands)

    def exchange(sent, step, before=()):
        received = []
        for stage in range(len(bits)):
            if stage:
                operands = [sent, received[-1], owner[step], *before]
                specs = [VMEM] * 3 + [ANY] * len(before)
                sent = call(functools.partial(merge, bits, stage - 1), "merge", operands, square, specs=specs)
            pairs = []
            for i in range(process_rows):
                for j in range(process_columns):
                    bit = bits[len(bits) - 1 - stage] if j % 2 else bits[stage]
                    pairs.append((i * process_columns + j, (i ^ bit) * process_columns + j))
            received.append(lax.ppermute(sent, ("prow", "pcol"), pairs))
        return sent, received

    chunks = rows_dev // width
    halves = [pltpu.VMEM((rows_dev, l_panels.shape[2]), BF16)] * 2
    block = shape(l_panels.shape[1:], F32)
    matrix, pivots, *own = call(
        load,
        "load",
        [pltpu.with_memory_space_constraint(x, pltpu.HBM) for x in (matrix, pivots, l_panels)],
        [full, shape(pivots.shape, pivots.dtype)] + [block] * steps,
        specs=[HBM] * 3,
        scratch=[pltpu.SemaphoreType.DMA((1 + steps + PARTS,))],
    )
    slots = call(first_slots, "first_slots", [matrix, pivots], square)

    near = across(own[1], process_columns)

    def after(panel, before, name="release"):
        return call(release, name, [panel, before], shape(panel.shape, F32), specs=[VMEM, ANY])

    indices = shape((width, columns), jnp.int32)
    owner = call(functools.partial(holders, rows_dev), "holders", [pivots], [indices] * steps)
    base, ahead, places = call(
        prepare, "prepare", [matrix, pivots], [full, square, shape((width, width), jnp.int32)]
    )
    first = forwarded(own[0], after(own[0], places, "down_block"), process_columns)
    joint = call(stack, "stack", first[:2], shape((2 * block.shape[0], block.shape[1]), F32))
    joint = across(joint, process_columns)
    first += [joint] + [across(piece, process_columns) for piece in first[2:]]
    sent, received = exchange(slots, 0, [joint])
    two = shape((2 * block.shape[0], block.shape[1]), F32)
    pair = call(pack, "pack", [own[1], near, sent], two, specs=[VMEM, VMEM, ANY])
    late = late_blocks(process_columns // 2)
    early = [piece for position, piece in enumerate(first) if position not in late]
    factor = call(functools.partial(collect, late), "collect", [places, *early], [shape((width, width), BF16)] * 2)
    operands = [matrix, pivots, l_inverse, owner[0], ahead, places, sent, *received, *factor, *[first[position] for position in late]]
    upper, displaced, slots = call(functools.partial(solve, bits, 0, late), "solve", operands, [square] * 3)
    far = shift(after(own[1], slots, "far_block"), process_columns // 4, process_columns)
    pairs = passed(pair, process_columns)
    base, top = call(
        functools.partial(update, 0),
        "update",
        [base, pivots, upper, displaced, *first],
        [full, square],
        scratch=halves,
    )
    sent, received = exchange(slots, 1, [top])
    second = [own[1], near, far, across(after(far, own[1], "far_piece"), process_columns)]
    second += pairs + [across(after(piece, sent, "pair_piece"), process_columns) for piece in pairs]
    high, low = call(
        functools.partial(halve, 1, rows_dev, width),
        "halve",
        second,
        [shape((rows_dev, l_panels.shape[2]), BF16)] * 2,
    )
    return call(
        functools.partial(finish, bits, 1),
        "finish",
        [base, pivots, l_inverse, owner[1], top, high, low, sent, *received],
        full,
        out_specs=HBM,
        scratch=[pltpu.VMEM((rows_dev, columns), F32), pltpu.SemaphoreType.DMA((chunks,))],
    )


def solution(mesh):
    placed = (P("prow", "pcol"), P(None, ("prow", "pcol"), None), P(), P())
    return jax.shard_map(
        functools.partial(per_device, mesh), mesh=mesh, in_specs=placed, out_specs=P("prow", "pcol"), check_vma=False
    )
```

```python
import functools

import jax
import jax.numpy as jnp
from jax import lax
from jax.experimental import pallas as pl
from jax.experimental.pallas import tpu as pltpu
from jax.sharding import PartitionSpec as P

VMEM = pl.BlockSpec(memory_space=pltpu.VMEM)
ANY = pl.BlockSpec(memory_space=pl.ANY)
HBM = pl.BlockSpec(memory_space=pltpu.HBM)
GRANT = pltpu.CompilerParams(vmem_limit_bytes=40 * 1024 * 1024)
F32 = jnp.float32
BF16 = jnp.bfloat16
NOWHERE = -(1 << 24)
COST = {
    "prepare": 1000 * 10**6,
    "down_block": 300 * 10**6,
    "far_block": 5000 * 10**6,
    "collect": 1500 * 10**6,
    "holders": 3000 * 10**6,
    "update": 5000 * 10**6,
    "pair_piece": 1000 * 10**6,
    "stack": 8000 * 10**6,
    "far_piece": 3000 * 10**6,
}
PARTS = 4


def product(left, right):
    return jnp.dot(left, right, preferred_element_type=F32)


def split(values):
    high = values.astype(BF16)
    low = (values - high.astype(F32)).astype(BF16)
    return high, low


def dot(left, right):
    return product(left[0], right[0]) + (product(left[0], right[1]) + product(left[1], right[0]))


def pick(chosen, right):
    return product(chosen, right[0]) + product(chosen, right[1])


def one_hot(left, right):
    return jnp.where(left == right, F32(1), F32(0)).astype(BF16)


def iota(shape, dimension):
    return lax.broadcasted_iota(jnp.int32, shape, dimension)


def column_of(row):
    n = row.shape[1]
    spread = jnp.where(iota((n, n), 0) == iota((n, n), 1), row.astype(F32), F32(0))
    return jnp.sum(spread, axis=1, keepdims=True).astype(jnp.int32)


def local_rows(pivots, step, rows_dev):
    offset = pivots[step : step + 1, :] - lax.axis_index("prow") * rows_dev
    return jnp.where((offset >= 0) & (offset < rows_dev), offset, NOWHERE)


def slot_rows(pivots, step, rows_dev):
    offset = local_rows(pivots, step, rows_dev)
    width = offset.shape[1]
    top = jnp.where(lax.axis_index("prow") == 0, step * width + iota(offset.shape, 1), NOWHERE)
    return jnp.where(offset >= 0, offset, top)


def load(matrix, pivots, panels, held, chosen, *refs):
    blocks, sems = refs[:-1], refs[-1]
    rows = held.shape[0] // PARTS
    parts = [pl.ds(part * rows, rows) for part in range(PARTS)]
    sources = [panels.at[step] for step in range(len(blocks))] + [pivots] + [matrix.at[part, :] for part in parts]
    targets = [*blocks, chosen] + [held.at[part, :] for part in parts]
    copies = [pltpu.make_async_copy(*pair, sems.at[i]) for i, pair in enumerate(zip(sources, targets))]
    for copy in copies:
        copy.start()
    for copy in copies:
        copy.wait()


def first_slots(matrix, pivots, out):
    rows_dev = matrix.shape[0]
    place = column_of(slot_rows(pivots, 0, rows_dev))
    width = place.shape[0]
    total = None
    for start in range(0, rows_dev, width):
        gather = one_hot(place, iota((width, width), 1) + start)
        term = pick(gather, split(matrix[start : start + width, :]))
        total = term if total is None else total + term
    out[...] = total


def holders(rows_dev, pivots, *owners):
    for step, owner in enumerate(owners):
        owner[...] = jnp.broadcast_to(column_of(pivots[step : step + 1, :]) // rows_dev, owner.shape)


def prepare(matrix, pivots, base, ahead, places):
    rows_dev = matrix.shape[0]
    offset = local_rows(pivots, 0, rows_dev)
    width = offset.shape[1]
    place = column_of(slot_rows(pivots, 1, rows_dev))
    places[...] = jnp.broadcast_to(place, places.shape)
    total = None
    for start in range(0, rows_dev, width):
        hit = jnp.where(offset == iota((width, width), 0) + start, F32(1), F32(0))
        keep = jnp.sum(hit, axis=1, keepdims=True) == 0
        kept = jnp.where(keep, matrix[start : start + width, :], F32(0))
        base[start : start + width, :] = kept
        gather = one_hot(place, iota((width, width), 1) + start)
        term = pick(gather, split(kept))
        total = term if total is None else total + term
    ahead[...] = total


def stage_bits(bits, stage):
    odd = lax.rem(lax.axis_index("pcol"), 2) == 1
    bit = jnp.where(odd, bits[len(bits) - 1 - stage], bits[stage])
    known = jnp.where(odd, sum(bits[len(bits) - stage :]) if stage else 0, sum(bits[:stage]))
    return bit, known


def merge(bits, stage, sent, received, owner, *refs):
    row = lax.axis_index("prow")
    bit, known = stage_bits(bits, stage)
    partner = row ^ bit
    who = owner[...]
    keep = ~known
    theirs = ((who ^ partner) & keep) == 0
    neither = ((who ^ row) & ~(known | bit)) != 0
    take = theirs | (neither & ((partner & keep) == 0))
    refs[-1][...] = jnp.where(take, received[...], sent[...])


def picked_rows(bits, sent, received, owner):
    bit, _ = stage_bits(bits, len(bits) - 1)
    mine = ((owner[...] ^ lax.axis_index("prow")) & bit) == 0
    return jnp.where(mine, sent[...], received[-1][...])


def displaced_rows(bits, received, top):
    row = lax.axis_index("prow")
    value = received[-1][...]
    for stage in reversed(range(len(bits) - 1)):
        bit, known = stage_bits(bits, stage)
        value = jnp.where((row & ~(known | bit)) == 0, received[stage][...], value)
    return jnp.where(row == 0, top, value)


def place_of(chip, core, chips, rows):
    return pl.multiple_of((lax.rem(chip + chips, chips) * 2 + core) * rows, rows)


def rows_of(ref, index, count=1):
    rows = ref.shape[0] // count
    return ref.at[pl.ds(index * rows, rows), :]


def ring_blocks(refs):
    chips = (len(refs) + 1) // 2
    mine, joint, rest = refs[:chips], refs[chips], refs[chips + 1 :]
    rows = next(ref for ref in [*mine, *rest] if ref is not None).shape[0]
    others = [joint if joint is None else rows_of(joint, half, 2) for half in range(2)] + list(rest)
    chip, core = lax.axis_index("pcol") // 2, lax.rem(lax.axis_index("pcol"), 2)
    found = []
    for order, distance in enumerate(ring_order(chips)):
        found.append((mine[order], place_of(chip - distance, core, chips, rows)))
        found.append((others[order], place_of(chip - distance, 1 - core, chips, rows)))
    return found


def pair_blocks(refs):
    own, near, far, far_back, *rest = refs
    rows = own.shape[0]
    hops = len(rest) // 2
    chips = 2 * hops + 2
    chip, core = lax.axis_index("pcol") // 2, lax.rem(lax.axis_index("pcol"), 2)
    opposite = chip + chips // 2
    found = [
        (own, place_of(chip, core, chips, rows)),
        (near, place_of(chip, 1 - core, chips, rows)),
        (far, place_of(opposite, core, chips, rows)),
        (far_back, place_of(opposite, 1 - core, chips, rows)),
    ]
    for hop in range(hops):
        along = (hop + 1) * (1 - 2 * core)
        for half in range(2):
            owner = core if half == 0 else 1 - core
            found.append((rows_of(rest[hop], half, 2), place_of(chip - along, owner, chips, rows)))
            found.append((rows_of(rest[hops + hop], half, 2), place_of(chip + along, 1 - owner, chips, rows)))
    return found


def panel_rows(places, blocks):
    high = low = None
    for block, start in blocks:
        rows = block.shape[0]
        gather = one_hot(places[:, :rows] - start, iota((places.shape[0], rows), 1))
        block_high, block_low = split(block[...])
        term_high, term_low = product(gather, block_high), product(gather, block_low)
        high = term_high if high is None else high + term_high
        low = term_low if low is None else low + term_low
    return high, low


def late_blocks(chips):
    return [chips + chips // 2 - 1, 2 * chips - 2]


def collect(late, places, *refs):
    blocks, (high, low) = list(refs[:-2]), refs[-2:]
    for position in late:
        blocks.insert(position, None)
    found_high, found_low = panel_rows(places, [pair for pair in ring_blocks(blocks) if pair[0] is not None])
    high[...] = found_high.astype(BF16)
    low[...] = found_low.astype(BF16)


def solve(bits, step, late, matrix, pivots, inverse, owner, ahead, places, sent, *refs):
    refs = list(refs)
    received = [refs.pop(0) for _ in bits]
    high, low, *found, upper_out, displaced_out, slots = refs
    rows_dev = matrix.shape[0]
    picked = picked_rows(bits, sent, received, owner)
    width = picked.shape[0]
    upper = dot(split(inverse[step]), split(picked))
    upper_out[...] = upper
    displaced = displaced_rows(bits, received, matrix[step * width : (step + 1) * width, :])
    displaced_out[...] = displaced
    moved = one_hot(places[...], local_rows(pivots, step, rows_dev))
    blocks = [None] * (rows_dev // found[0].shape[0] - 1)
    for position, block in zip(late, found):
        blocks[position] = block
    rest_high, rest_low = panel_rows(places, [pair for pair in ring_blocks(blocks) if pair[0] is not None])
    factor = ((high[...].astype(F32) + rest_high).astype(BF16), (low[...].astype(F32) + rest_low).astype(BF16))
    slots[...] = ahead[...] + (pick(moved, split(displaced)) - dot(factor, split(upper)))


def assemble(step, blocks, rows_dev, width, high, low):
    limit = (step + 1) * width - lax.axis_index("prow") * rows_dev
    for block, start in blocks:
        if block is None:
            continue
        rows = block.shape[0]
        below = start + iota(block.shape, 0) >= limit
        block_high, block_low = split(jnp.where(below, -block[...], F32(0)))
        high[pl.ds(start, rows), :] = block_high
        low[pl.ds(start, rows), :] = block_low


def halve(step, rows_dev, width, own, near, *refs):
    blocks = pair_blocks([own, near, None, None, *refs[:-2]])
    assemble(step, blocks, rows_dev, width, refs[-2], refs[-1])


def update(step, base, pivots, upper_in, displaced_in, *refs):
    blocks, (out, top_out, high, low) = refs[:-4], refs[-4:]
    rows_dev = base.shape[0]
    width = upper_in.shape[0]
    assemble(step, ring_blocks(blocks), rows_dev, width, high, low)
    offset = local_rows(pivots, step, rows_dev)
    later = local_rows(pivots, step + 1, rows_dev)
    upper = split(upper_in[...])
    displaced = split(displaced_in[...])
    for start in range(0, rows_dev, width):
        part = slice(start, start + width)
        rows = iota((width, width), 0) + start
        value = base[part, :] + (pick(one_hot(rows, offset), displaced) + dot((high[part, :], low[part, :]), upper))
        if start == step * width:
            value = jnp.where(lax.axis_index("prow") == 0, upper_in[...], value)
        if start == (step + 1) * width:
            top_out[...] = value
        hit = jnp.where(later == rows, F32(1), F32(0))
        out[part, :] = jnp.where(jnp.sum(hit, axis=1, keepdims=True) == 0, value, F32(0))


def opposite_chip(chips):
    return lax.rem(lax.axis_index("pcol") // 2 + chips // 2, chips)


def with_top(step, start, value, upper):
    part, width = value.shape[0], upper.shape[0]
    inside = start - step * width
    chosen = (lax.axis_index("prow") == 0) & (inside >= 0) & (inside < width)
    place = pl.multiple_of(jnp.clip(inside, 0, width - part), part)
    return jnp.where(chosen, upper[pl.ds(place, part), :], value)


def finish(bits, step, part, base, pivots, inverse, owner, top, high, low, sent, *refs):
    received, (out, upper_out, partial, result, sems) = refs[:-5], refs[-5:]
    rows_dev = base.shape[0]
    chips = rows_dev // part
    picked = picked_rows(bits, sent, received, owner)
    width = picked.shape[0]
    upper_out[...] = dot(split(inverse[step]), split(picked))
    offset = local_rows(pivots, step, rows_dev)
    upper = split(upper_out[...])
    displaced = split(displaced_rows(bits, received, top[...]))
    copies = []
    for turn in range(1, chips + 1):
        start = pl.multiple_of(lax.rem(opposite_chip(chips) + turn, chips) * part, part)
        rows = pl.ds(start, part)
        value = base[rows, :] + pick(one_hot(iota((part, width), 0) + start, offset), displaced)
        if turn == chips:
            partial[...] = value
            break
        value = value + dot((high[rows, :], low[rows, :]), upper)
        result[rows, :] = with_top(step, start, value, upper_out)
        copies.append(pltpu.make_async_copy(result.at[rows, :], out.at[rows, :], sems.at[turn - 1]))
        copies[-1].start()
    for copy in copies:
        copy.wait()


def far_rows(step, chips, far, far_back, upper, partial, before, out, panel, result, sem):
    rows, (part, width) = far.shape[0], partial.shape
    core = lax.rem(lax.axis_index("pcol"), 2)
    panel[pl.ds(pl.multiple_of(core * rows, rows), rows), :] = far[...]
    panel[pl.ds(pl.multiple_of((1 - core) * rows, rows), rows), :] = far_back[...]
    start = pl.multiple_of(opposite_chip(chips) * part, part)
    limit = (step + 1) * upper.shape[0] - lax.axis_index("prow") * chips * part
    factor = jnp.where(start + iota(panel.shape, 0) >= limit, -panel[...], F32(0))
    value = partial[...] + dot(split(factor), split(upper[...]))
    result[...] = with_top(step, start, value, upper)
    copy = pltpu.make_async_copy(result, out.at[pl.ds(start, part), :], sem)
    copy.start()
    copy.wait()


def stack(one, other, out):
    rows = one.shape[0]
    out[:rows, :] = one[...]
    out[rows:, :] = other[...]


def pack(own, near, before, out):
    rows = own.shape[0]
    out[:rows, :] = own[...]
    out[rows:, :] = near[...]


def ring_order(chips):
    return [0] + list(range(1, chips // 2 + 1)) + list(range(chips - 1, chips // 2, -1))


def release(panel, before, out):
    out[...] = panel[...]


def shift(block, distance, count):
    return lax.ppermute(block, "pcol", [(i, (i + 2 * distance) % count) for i in range(count)])


def across(block, count):
    return lax.ppermute(block, "pcol", [(i, i ^ 1) for i in range(count)])


def forwarded(block, down, count):
    chips = count // 2
    own = [block]
    for distance in ring_order(chips)[1:]:
        if distance <= chips // 2:
            own.append(shift(own[-1], 1, count))
        else:
            own.append(shift(down if distance == chips - 1 else own[-1], -1, count))
    return own


def passed(pair, count):
    onward = [(i, (i + (2 if i % 2 == 0 else -2)) % count) for i in range(count)]
    pairs = [pair]
    for _ in range(count // 4 - 1):
        pairs.append(lax.ppermute(pairs[-1], "pcol", onward))
    return pairs[1:]


def per_device(mesh, matrix, l_panels, l_inverse, pivots):
    rows_dev, columns = matrix.shape
    steps, width = pivots.shape
    process_rows, process_columns = mesh.shape["prow"], mesh.shape["pcol"]
    bits = [1 << b for b in range(process_rows.bit_length() - 1)]
    shape = jax.ShapeDtypeStruct
    square = shape((width, columns), F32)
    full = shape((rows_dev, columns), F32)

    def call(kernel, name, operands, outs, specs=None, out_specs=None, scratch=(), aliases=None):
        return pl.pallas_call(
            kernel,
            out_shape=outs,
            in_specs=specs or [VMEM] * len(operands),
            out_specs=out_specs or jax.tree.map(lambda _: VMEM, outs),
            scratch_shapes=scratch,
            input_output_aliases=aliases or {},
            compiler_params=GRANT,
            cost_estimate=pl.CostEstimate(COST[name], 0, 0) if name in COST else None,
            name=name,
        )(*operands)

    def exchange(sent, step, before=()):
        received = []
        for stage in range(len(bits)):
            if stage:
                operands = [sent, received[-1], owner[step], *before]
                specs = [VMEM] * 3 + [ANY] * len(before)
                sent = call(functools.partial(merge, bits, stage - 1), "merge", operands, square, specs=specs)
            pairs = []
            for i in range(process_rows):
                for j in range(process_columns):
                    bit = bits[len(bits) - 1 - stage] if j % 2 else bits[stage]
                    pairs.append((i * process_columns + j, (i ^ bit) * process_columns + j))
            received.append(lax.ppermute(sent, ("prow", "pcol"), pairs))
        return sent, received

    chunks = rows_dev // width
    halves = [pltpu.VMEM((rows_dev, l_panels.shape[2]), BF16)] * 2
    block = shape(l_panels.shape[1:], F32)
    matrix, pivots, *own = call(
        load,
        "load",
        [pltpu.with_memory_space_constraint(x, pltpu.HBM) for x in (matrix, pivots, l_panels)],
        [full, shape(pivots.shape, pivots.dtype)] + [block] * steps,
        specs=[HBM] * 3,
        scratch=[pltpu.SemaphoreType.DMA((1 + steps + PARTS,))],
    )
    slots = call(first_slots, "first_slots", [matrix, pivots], square)

    near = across(own[1], process_columns)

    def after(panel, before, name="release"):
        return call(release, name, [panel, before], shape(panel.shape, F32), specs=[VMEM, ANY])

    indices = shape((width, columns), jnp.int32)
    owner = call(functools.partial(holders, rows_dev), "holders", [pivots], [indices] * steps)
    base, ahead, places = call(
        prepare, "prepare", [matrix, pivots], [full, square, shape((width, width), jnp.int32)]
    )
    first = forwarded(own[0], after(own[0], places, "down_block"), process_columns)
    joint = call(stack, "stack", first[:2], shape((2 * block.shape[0], block.shape[1]), F32))
    joint = across(joint, process_columns)
    first += [joint] + [across(piece, process_columns) for piece in first[2:]]
    sent, received = exchange(slots, 0, [joint])
    two = shape((2 * block.shape[0], block.shape[1]), F32)
    pair = call(pack, "pack", [own[1], near, sent], two, specs=[VMEM, VMEM, ANY])
    late = late_blocks(process_columns // 2)
    early = [piece for position, piece in enumerate(first) if position not in late]
    factor = call(functools.partial(collect, late), "collect", [places, *early], [shape((width, width), BF16)] * 2)
    operands = [matrix, pivots, l_inverse, owner[0], ahead, places, sent, *received, *factor, *[first[position] for position in late]]
    upper, displaced, slots = call(functools.partial(solve, bits, 0, late), "solve", operands, [square] * 3)
    far = shift(after(own[1], slots, "far_block"), process_columns // 4, process_columns)
    pairs = passed(pair, process_columns)
    base, top = call(
        functools.partial(update, 0),
        "update",
        [base, pivots, upper, displaced, *first],
        [full, square],
        scratch=halves,
    )
    sent, received = exchange(slots, 1, [top])
    second = [own[1], near, far, across(after(far, own[1], "far_piece"), process_columns)]
    second += pairs + [across(after(piece, sent, "pair_piece"), process_columns) for piece in pairs]
    part, depth = 2 * block.shape[0], block.shape[1]
    high, low = call(
        functools.partial(halve, 1, rows_dev, width),
        "halve",
        second[:2] + second[4:],
        [shape((rows_dev, depth), BF16)] * 2,
    )
    out, upper, partial = call(
        functools.partial(finish, bits, 1, part),
        "finish",
        [base, pivots, l_inverse, owner[1], top, high, low, sent, *received],
        [full, square, shape((part, columns), F32)],
        out_specs=[HBM, VMEM, VMEM],
        scratch=[pltpu.VMEM((rows_dev, columns), F32), pltpu.SemaphoreType.DMA((rows_dev // part - 1,))],
    )
    return call(
        functools.partial(far_rows, 1, rows_dev // part),
        "far_rows",
        [*second[2:4], upper, partial, out],
        full,
        specs=[VMEM] * 4 + [HBM],
        out_specs=HBM,
        scratch=[pltpu.VMEM((part, depth), F32), pltpu.VMEM((part, columns), F32), pltpu.SemaphoreType.DMA],
        aliases={4: 0},
    )


def solution(mesh):
    placed = (P("prow", "pcol"), P(None, ("prow", "pcol"), None), P(), P())
    return jax.shard_map(
        functools.partial(per_device, mesh), mesh=mesh, in_specs=placed, out_specs=P("prow", "pcol"), check_vma=False
    )
```

```python
import functools

import jax
import jax.numpy as jnp
from jax import lax
from jax.experimental import pallas as pl
from jax.experimental.pallas import tpu as pltpu
from jax.sharding import PartitionSpec as P

VMEM = pl.BlockSpec(memory_space=pltpu.VMEM)
ANY = pl.BlockSpec(memory_space=pl.ANY)
HBM = pl.BlockSpec(memory_space=pltpu.HBM)
GRANT = pltpu.CompilerParams(vmem_limit_bytes=40 * 1024 * 1024)
F32 = jnp.float32
BF16 = jnp.bfloat16
NOWHERE = -(1 << 24)
COST = {
    "prepare": 1000 * 10**6,
    "down_block": 300 * 10**6,
    "far_block": 5000 * 10**6,
    "collect": 1500 * 10**6,
    "holders": 3000 * 10**6,
    "update": 5000 * 10**6,
    "pair_piece": 1000 * 10**6,
    "stack": 8000 * 10**6,
    "far_piece": 3000 * 10**6,
}
PARTS = 4


def product(left, right):
    return jnp.dot(left, right, preferred_element_type=F32)


def split(values):
    high = values.astype(BF16)
    low = (values - high.astype(F32)).astype(BF16)
    return high, low


def dot(left, right):
    return product(left[0], right[0]) + (product(left[0], right[1]) + product(left[1], right[0]))


def pick(chosen, right):
    return product(chosen, right[0]) + product(chosen, right[1])


def one_hot(left, right):
    return jnp.where(left == right, F32(1), F32(0)).astype(BF16)


def iota(shape, dimension):
    return lax.broadcasted_iota(jnp.int32, shape, dimension)


def column_of(row):
    n = row.shape[1]
    spread = jnp.where(iota((n, n), 0) == iota((n, n), 1), row.astype(F32), F32(0))
    return jnp.sum(spread, axis=1, keepdims=True).astype(jnp.int32)


def local_rows(pivots, step, rows_dev):
    offset = pivots[step : step + 1, :] - lax.axis_index("prow") * rows_dev
    return jnp.where((offset >= 0) & (offset < rows_dev), offset, NOWHERE)


def slot_rows(pivots, step, rows_dev):
    offset = local_rows(pivots, step, rows_dev)
    width = offset.shape[1]
    top = jnp.where(lax.axis_index("prow") == 0, step * width + iota(offset.shape, 1), NOWHERE)
    return jnp.where(offset >= 0, offset, top)


def load(matrix, pivots, panels, held, chosen, *refs):
    blocks, sems = refs[:-1], refs[-1]
    rows = held.shape[0] // PARTS
    parts = [pl.ds(part * rows, rows) for part in range(PARTS)]
    sources = [panels.at[step] for step in range(len(blocks))] + [pivots] + [matrix.at[part, :] for part in parts]
    targets = [*blocks, chosen] + [held.at[part, :] for part in parts]
    copies = [pltpu.make_async_copy(*pair, sems.at[i]) for i, pair in enumerate(zip(sources, targets))]
    for copy in copies:
        copy.start()
    for copy in copies:
        copy.wait()


def first_slots(matrix, pivots, out):
    rows_dev = matrix.shape[0]
    place = column_of(slot_rows(pivots, 0, rows_dev))
    width = place.shape[0]
    total = None
    for start in range(0, rows_dev, width):
        gather = one_hot(place, iota((width, width), 1) + start)
        term = pick(gather, split(matrix[start : start + width, :]))
        total = term if total is None else total + term
    out[...] = total


def holders(rows_dev, pivots, *owners):
    for step, owner in enumerate(owners):
        owner[...] = jnp.broadcast_to(column_of(pivots[step : step + 1, :]) // rows_dev, owner.shape)


def prepare(matrix, pivots, base, ahead, places):
    rows_dev = matrix.shape[0]
    offset = local_rows(pivots, 0, rows_dev)
    width = offset.shape[1]
    place = column_of(slot_rows(pivots, 1, rows_dev))
    places[...] = jnp.broadcast_to(place, places.shape)
    total = None
    for start in range(0, rows_dev, width):
        hit = jnp.where(offset == iota((width, width), 0) + start, F32(1), F32(0))
        keep = jnp.sum(hit, axis=1, keepdims=True) == 0
        kept = jnp.where(keep, matrix[start : start + width, :], F32(0))
        base[start : start + width, :] = kept
        gather = one_hot(place, iota((width, width), 1) + start)
        term = pick(gather, split(kept))
        total = term if total is None else total + term
    ahead[...] = total


def stage_bits(bits, stage):
    odd = lax.rem(lax.axis_index("pcol"), 2) == 1
    bit = jnp.where(odd, bits[len(bits) - 1 - stage], bits[stage])
    known = jnp.where(odd, sum(bits[len(bits) - stage :]) if stage else 0, sum(bits[:stage]))
    return bit, known


def merge(bits, stage, sent, received, owner, *refs):
    row = lax.axis_index("prow")
    bit, known = stage_bits(bits, stage)
    partner = row ^ bit
    who = owner[...]
    keep = ~known
    theirs = ((who ^ partner) & keep) == 0
    neither = ((who ^ row) & ~(known | bit)) != 0
    take = theirs | (neither & ((partner & keep) == 0))
    refs[-1][...] = jnp.where(take, received[...], sent[...])


def picked_rows(bits, sent, received, owner):
    bit, _ = stage_bits(bits, len(bits) - 1)
    mine = ((owner[...] ^ lax.axis_index("prow")) & bit) == 0
    return jnp.where(mine, sent[...], received[-1][...])


def displaced_rows(bits, received, top):
    row = lax.axis_index("prow")
    value = received[-1][...]
    for stage in reversed(range(len(bits) - 1)):
        bit, known = stage_bits(bits, stage)
        value = jnp.where((row & ~(known | bit)) == 0, received[stage][...], value)
    return jnp.where(row == 0, top, value)


def place_of(chip, core, chips, rows):
    return pl.multiple_of((lax.rem(chip + chips, chips) * 2 + core) * rows, rows)


def rows_of(ref, index, count=1):
    rows = ref.shape[0] // count
    return ref.at[pl.ds(index * rows, rows), :]


def ring_blocks(refs):
    chips = (len(refs) + 1) // 2
    mine, joint, rest = refs[:chips], refs[chips], refs[chips + 1 :]
    rows = next(ref for ref in [*mine, *rest] if ref is not None).shape[0]
    others = [joint if joint is None else rows_of(joint, half, 2) for half in range(2)] + list(rest)
    chip, core = lax.axis_index("pcol") // 2, lax.rem(lax.axis_index("pcol"), 2)
    found = []
    for order, distance in enumerate(ring_order(chips)):
        found.append((mine[order], place_of(chip - distance, core, chips, rows)))
        found.append((others[order], place_of(chip - distance, 1 - core, chips, rows)))
    return found


def pair_blocks(refs):
    own, near, far, far_back, *rest = refs
    rows = own.shape[0]
    hops = len(rest) // 2
    chips = 2 * hops + 2
    chip, core = lax.axis_index("pcol") // 2, lax.rem(lax.axis_index("pcol"), 2)
    opposite = chip + chips // 2
    found = [
        (own, place_of(chip, core, chips, rows)),
        (near, place_of(chip, 1 - core, chips, rows)),
        (far, place_of(opposite, core, chips, rows)),
        (far_back, place_of(opposite, 1 - core, chips, rows)),
    ]
    for hop in range(hops):
        along = (hop + 1) * (1 - 2 * core)
        for half in range(2):
            owner = core if half == 0 else 1 - core
            found.append((rows_of(rest[hop], half, 2), place_of(chip - along, owner, chips, rows)))
            found.append((rows_of(rest[hops + hop], half, 2), place_of(chip + along, 1 - owner, chips, rows)))
    return found


def panel_rows(places, blocks):
    high = low = None
    for block, start in blocks:
        rows = block.shape[0]
        gather = one_hot(places[:, :rows] - start, iota((places.shape[0], rows), 1))
        block_high, block_low = split(block[...])
        term_high, term_low = product(gather, block_high), product(gather, block_low)
        high = term_high if high is None else high + term_high
        low = term_low if low is None else low + term_low
    return high, low


def late_blocks(chips):
    return [chips + chips // 2 - 1, 2 * chips - 2]


def collect(late, places, *refs):
    blocks, (high, low) = list(refs[:-2]), refs[-2:]
    for position in late:
        blocks.insert(position, None)
    found_high, found_low = panel_rows(places, [pair for pair in ring_blocks(blocks) if pair[0] is not None])
    high[...] = found_high.astype(BF16)
    low[...] = found_low.astype(BF16)


def solve(bits, step, late, matrix, pivots, inverse, owner, ahead, places, sent, *refs):
    refs = list(refs)
    received = [refs.pop(0) for _ in bits]
    high, low, *found, upper_out, displaced_out, slots = refs
    rows_dev = matrix.shape[0]
    picked = picked_rows(bits, sent, received, owner)
    width = picked.shape[0]
    upper = dot(split(inverse[step]), split(picked))
    upper_out[...] = upper
    displaced = displaced_rows(bits, received, matrix[step * width : (step + 1) * width, :])
    displaced_out[...] = displaced
    moved = one_hot(places[...], local_rows(pivots, step, rows_dev))
    blocks = [None] * (rows_dev // found[0].shape[0] - 1)
    for position, block in zip(late, found):
        blocks[position] = block
    rest_high, rest_low = panel_rows(places, [pair for pair in ring_blocks(blocks) if pair[0] is not None])
    factor = ((high[...].astype(F32) + rest_high).astype(BF16), (low[...].astype(F32) + rest_low).astype(BF16))
    slots[...] = ahead[...] + (pick(moved, split(displaced)) - dot(factor, split(upper)))


def assemble(step, blocks, rows_dev, width, high, low):
    limit = (step + 1) * width - lax.axis_index("prow") * rows_dev
    for block, start in blocks:
        if block is None:
            continue
        rows = block.shape[0]
        below = start + iota(block.shape, 0) >= limit
        block_high, block_low = split(jnp.where(below, -block[...], F32(0)))
        high[pl.ds(start, rows), :] = block_high
        low[pl.ds(start, rows), :] = block_low


def halve(step, rows_dev, width, own, near, *refs):
    blocks = pair_blocks([own, near, None, None, *refs[:-2]])
    assemble(step, blocks, rows_dev, width, refs[-2], refs[-1])


def update(step, base, pivots, upper_in, displaced_in, *refs):
    blocks, (out, top_out, high, low) = refs[:-4], refs[-4:]
    rows_dev = base.shape[0]
    width = upper_in.shape[0]
    assemble(step, ring_blocks(blocks), rows_dev, width, high, low)
    offset = local_rows(pivots, step, rows_dev)
    later = local_rows(pivots, step + 1, rows_dev)
    upper = split(upper_in[...])
    displaced = split(displaced_in[...])
    for start in range(0, rows_dev, width):
        part = slice(start, start + width)
        rows = iota((width, width), 0) + start
        value = base[part, :] + (pick(one_hot(rows, offset), displaced) + dot((high[part, :], low[part, :]), upper))
        if start == step * width:
            value = jnp.where(lax.axis_index("prow") == 0, upper_in[...], value)
        if start == (step + 1) * width:
            top_out[...] = value
        hit = jnp.where(later == rows, F32(1), F32(0))
        out[part, :] = jnp.where(jnp.sum(hit, axis=1, keepdims=True) == 0, value, F32(0))


def opposite_chip(chips):
    return lax.rem(lax.axis_index("pcol") // 2 + chips // 2, chips)


def with_top(step, start, value, upper):
    part, width = value.shape[0], upper.shape[0]
    inside = start - step * width
    chosen = (lax.axis_index("prow") == 0) & (inside >= 0) & (inside < width)
    place = pl.multiple_of(jnp.clip(inside, 0, width - part), part)
    return jnp.where(chosen, upper[pl.ds(place, part), :], value)


def finish(bits, step, base, pivots, inverse, owner, top, high, low, far, far_back, sent, *refs):
    received, (out, panel, upper_ref, result, sems) = refs[:-5], refs[-5:]
    rows_dev, chips = base.shape[0], sems.shape[0]
    part = rows_dev // chips
    picked = picked_rows(bits, sent, received, owner)
    width = picked.shape[0]
    upper_ref[...] = dot(split(inverse[step]), split(picked))
    offset = local_rows(pivots, step, rows_dev)
    upper = split(upper_ref[...])
    displaced = split(displaced_rows(bits, received, top[...]))
    rows = far.shape[0]
    core = lax.rem(lax.axis_index("pcol"), 2)
    panel[pl.ds(pl.multiple_of(core * rows, rows), rows), :] = far[...]
    panel[pl.ds(pl.multiple_of((1 - core) * rows, rows), rows), :] = far_back[...]
    limit = (step + 1) * width - lax.axis_index("prow") * rows_dev
    copies = []
    for turn in range(1, chips + 1):
        start = pl.multiple_of(lax.rem(opposite_chip(chips) + turn, chips) * part, part)
        rows = pl.ds(start, part)
        if turn < chips:
            factor = (high[rows, :], low[rows, :])
        else:
            factor = split(jnp.where(start + iota(panel.shape, 0) >= limit, -panel[...], F32(0)))
        gather = one_hot(iota((part, width), 0) + start, offset)
        value = base[rows, :] + (pick(gather, displaced) + dot(factor, upper))
        result[rows, :] = with_top(step, start, value, upper_ref)
        copies.append(pltpu.make_async_copy(result.at[rows, :], out.at[rows, :], sems.at[turn - 1]))
        copies[-1].start()
    for copy in copies:
        copy.wait()


def stack(one, other, out):
    rows = one.shape[0]
    out[:rows, :] = one[...]
    out[rows:, :] = other[...]


def pack(own, near, before, out):
    rows = own.shape[0]
    out[:rows, :] = own[...]
    out[rows:, :] = near[...]


def ring_order(chips):
    return [0] + list(range(1, chips // 2 + 1)) + list(range(chips - 1, chips // 2, -1))


def release(panel, before, out):
    out[...] = panel[...]


def shift(block, distance, count):
    return lax.ppermute(block, "pcol", [(i, (i + 2 * distance) % count) for i in range(count)])


def across(block, count):
    return lax.ppermute(block, "pcol", [(i, i ^ 1) for i in range(count)])


def forwarded(block, down, count):
    chips = count // 2
    own = [block]
    for distance in ring_order(chips)[1:]:
        if distance <= chips // 2:
            own.append(shift(own[-1], 1, count))
        else:
            own.append(shift(down if distance == chips - 1 else own[-1], -1, count))
    return own


def passed(pair, count):
    onward = [(i, (i + (2 if i % 2 == 0 else -2)) % count) for i in range(count)]
    pairs = [pair]
    for _ in range(count // 4 - 1):
        pairs.append(lax.ppermute(pairs[-1], "pcol", onward))
    return pairs[1:]


def per_device(mesh, matrix, l_panels, l_inverse, pivots):
    rows_dev, columns = matrix.shape
    steps, width = pivots.shape
    process_rows, process_columns = mesh.shape["prow"], mesh.shape["pcol"]
    bits = [1 << b for b in range(process_rows.bit_length() - 1)]
    shape = jax.ShapeDtypeStruct
    square = shape((width, columns), F32)
    full = shape((rows_dev, columns), F32)

    def call(kernel, name, operands, outs, specs=None, out_specs=None, scratch=()):
        return pl.pallas_call(
            kernel,
            out_shape=outs,
            in_specs=specs or [VMEM] * len(operands),
            out_specs=out_specs or jax.tree.map(lambda _: VMEM, outs),
            scratch_shapes=scratch,
            compiler_params=GRANT,
            cost_estimate=pl.CostEstimate(COST[name], 0, 0) if name in COST else None,
            name=name,
        )(*operands)

    def exchange(sent, step, before=()):
        received = []
        for stage in range(len(bits)):
            if stage:
                operands = [sent, received[-1], owner[step], *before]
                specs = [VMEM] * 3 + [ANY] * len(before)
                sent = call(functools.partial(merge, bits, stage - 1), "merge", operands, square, specs=specs)
            pairs = []
            for i in range(process_rows):
                for j in range(process_columns):
                    bit = bits[len(bits) - 1 - stage] if j % 2 else bits[stage]
                    pairs.append((i * process_columns + j, (i ^ bit) * process_columns + j))
            received.append(lax.ppermute(sent, ("prow", "pcol"), pairs))
        return sent, received

    chunks = rows_dev // width
    halves = [pltpu.VMEM((rows_dev, l_panels.shape[2]), BF16)] * 2
    block = shape(l_panels.shape[1:], F32)
    matrix, pivots, *own = call(
        load,
        "load",
        [pltpu.with_memory_space_constraint(x, pltpu.HBM) for x in (matrix, pivots, l_panels)],
        [full, shape(pivots.shape, pivots.dtype)] + [block] * steps,
        specs=[HBM] * 3,
        scratch=[pltpu.SemaphoreType.DMA((1 + steps + PARTS,))],
    )
    slots = call(first_slots, "first_slots", [matrix, pivots], square)

    near = across(own[1], process_columns)

    def after(panel, before, name="release"):
        return call(release, name, [panel, before], shape(panel.shape, F32), specs=[VMEM, ANY])

    indices = shape((width, columns), jnp.int32)
    owner = call(functools.partial(holders, rows_dev), "holders", [pivots], [indices] * steps)
    base, ahead, places = call(
        prepare, "prepare", [matrix, pivots], [full, square, shape((width, width), jnp.int32)]
    )
    first = forwarded(own[0], after(own[0], places, "down_block"), process_columns)
    joint = call(stack, "stack", first[:2], shape((2 * block.shape[0], block.shape[1]), F32))
    joint = across(joint, process_columns)
    first += [joint] + [across(piece, process_columns) for piece in first[2:]]
    sent, received = exchange(slots, 0, [joint])
    two = shape((2 * block.shape[0], block.shape[1]), F32)
    pair = call(pack, "pack", [own[1], near, sent], two, specs=[VMEM, VMEM, ANY])
    late = late_blocks(process_columns // 2)
    early = [piece for position, piece in enumerate(first) if position not in late]
    factor = call(functools.partial(collect, late), "collect", [places, *early], [shape((width, width), BF16)] * 2)
    operands = [matrix, pivots, l_inverse, owner[0], ahead, places, sent, *received, *factor, *[first[position] for position in late]]
    upper, displaced, slots = call(functools.partial(solve, bits, 0, late), "solve", operands, [square] * 3)
    far = shift(after(own[1], slots, "far_block"), process_columns // 4, process_columns)
    pairs = passed(pair, process_columns)
    base, top = call(
        functools.partial(update, 0),
        "update",
        [base, pivots, upper, displaced, *first],
        [full, square],
        scratch=halves,
    )
    sent, received = exchange(slots, 1, [top])
    second = [own[1], near, far, across(after(far, own[1], "far_piece"), process_columns)]
    second += pairs + [across(after(piece, sent, "pair_piece"), process_columns) for piece in pairs]
    part, depth = 2 * block.shape[0], block.shape[1]
    high, low = call(
        functools.partial(halve, 1, rows_dev, width),
        "halve",
        second[:2] + second[4:],
        [shape((rows_dev, depth), BF16)] * 2,
    )
    return call(
        functools.partial(finish, bits, 1),
        "finish",
        [base, pivots, l_inverse, owner[1], top, high, low, *second[2:4], sent, *received],
        full,
        out_specs=HBM,
        scratch=[
            pltpu.VMEM((part, depth), F32),
            pltpu.VMEM((width, columns), F32),
            pltpu.VMEM((rows_dev, columns), F32),
            pltpu.SemaphoreType.DMA((rows_dev // part,)),
        ],
    )


def solution(mesh):
    placed = (P("prow", "pcol"), P(None, ("prow", "pcol"), None), P(), P())
    return jax.shard_map(
        functools.partial(per_device, mesh), mesh=mesh, in_specs=placed, out_specs=P("prow", "pcol"), check_vma=False
    )
```

```python
import functools

import jax
import jax.numpy as jnp
from jax import lax
from jax.experimental import pallas as pl
from jax.experimental.pallas import tpu as pltpu
from jax.sharding import PartitionSpec as P

VMEM = pl.BlockSpec(memory_space=pltpu.VMEM)
ANY = pl.BlockSpec(memory_space=pl.ANY)
HBM = pl.BlockSpec(memory_space=pltpu.HBM)
GRANT = pltpu.CompilerParams(vmem_limit_bytes=40 * 1024 * 1024)
F32 = jnp.float32
BF16 = jnp.bfloat16
NOWHERE = -(1 << 24)
COST = {
    "prepare": 1000 * 10**6,
    "down_block": 300 * 10**6,
    "far_block": 5000 * 10**6,
    "collect": 1500 * 10**6,
    "holders": 3000 * 10**6,
    "update": 5000 * 10**6,
    "pair_piece": 1000 * 10**6,
    "stack": 8000 * 10**6,
    "far_piece": 3000 * 10**6,
}
PARTS = 4


def product(left, right):
    return jnp.dot(left, right, preferred_element_type=F32)


def split(values):
    high = values.astype(BF16)
    low = (values - high.astype(F32)).astype(BF16)
    return high, low


def dot(left, right, gather=None, moved=None):
    lefts, rights = [left[0], left[0], left[1]], [right[0], right[1], right[0]]
    if gather is not None:
        lefts, rights = [gather, gather, *lefts], [*moved, *rights]
    return product(jnp.concatenate(lefts, axis=1), jnp.concatenate(rights, axis=0))


def pick(chosen, right):
    return product(jnp.concatenate([chosen, chosen], axis=1), jnp.concatenate(right, axis=0))


def one_hot(left, right):
    return jnp.where(left == right, F32(1), F32(0)).astype(BF16)


def iota(shape, dimension):
    return lax.broadcasted_iota(jnp.int32, shape, dimension)


def column_of(row):
    n = row.shape[1]
    spread = jnp.where(iota((n, n), 0) == iota((n, n), 1), row.astype(F32), F32(0))
    return jnp.sum(spread, axis=1, keepdims=True).astype(jnp.int32)


def local_rows(pivots, step, rows_dev):
    offset = pivots[step : step + 1, :] - lax.axis_index("prow") * rows_dev
    return jnp.where((offset >= 0) & (offset < rows_dev), offset, NOWHERE)


def slot_rows(pivots, step, rows_dev):
    offset = local_rows(pivots, step, rows_dev)
    width = offset.shape[1]
    top = jnp.where(lax.axis_index("prow") == 0, step * width + iota(offset.shape, 1), NOWHERE)
    return jnp.where(offset >= 0, offset, top)


def load(matrix, pivots, panels, held, chosen, *refs):
    blocks, sems = refs[:-1], refs[-1]
    rows = held.shape[0] // PARTS
    parts = [pl.ds(part * rows, rows) for part in range(PARTS)]
    sources = [panels.at[step] for step in range(len(blocks))] + [pivots] + [matrix.at[part, :] for part in parts]
    targets = [*blocks, chosen] + [held.at[part, :] for part in parts]
    copies = [pltpu.make_async_copy(*pair, sems.at[i]) for i, pair in enumerate(zip(sources, targets))]
    for copy in copies:
        copy.start()
    for copy in copies:
        copy.wait()


def first_slots(matrix, pivots, out):
    rows_dev = matrix.shape[0]
    place = column_of(slot_rows(pivots, 0, rows_dev))
    width = place.shape[0]
    total = None
    for start in range(0, rows_dev, width):
        gather = one_hot(place, iota((width, width), 1) + start)
        term = pick(gather, split(matrix[start : start + width, :]))
        total = term if total is None else total + term
    out[...] = total


def holders(rows_dev, pivots, *owners):
    for step, owner in enumerate(owners):
        owner[...] = jnp.broadcast_to(column_of(pivots[step : step + 1, :]) // rows_dev, owner.shape)


def prepare(matrix, pivots, base, ahead, places):
    rows_dev = matrix.shape[0]
    offset = local_rows(pivots, 0, rows_dev)
    width = offset.shape[1]
    place = column_of(slot_rows(pivots, 1, rows_dev))
    places[...] = jnp.broadcast_to(place, places.shape)
    total = None
    for start in range(0, rows_dev, width):
        hit = jnp.where(offset == iota((width, width), 0) + start, F32(1), F32(0))
        keep = jnp.sum(hit, axis=1, keepdims=True) == 0
        kept = jnp.where(keep, matrix[start : start + width, :], F32(0))
        base[start : start + width, :] = kept
        gather = one_hot(place, iota((width, width), 1) + start)
        term = pick(gather, split(kept))
        total = term if total is None else total + term
    ahead[...] = total


def stage_bits(bits, stage):
    odd = lax.rem(lax.axis_index("pcol"), 2) == 1
    bit = jnp.where(odd, bits[len(bits) - 1 - stage], bits[stage])
    known = jnp.where(odd, sum(bits[len(bits) - stage :]) if stage else 0, sum(bits[:stage]))
    return bit, known


def merge(bits, stage, sent, received, owner, *refs):
    row = lax.axis_index("prow")
    bit, known = stage_bits(bits, stage)
    partner = row ^ bit
    who = owner[...]
    keep = ~known
    theirs = ((who ^ partner) & keep) == 0
    neither = ((who ^ row) & ~(known | bit)) != 0
    take = theirs | (neither & ((partner & keep) == 0))
    refs[-1][...] = jnp.where(take, received[...], sent[...])


def picked_rows(bits, sent, received, owner):
    bit, _ = stage_bits(bits, len(bits) - 1)
    mine = ((owner[...] ^ lax.axis_index("prow")) & bit) == 0
    return jnp.where(mine, sent[...], received[-1][...])


def displaced_rows(bits, received, top):
    row = lax.axis_index("prow")
    value = received[-1][...]
    for stage in reversed(range(len(bits) - 1)):
        bit, known = stage_bits(bits, stage)
        value = jnp.where((row & ~(known | bit)) == 0, received[stage][...], value)
    return jnp.where(row == 0, top, value)


def place_of(chip, core, chips, rows):
    return pl.multiple_of((lax.rem(chip + chips, chips) * 2 + core) * rows, rows)


def rows_of(ref, index, count=1):
    rows = ref.shape[0] // count
    return ref.at[pl.ds(index * rows, rows), :]


def ring_blocks(refs):
    chips = (len(refs) + 1) // 2
    mine, joint, rest = refs[:chips], refs[chips], refs[chips + 1 :]
    rows = next(ref for ref in [*mine, *rest] if ref is not None).shape[0]
    others = [joint if joint is None else rows_of(joint, half, 2) for half in range(2)] + list(rest)
    chip, core = lax.axis_index("pcol") // 2, lax.rem(lax.axis_index("pcol"), 2)
    found = []
    for order, distance in enumerate(ring_order(chips)):
        found.append((mine[order], place_of(chip - distance, core, chips, rows)))
        found.append((others[order], place_of(chip - distance, 1 - core, chips, rows)))
    return found


def pair_blocks(refs):
    own, near, far, far_back, *rest = refs
    rows = own.shape[0]
    hops = len(rest) // 2
    chips = 2 * hops + 2
    chip, core = lax.axis_index("pcol") // 2, lax.rem(lax.axis_index("pcol"), 2)
    opposite = chip + chips // 2
    found = [
        (own, place_of(chip, core, chips, rows)),
        (near, place_of(chip, 1 - core, chips, rows)),
        (far, place_of(opposite, core, chips, rows)),
        (far_back, place_of(opposite, 1 - core, chips, rows)),
    ]
    for hop in range(hops):
        along = (hop + 1) * (1 - 2 * core)
        for half in range(2):
            owner = core if half == 0 else 1 - core
            found.append((rows_of(rest[hop], half, 2), place_of(chip - along, owner, chips, rows)))
            found.append((rows_of(rest[hops + hop], half, 2), place_of(chip + along, 1 - owner, chips, rows)))
    return found


def panel_rows(places, blocks):
    high = low = None
    for block, start in blocks:
        rows = block.shape[0]
        gather = one_hot(places[:, :rows] - start, iota((places.shape[0], rows), 1))
        block_high, block_low = split(block[...])
        term_high, term_low = product(gather, block_high), product(gather, block_low)
        high = term_high if high is None else high + term_high
        low = term_low if low is None else low + term_low
    return high, low


def late_blocks(chips):
    return [chips + chips // 2 - 1, 2 * chips - 2]


def collect(late, places, *refs):
    blocks, (high, low) = list(refs[:-2]), refs[-2:]
    for position in late:
        blocks.insert(position, None)
    found_high, found_low = panel_rows(places, [pair for pair in ring_blocks(blocks) if pair[0] is not None])
    high[...] = found_high.astype(BF16)
    low[...] = found_low.astype(BF16)


def solve(bits, step, late, matrix, pivots, inverse, owner, ahead, places, sent, *refs):
    refs = list(refs)
    received = [refs.pop(0) for _ in bits]
    high, low, *found, upper_out, displaced_out, slots = refs
    rows_dev = matrix.shape[0]
    picked = picked_rows(bits, sent, received, owner)
    width = picked.shape[0]
    upper = dot(split(inverse[step]), split(picked))
    upper_out[...] = upper
    displaced = displaced_rows(bits, received, matrix[step * width : (step + 1) * width, :])
    displaced_out[...] = displaced
    moved = one_hot(places[...], local_rows(pivots, step, rows_dev))
    blocks = [None] * (rows_dev // found[0].shape[0] - 1)
    for position, block in zip(late, found):
        blocks[position] = block
    rest_high, rest_low = panel_rows(places, [pair for pair in ring_blocks(blocks) if pair[0] is not None])
    factor = ((high[...].astype(F32) + rest_high).astype(BF16), (low[...].astype(F32) + rest_low).astype(BF16))
    slots[...] = ahead[...] + (pick(moved, split(displaced)) - dot(factor, split(upper)))


def assemble(step, blocks, rows_dev, width, high, low):
    limit = (step + 1) * width - lax.axis_index("prow") * rows_dev
    for block, start in blocks:
        if block is None:
            continue
        rows = block.shape[0]
        below = start + iota(block.shape, 0) >= limit
        block_high, block_low = split(jnp.where(below, -block[...], F32(0)))
        high[pl.ds(start, rows), :] = block_high
        low[pl.ds(start, rows), :] = block_low


def halve(step, rows_dev, width, own, near, *refs):
    blocks = pair_blocks([own, near, None, None, *refs[:-2]])
    assemble(step, blocks, rows_dev, width, refs[-2], refs[-1])


def update(step, base, pivots, upper_in, displaced_in, *refs):
    blocks, (out, top_out, high, low) = refs[:-4], refs[-4:]
    rows_dev = base.shape[0]
    width = upper_in.shape[0]
    assemble(step, ring_blocks(blocks), rows_dev, width, high, low)
    offset = local_rows(pivots, step, rows_dev)
    later = local_rows(pivots, step + 1, rows_dev)
    upper = split(upper_in[...])
    displaced = split(displaced_in[...])
    for start in range(0, rows_dev, width):
        part = slice(start, start + width)
        rows = iota((width, width), 0) + start
        value = base[part, :] + dot((high[part, :], low[part, :]), upper, one_hot(rows, offset), displaced)
        if start == step * width:
            value = jnp.where(lax.axis_index("prow") == 0, upper_in[...], value)
        if start == (step + 1) * width:
            top_out[...] = value
        hit = jnp.where(later == rows, F32(1), F32(0))
        out[part, :] = jnp.where(jnp.sum(hit, axis=1, keepdims=True) == 0, value, F32(0))


def opposite_chip(chips):
    return lax.rem(lax.axis_index("pcol") // 2 + chips // 2, chips)


def with_top(step, start, value, upper):
    part, width = value.shape[0], upper.shape[0]
    inside = start - step * width
    chosen = (lax.axis_index("prow") == 0) & (inside >= 0) & (inside < width)
    place = pl.multiple_of(jnp.clip(inside, 0, width - part), part)
    return jnp.where(chosen, upper[pl.ds(place, part), :], value)


def finish(bits, step, base, pivots, inverse, owner, top, high, low, far, far_back, sent, *refs):
    received, (out, panel, upper_ref, result, sems) = refs[:-5], refs[-5:]
    rows_dev, chips = base.shape[0], sems.shape[0]
    part = rows_dev // chips
    picked = picked_rows(bits, sent, received, owner)
    width = picked.shape[0]
    upper_ref[...] = dot(split(inverse[step]), split(picked))
    offset = local_rows(pivots, step, rows_dev)
    upper = split(upper_ref[...])
    displaced = split(displaced_rows(bits, received, top[...]))
    rows = far.shape[0]
    core = lax.rem(lax.axis_index("pcol"), 2)
    panel[pl.ds(pl.multiple_of(core * rows, rows), rows), :] = far[...]
    panel[pl.ds(pl.multiple_of((1 - core) * rows, rows), rows), :] = far_back[...]
    limit = (step + 1) * width - lax.axis_index("prow") * rows_dev
    copies = []
    for turn in range(1, chips + 1):
        start = pl.multiple_of(lax.rem(opposite_chip(chips) + turn, chips) * part, part)
        rows = pl.ds(start, part)
        if turn < chips:
            factor = (high[rows, :], low[rows, :])
        else:
            factor = split(jnp.where(start + iota(panel.shape, 0) >= limit, -panel[...], F32(0)))
        gather = one_hot(iota((part, width), 0) + start, offset)
        value = base[rows, :] + dot(factor, upper, gather, displaced)
        result[rows, :] = with_top(step, start, value, upper_ref)
        copies.append(pltpu.make_async_copy(result.at[rows, :], out.at[rows, :], sems.at[turn - 1]))
        copies[-1].start()
    for copy in copies:
        copy.wait()


def stack(one, other, out):
    rows = one.shape[0]
    out[:rows, :] = one[...]
    out[rows:, :] = other[...]


def pack(own, near, before, out):
    rows = own.shape[0]
    out[:rows, :] = own[...]
    out[rows:, :] = near[...]


def ring_order(chips):
    return [0] + list(range(1, chips // 2 + 1)) + list(range(chips - 1, chips // 2, -1))


def release(panel, before, out):
    out[...] = panel[...]


def shift(block, distance, count):
    return lax.ppermute(block, "pcol", [(i, (i + 2 * distance) % count) for i in range(count)])


def across(block, count):
    return lax.ppermute(block, "pcol", [(i, i ^ 1) for i in range(count)])


def forwarded(block, down, count):
    chips = count // 2
    own = [block]
    for distance in ring_order(chips)[1:]:
        if distance <= chips // 2:
            own.append(shift(own[-1], 1, count))
        else:
            own.append(shift(down if distance == chips - 1 else own[-1], -1, count))
    return own


def passed(pair, count):
    onward = [(i, (i + (2 if i % 2 == 0 else -2)) % count) for i in range(count)]
    pairs = [pair]
    for _ in range(count // 4 - 1):
        pairs.append(lax.ppermute(pairs[-1], "pcol", onward))
    return pairs[1:]


def per_device(mesh, matrix, l_panels, l_inverse, pivots):
    rows_dev, columns = matrix.shape
    steps, width = pivots.shape
    process_rows, process_columns = mesh.shape["prow"], mesh.shape["pcol"]
    bits = [1 << b for b in range(process_rows.bit_length() - 1)]
    shape = jax.ShapeDtypeStruct
    square = shape((width, columns), F32)
    full = shape((rows_dev, columns), F32)

    def call(kernel, name, operands, outs, specs=None, out_specs=None, scratch=()):
        return pl.pallas_call(
            kernel,
            out_shape=outs,
            in_specs=specs or [VMEM] * len(operands),
            out_specs=out_specs or jax.tree.map(lambda _: VMEM, outs),
            scratch_shapes=scratch,
            compiler_params=GRANT,
            cost_estimate=pl.CostEstimate(COST[name], 0, 0) if name in COST else None,
            name=name,
        )(*operands)

    def exchange(sent, step, before=()):
        received = []
        for stage in range(len(bits)):
            if stage:
                operands = [sent, received[-1], owner[step], *before]
                specs = [VMEM] * 3 + [ANY] * len(before)
                sent = call(functools.partial(merge, bits, stage - 1), "merge", operands, square, specs=specs)
            pairs = []
            for i in range(process_rows):
                for j in range(process_columns):
                    bit = bits[len(bits) - 1 - stage] if j % 2 else bits[stage]
                    pairs.append((i * process_columns + j, (i ^ bit) * process_columns + j))
            received.append(lax.ppermute(sent, ("prow", "pcol"), pairs))
        return sent, received

    chunks = rows_dev // width
    halves = [pltpu.VMEM((rows_dev, l_panels.shape[2]), BF16)] * 2
    block = shape(l_panels.shape[1:], F32)
    matrix, pivots, *own = call(
        load,
        "load",
        [pltpu.with_memory_space_constraint(x, pltpu.HBM) for x in (matrix, pivots, l_panels)],
        [full, shape(pivots.shape, pivots.dtype)] + [block] * steps,
        specs=[HBM] * 3,
        scratch=[pltpu.SemaphoreType.DMA((1 + steps + PARTS,))],
    )
    slots = call(first_slots, "first_slots", [matrix, pivots], square)

    near = across(own[1], process_columns)

    def after(panel, before, name="release"):
        return call(release, name, [panel, before], shape(panel.shape, F32), specs=[VMEM, ANY])

    indices = shape((width, columns), jnp.int32)
    owner = call(functools.partial(holders, rows_dev), "holders", [pivots], [indices] * steps)
    base, ahead, places = call(
        prepare, "prepare", [matrix, pivots], [full, square, shape((width, width), jnp.int32)]
    )
    first = forwarded(own[0], after(own[0], places, "down_block"), process_columns)
    joint = call(stack, "stack", first[:2], shape((2 * block.shape[0], block.shape[1]), F32))
    joint = across(joint, process_columns)
    first += [joint] + [across(piece, process_columns) for piece in first[2:]]
    sent, received = exchange(slots, 0, [joint])
    two = shape((2 * block.shape[0], block.shape[1]), F32)
    pair = call(pack, "pack", [own[1], near, sent], two, specs=[VMEM, VMEM, ANY])
    late = late_blocks(process_columns // 2)
    early = [piece for position, piece in enumerate(first) if position not in late]
    factor = call(functools.partial(collect, late), "collect", [places, *early], [shape((width, width), BF16)] * 2)
    operands = [matrix, pivots, l_inverse, owner[0], ahead, places, sent, *received, *factor, *[first[position] for position in late]]
    upper, displaced, slots = call(functools.partial(solve, bits, 0, late), "solve", operands, [square] * 3)
    far = shift(after(own[1], slots, "far_block"), process_columns // 4, process_columns)
    pairs = passed(pair, process_columns)
    base, top = call(
        functools.partial(update, 0),
        "update",
        [base, pivots, upper, displaced, *first],
        [full, square],
        scratch=halves,
    )
    sent, received = exchange(slots, 1, [top])
    second = [own[1], near, far, across(after(far, own[1], "far_piece"), process_columns)]
    second += pairs + [across(after(piece, sent, "pair_piece"), process_columns) for piece in pairs]
    part, depth = 2 * block.shape[0], block.shape[1]
    high, low = call(
        functools.partial(halve, 1, rows_dev, width),
        "halve",
        second[:2] + second[4:],
        [shape((rows_dev, depth), BF16)] * 2,
    )
    return call(
        functools.partial(finish, bits, 1),
        "finish",
        [base, pivots, l_inverse, owner[1], top, high, low, *second[2:4], sent, *received],
        full,
        out_specs=HBM,
        scratch=[
            pltpu.VMEM((part, depth), F32),
            pltpu.VMEM((width, columns), F32),
            pltpu.VMEM((rows_dev, columns), F32),
            pltpu.SemaphoreType.DMA((rows_dev // part,)),
        ],
    )


def solution(mesh):
    placed = (P("prow", "pcol"), P(None, ("prow", "pcol"), None), P(), P())
    return jax.shard_map(
        functools.partial(per_device, mesh), mesh=mesh, in_specs=placed, out_specs=P("prow", "pcol"), check_vma=False
    )
```

```python
import functools

import jax
import jax.numpy as jnp
from jax import lax
from jax.experimental import pallas as pl
from jax.experimental.pallas import tpu as pltpu
from jax.sharding import PartitionSpec as P

VMEM = pl.BlockSpec(memory_space=pltpu.VMEM)
ANY = pl.BlockSpec(memory_space=pl.ANY)
HBM = pl.BlockSpec(memory_space=pltpu.HBM)
GRANT = pltpu.CompilerParams(vmem_limit_bytes=40 * 1024 * 1024)
F32 = jnp.float32
BF16 = jnp.bfloat16
NOWHERE = -(1 << 24)
COST = {
    "prepare": 1000 * 10**6,
    "down_block": 300 * 10**6,
    "far_block": 5000 * 10**6,
    "collect": 1500 * 10**6,
    "holders": 3000 * 10**6,
    "update": 5000 * 10**6,
    "pair_piece": 1000 * 10**6,
    "stack": 8000 * 10**6,
    "far_piece": 3000 * 10**6,
}
PARTS = 4


def product(left, right):
    return jnp.dot(left, right, preferred_element_type=F32)


def split(values):
    high = values.astype(BF16)
    low = (values - high.astype(F32)).astype(BF16)
    return high, low


def dot(left, right, gather=None, moved=None):
    lefts, rights = [left[0], left[0], left[1]], [right[0], right[1], right[0]]
    if gather is not None:
        lefts, rights = [gather, gather, *lefts], [*moved, *rights]
    return product(jnp.concatenate(lefts, axis=1), jnp.concatenate(rights, axis=0))


def pick(chosen, right):
    return product(jnp.concatenate([chosen, chosen], axis=1), jnp.concatenate(right, axis=0))


def one_hot(left, right):
    return jnp.where(left == right, F32(1), F32(0)).astype(BF16)


def iota(shape, dimension):
    return lax.broadcasted_iota(jnp.int32, shape, dimension)


def column_of(row):
    n = row.shape[1]
    spread = jnp.where(iota((n, n), 0) == iota((n, n), 1), row.astype(F32), F32(0))
    return jnp.sum(spread, axis=1, keepdims=True).astype(jnp.int32)


def local_rows(pivots, step, rows_dev):
    offset = pivots[step : step + 1, :] - lax.axis_index("prow") * rows_dev
    return jnp.where((offset >= 0) & (offset < rows_dev), offset, NOWHERE)


def slot_rows(pivots, step, rows_dev):
    offset = local_rows(pivots, step, rows_dev)
    width = offset.shape[1]
    top = jnp.where(lax.axis_index("prow") == 0, step * width + iota(offset.shape, 1), NOWHERE)
    return jnp.where(offset >= 0, offset, top)


def load(matrix, pivots, panels, held, chosen, *refs):
    blocks, sems = refs[:-1], refs[-1]
    rows = held.shape[0] // PARTS
    parts = [pl.ds(part * rows, rows) for part in range(PARTS)]
    sources = [panels.at[step] for step in range(len(blocks))] + [pivots] + [matrix.at[part, :] for part in parts]
    targets = [*blocks, chosen] + [held.at[part, :] for part in parts]
    copies = [pltpu.make_async_copy(*pair, sems.at[i]) for i, pair in enumerate(zip(sources, targets))]
    for copy in copies:
        copy.start()
    for copy in copies:
        copy.wait()


def first_slots(matrix, pivots, out):
    rows_dev = matrix.shape[0]
    place = column_of(slot_rows(pivots, 0, rows_dev))
    width = place.shape[0]
    total = None
    for start in range(0, rows_dev, width):
        gather = one_hot(place, iota((width, width), 1) + start)
        term = pick(gather, split(matrix[start : start + width, :]))
        total = term if total is None else total + term
    out[...] = total


def holders(rows_dev, pivots, *owners):
    for step, owner in enumerate(owners):
        owner[...] = jnp.broadcast_to(column_of(pivots[step : step + 1, :]) // rows_dev, owner.shape)


def prepare(matrix, pivots, base, ahead, places):
    rows_dev = matrix.shape[0]
    offset = local_rows(pivots, 0, rows_dev)
    width = offset.shape[1]
    place = column_of(slot_rows(pivots, 1, rows_dev))
    places[...] = jnp.broadcast_to(place, places.shape)
    total = None
    for start in range(0, rows_dev, width):
        hit = jnp.where(offset == iota((width, width), 0) + start, F32(1), F32(0))
        keep = jnp.sum(hit, axis=1, keepdims=True) == 0
        kept = jnp.where(keep, matrix[start : start + width, :], F32(0))
        base[start : start + width, :] = kept
        gather = one_hot(place, iota((width, width), 1) + start)
        term = pick(gather, split(kept))
        total = term if total is None else total + term
    ahead[...] = total


def stage_bits(bits, stage):
    odd = lax.rem(lax.axis_index("pcol"), 2) == 1
    bit = jnp.where(odd, bits[len(bits) - 1 - stage], bits[stage])
    known = jnp.where(odd, sum(bits[len(bits) - stage :]) if stage else 0, sum(bits[:stage]))
    return bit, known


def merge(bits, stage, sent, received, owner, *refs):
    row = lax.axis_index("prow")
    bit, known = stage_bits(bits, stage)
    partner = row ^ bit
    who = owner[...]
    keep = ~known
    theirs = ((who ^ partner) & keep) == 0
    neither = ((who ^ row) & ~(known | bit)) != 0
    take = theirs | (neither & ((partner & keep) == 0))
    refs[-1][...] = jnp.where(take, received[...], sent[...])


def picked_rows(bits, sent, received, owner):
    bit, _ = stage_bits(bits, len(bits) - 1)
    mine = ((owner[...] ^ lax.axis_index("prow")) & bit) == 0
    return jnp.where(mine, sent[...], received[-1][...])


def displaced_rows(bits, received, top):
    row = lax.axis_index("prow")
    value = received[-1][...]
    for stage in reversed(range(len(bits) - 1)):
        bit, known = stage_bits(bits, stage)
        value = jnp.where((row & ~(known | bit)) == 0, received[stage][...], value)
    return jnp.where(row == 0, top, value)


def place_of(chip, core, chips, rows):
    return pl.multiple_of((lax.rem(chip + chips, chips) * 2 + core) * rows, rows)


def rows_of(ref, index, count=1):
    rows = ref.shape[0] // count
    return ref.at[pl.ds(index * rows, rows), :]


def ring_blocks(refs):
    chips = (len(refs) + 1) // 2
    mine, joint, rest = refs[:chips], refs[chips], refs[chips + 1 :]
    rows = next(ref for ref in [*mine, *rest] if ref is not None).shape[0]
    others = [joint if joint is None else rows_of(joint, half, 2) for half in range(2)] + list(rest)
    chip, core = lax.axis_index("pcol") // 2, lax.rem(lax.axis_index("pcol"), 2)
    found = []
    for order, distance in enumerate(ring_order(chips)):
        found.append((mine[order], place_of(chip - distance, core, chips, rows)))
        found.append((others[order], place_of(chip - distance, 1 - core, chips, rows)))
    return found


def pair_blocks(refs):
    own, near, far, far_back, *rest = refs
    rows = own.shape[0]
    hops = len(rest) // 2
    chips = 2 * hops + 2
    chip, core = lax.axis_index("pcol") // 2, lax.rem(lax.axis_index("pcol"), 2)
    opposite = chip + chips // 2
    found = [
        (own, place_of(chip, core, chips, rows)),
        (near, place_of(chip, 1 - core, chips, rows)),
        (far, place_of(opposite, core, chips, rows)),
        (far_back, place_of(opposite, 1 - core, chips, rows)),
    ]
    for hop in range(hops):
        along = (hop + 1) * (1 - 2 * core)
        for half in range(2):
            owner = core if half == 0 else 1 - core
            found.append((rows_of(rest[hop], half, 2), place_of(chip - along, owner, chips, rows)))
            found.append((rows_of(rest[hops + hop], half, 2), place_of(chip + along, 1 - owner, chips, rows)))
    return found


def panel_rows(places, blocks):
    high = low = None
    for block, start in blocks:
        rows = block.shape[0]
        gather = one_hot(places[:, :rows] - start, iota((places.shape[0], rows), 1))
        block_high, block_low = split(block[...])
        term_high, term_low = product(gather, block_high), product(gather, block_low)
        high = term_high if high is None else high + term_high
        low = term_low if low is None else low + term_low
    return high, low


def late_blocks(chips):
    return [chips + chips // 2 - 1, 2 * chips - 2]


def collect(late, places, *refs):
    blocks, (high, low) = list(refs[:-2]), refs[-2:]
    for position in late:
        blocks.insert(position, None)
    found_high, found_low = panel_rows(places, [pair for pair in ring_blocks(blocks) if pair[0] is not None])
    high[...] = found_high.astype(BF16)
    low[...] = found_low.astype(BF16)


def solve(bits, step, late, matrix, pivots, inverse, owner, ahead, places, sent, *refs):
    refs = list(refs)
    received = [refs.pop(0) for _ in bits]
    high, low, *found, upper_out, displaced_out, slots = refs
    rows_dev = matrix.shape[0]
    picked = picked_rows(bits, sent, received, owner)
    width = picked.shape[0]
    upper = dot(split(inverse[step]), split(picked))
    upper_out[...] = upper
    displaced = displaced_rows(bits, received, matrix[step * width : (step + 1) * width, :])
    displaced_out[...] = displaced
    moved = one_hot(places[...], local_rows(pivots, step, rows_dev))
    blocks = [None] * (rows_dev // found[0].shape[0] - 1)
    for position, block in zip(late, found):
        blocks[position] = block
    rest_high, rest_low = panel_rows(places, [pair for pair in ring_blocks(blocks) if pair[0] is not None])
    factor = ((high[...].astype(F32) + rest_high).astype(BF16), (low[...].astype(F32) + rest_low).astype(BF16))
    slots[...] = ahead[...] + (pick(moved, split(displaced)) - dot(factor, split(upper)))


def assemble(step, blocks, rows_dev, width, high, low):
    limit = (step + 1) * width - lax.axis_index("prow") * rows_dev
    for block, start in blocks:
        if block is None:
            continue
        rows = block.shape[0]
        below = start + iota(block.shape, 0) >= limit
        block_high, block_low = split(jnp.where(below, -block[...], F32(0)))
        high[pl.ds(start, rows), :] = block_high
        low[pl.ds(start, rows), :] = block_low


def halve(step, rows_dev, width, own, near, *refs):
    blocks = pair_blocks([own, near, None, None, *refs[:-2]])
    assemble(step, blocks, rows_dev, width, refs[-2], refs[-1])


def update(step, base, pivots, upper_in, displaced_in, *refs):
    blocks, (out, top_out, high, low) = refs[:-4], refs[-4:]
    rows_dev = base.shape[0]
    width = upper_in.shape[0]
    assemble(step, ring_blocks(blocks), rows_dev, width, high, low)
    offset = local_rows(pivots, step, rows_dev)
    later = local_rows(pivots, step + 1, rows_dev)
    upper = split(upper_in[...])
    displaced = split(displaced_in[...])
    for start in range(0, rows_dev, width):
        part = slice(start, start + width)
        rows = iota((width, width), 0) + start
        value = base[part, :] + dot((high[part, :], low[part, :]), upper, one_hot(rows, offset), displaced)
        if start == step * width:
            value = jnp.where(lax.axis_index("prow") == 0, upper_in[...], value)
        if start == (step + 1) * width:
            top_out[...] = value
        hit = jnp.where(later == rows, F32(1), F32(0))
        out[part, :] = jnp.where(jnp.sum(hit, axis=1, keepdims=True) == 0, value, F32(0))


def opposite_chip(chips):
    return lax.rem(lax.axis_index("pcol") // 2 + chips // 2, chips)


def with_top(step, start, value, upper):
    part, width = value.shape[0], upper.shape[0]
    inside = start - step * width
    chosen = (lax.axis_index("prow") == 0) & (inside >= 0) & (inside < width)
    place = pl.multiple_of(jnp.clip(inside, 0, width - part), part)
    return jnp.where(chosen, upper[pl.ds(place, part), :], value)


def finish(bits, step, base, pivots, inverse, owner, top, high, low, far, far_back, sent, *refs):
    received, (out, panel, upper_ref, result, sems) = refs[:-5], refs[-5:]
    rows_dev, chips = base.shape[0], sems.shape[0] - 1
    part = rows_dev // chips
    picked = picked_rows(bits, sent, received, owner)
    width = picked.shape[0]
    upper_ref[...] = dot(split(inverse[step]), split(picked))
    offset = local_rows(pivots, step, rows_dev)
    upper = split(upper_ref[...])
    displaced = split(displaced_rows(bits, received, top[...]))
    rows = far.shape[0]
    core = lax.rem(lax.axis_index("pcol"), 2)
    panel[pl.ds(pl.multiple_of(core * rows, rows), rows), :] = far[...]
    panel[pl.ds(pl.multiple_of((1 - core) * rows, rows), rows), :] = far_back[...]
    limit = (step + 1) * width - lax.axis_index("prow") * rows_dev
    copies = []
    pieces = [(turn, 0, part) for turn in range(1, chips)] + [(chips, 0, part // 2), (chips, part // 2, part // 2)]
    for turn, skip, size in pieces:
        start = pl.multiple_of(lax.rem(opposite_chip(chips) + turn, chips) * part + skip, size)
        rows = pl.ds(start, size)
        if turn < chips:
            factor = (high[rows, :], low[rows, :])
        else:
            block = panel[skip : skip + size, :]
            factor = split(jnp.where(start + iota(block.shape, 0) >= limit, -block, F32(0)))
        gather = one_hot(iota((size, width), 0) + start, offset)
        value = base[rows, :] + dot(factor, upper, gather, displaced)
        result[rows, :] = with_top(step, start, value, upper_ref)
        copies.append(pltpu.make_async_copy(result.at[rows, :], out.at[rows, :], sems.at[len(copies)]))
        copies[-1].start()
    for copy in copies:
        copy.wait()


def stack(one, other, out):
    rows = one.shape[0]
    out[:rows, :] = one[...]
    out[rows:, :] = other[...]


def pack(own, near, before, out):
    rows = own.shape[0]
    out[:rows, :] = own[...]
    out[rows:, :] = near[...]


def ring_order(chips):
    return [0] + list(range(1, chips // 2 + 1)) + list(range(chips - 1, chips // 2, -1))


def release(panel, before, out):
    out[...] = panel[...]


def shift(block, distance, count):
    return lax.ppermute(block, "pcol", [(i, (i + 2 * distance) % count) for i in range(count)])


def across(block, count):
    return lax.ppermute(block, "pcol", [(i, i ^ 1) for i in range(count)])


def forwarded(block, down, count):
    chips = count // 2
    own = [block]
    for distance in ring_order(chips)[1:]:
        if distance <= chips // 2:
            own.append(shift(own[-1], 1, count))
        else:
            own.append(shift(down if distance == chips - 1 else own[-1], -1, count))
    return own


def passed(pair, count):
    onward = [(i, (i + (2 if i % 2 == 0 else -2)) % count) for i in range(count)]
    pairs = [pair]
    for _ in range(count // 4 - 1):
        pairs.append(lax.ppermute(pairs[-1], "pcol", onward))
    return pairs[1:]


def per_device(mesh, matrix, l_panels, l_inverse, pivots):
    rows_dev, columns = matrix.shape
    steps, width = pivots.shape
    process_rows, process_columns = mesh.shape["prow"], mesh.shape["pcol"]
    bits = [1 << b for b in range(process_rows.bit_length() - 1)]
    shape = jax.ShapeDtypeStruct
    square = shape((width, columns), F32)
    full = shape((rows_dev, columns), F32)

    def call(kernel, name, operands, outs, specs=None, out_specs=None, scratch=()):
        return pl.pallas_call(
            kernel,
            out_shape=outs,
            in_specs=specs or [VMEM] * len(operands),
            out_specs=out_specs or jax.tree.map(lambda _: VMEM, outs),
            scratch_shapes=scratch,
            compiler_params=GRANT,
            cost_estimate=pl.CostEstimate(COST[name], 0, 0) if name in COST else None,
            name=name,
        )(*operands)

    def exchange(sent, step, before=()):
        received = []
        for stage in range(len(bits)):
            if stage:
                operands = [sent, received[-1], owner[step], *before]
                specs = [VMEM] * 3 + [ANY] * len(before)
                sent = call(functools.partial(merge, bits, stage - 1), "merge", operands, square, specs=specs)
            pairs = []
            for i in range(process_rows):
                for j in range(process_columns):
                    bit = bits[len(bits) - 1 - stage] if j % 2 else bits[stage]
                    pairs.append((i * process_columns + j, (i ^ bit) * process_columns + j))
            received.append(lax.ppermute(sent, ("prow", "pcol"), pairs))
        return sent, received

    chunks = rows_dev // width
    halves = [pltpu.VMEM((rows_dev, l_panels.shape[2]), BF16)] * 2
    block = shape(l_panels.shape[1:], F32)
    matrix, pivots, *own = call(
        load,
        "load",
        [pltpu.with_memory_space_constraint(x, pltpu.HBM) for x in (matrix, pivots, l_panels)],
        [full, shape(pivots.shape, pivots.dtype)] + [block] * steps,
        specs=[HBM] * 3,
        scratch=[pltpu.SemaphoreType.DMA((1 + steps + PARTS,))],
    )
    slots = call(first_slots, "first_slots", [matrix, pivots], square)

    near = across(own[1], process_columns)

    def after(panel, before, name="release"):
        return call(release, name, [panel, before], shape(panel.shape, F32), specs=[VMEM, ANY])

    indices = shape((width, columns), jnp.int32)
    owner = call(functools.partial(holders, rows_dev), "holders", [pivots], [indices] * steps)
    base, ahead, places = call(
        prepare, "prepare", [matrix, pivots], [full, square, shape((width, width), jnp.int32)]
    )
    first = forwarded(own[0], after(own[0], places, "down_block"), process_columns)
    joint = call(stack, "stack", first[:2], shape((2 * block.shape[0], block.shape[1]), F32))
    joint = across(joint, process_columns)
    first += [joint] + [across(piece, process_columns) for piece in first[2:]]
    sent, received = exchange(slots, 0, [joint])
    two = shape((2 * block.shape[0], block.shape[1]), F32)
    pair = call(pack, "pack", [own[1], near, sent], two, specs=[VMEM, VMEM, ANY])
    late = late_blocks(process_columns // 2)
    early = [piece for position, piece in enumerate(first) if position not in late]
    factor = call(functools.partial(collect, late), "collect", [places, *early], [shape((width, width), BF16)] * 2)
    operands = [matrix, pivots, l_inverse, owner[0], ahead, places, sent, *received, *factor, *[first[position] for position in late]]
    upper, displaced, slots = call(functools.partial(solve, bits, 0, late), "solve", operands, [square] * 3)
    far = shift(after(own[1], slots, "far_block"), process_columns // 4, process_columns)
    pairs = passed(pair, process_columns)
    base, top = call(
        functools.partial(update, 0),
        "update",
        [base, pivots, upper, displaced, *first],
        [full, square],
        scratch=halves,
    )
    sent, received = exchange(slots, 1, [top])
    second = [own[1], near, far, across(after(far, own[1], "far_piece"), process_columns)]
    second += pairs + [across(after(piece, sent, "pair_piece"), process_columns) for piece in pairs]
    part, depth = 2 * block.shape[0], block.shape[1]
    high, low = call(
        functools.partial(halve, 1, rows_dev, width),
        "halve",
        second[:2] + second[4:],
        [shape((rows_dev, depth), BF16)] * 2,
    )
    return call(
        functools.partial(finish, bits, 1),
        "finish",
        [base, pivots, l_inverse, owner[1], top, high, low, *second[2:4], sent, *received],
        full,
        out_specs=HBM,
        scratch=[
            pltpu.VMEM((part, depth), F32),
            pltpu.VMEM((width, columns), F32),
            pltpu.VMEM((rows_dev, columns), F32),
            pltpu.SemaphoreType.DMA((rows_dev // part + 1,)),
        ],
    )


def solution(mesh):
    placed = (P("prow", "pcol"), P(None, ("prow", "pcol"), None), P(), P())
    return jax.shard_map(
        functools.partial(per_device, mesh), mesh=mesh, in_specs=placed, out_specs=P("prow", "pcol"), check_vma=False
    )
```

```python
import functools

import jax
import jax.numpy as jnp
from jax import lax
from jax.experimental import pallas as pl
from jax.experimental.pallas import tpu as pltpu
from jax.sharding import PartitionSpec as P

VMEM = pl.BlockSpec(memory_space=pltpu.VMEM)
ANY = pl.BlockSpec(memory_space=pl.ANY)
HBM = pl.BlockSpec(memory_space=pltpu.HBM)
GRANT = pltpu.CompilerParams(vmem_limit_bytes=40 * 1024 * 1024)
F32 = jnp.float32
BF16 = jnp.bfloat16
NOWHERE = -(1 << 24)
COST = {
    "prepare": 1000 * 10**6,
    "down_block": 300 * 10**6,
    "far_block": 5000 * 10**6,
    "collect": 1500 * 10**6,
    "holders": 3000 * 10**6,
    "update": 5000 * 10**6,
    "pair_piece": 1000 * 10**6,
    "stack": 8000 * 10**6,
    "far_piece": 3000 * 10**6,
}
PARTS = 4


def product(left, right):
    return jnp.dot(left, right, preferred_element_type=F32)


def split(values):
    high = values.astype(BF16)
    low = (values - high.astype(F32)).astype(BF16)
    return high, low


def dot(left, right, gather=None, moved=None):
    lefts, rights = [left[0], left[0], left[1]], [right[0], right[1], right[0]]
    if gather is not None:
        lefts, rights = [gather, gather, *lefts], [*moved, *rights]
    return product(jnp.concatenate(lefts, axis=1), jnp.concatenate(rights, axis=0))


def pick(chosen, right):
    return product(chosen, right[0]) + product(chosen, right[1])


def one_hot(left, right):
    return jnp.where(left == right, F32(1), F32(0)).astype(BF16)


def iota(shape, dimension):
    return lax.broadcasted_iota(jnp.int32, shape, dimension)


def column_of(row):
    n = row.shape[1]
    spread = jnp.where(iota((n, n), 0) == iota((n, n), 1), row.astype(F32), F32(0))
    return jnp.sum(spread, axis=1, keepdims=True).astype(jnp.int32)


def local_rows(pivots, step, rows_dev):
    offset = pivots[step : step + 1, :] - lax.axis_index("prow") * rows_dev
    return jnp.where((offset >= 0) & (offset < rows_dev), offset, NOWHERE)


def slot_rows(pivots, step, rows_dev):
    offset = local_rows(pivots, step, rows_dev)
    width = offset.shape[1]
    top = jnp.where(lax.axis_index("prow") == 0, step * width + iota(offset.shape, 1), NOWHERE)
    return jnp.where(offset >= 0, offset, top)


def load(matrix, pivots, panels, held, chosen, *refs):
    blocks, sems = refs[:-1], refs[-1]
    rows = held.shape[0] // PARTS
    parts = [pl.ds(part * rows, rows) for part in range(PARTS)]
    sources = [panels.at[step] for step in range(len(blocks))] + [pivots] + [matrix.at[part, :] for part in parts]
    targets = [*blocks, chosen] + [held.at[part, :] for part in parts]
    copies = [pltpu.make_async_copy(*pair, sems.at[i]) for i, pair in enumerate(zip(sources, targets))]
    for copy in copies:
        copy.start()
    for copy in copies:
        copy.wait()


def first_slots(matrix, pivots, out):
    rows_dev = matrix.shape[0]
    place = column_of(slot_rows(pivots, 0, rows_dev))
    width = place.shape[0]
    total = None
    for start in range(0, rows_dev, width):
        gather = one_hot(place, iota((width, width), 1) + start)
        term = pick(gather, split(matrix[start : start + width, :]))
        total = term if total is None else total + term
    out[...] = total


def holders(rows_dev, pivots, *owners):
    for step, owner in enumerate(owners):
        owner[...] = jnp.broadcast_to(column_of(pivots[step : step + 1, :]) // rows_dev, owner.shape)


def prepare(matrix, pivots, base, ahead, places):
    rows_dev = matrix.shape[0]
    offset = local_rows(pivots, 0, rows_dev)
    width = offset.shape[1]
    place = column_of(slot_rows(pivots, 1, rows_dev))
    places[...] = jnp.broadcast_to(place, places.shape)
    total = None
    for start in range(0, rows_dev, width):
        hit = jnp.where(offset == iota((width, width), 0) + start, F32(1), F32(0))
        keep = jnp.sum(hit, axis=1, keepdims=True) == 0
        kept = jnp.where(keep, matrix[start : start + width, :], F32(0))
        base[start : start + width, :] = kept
        gather = one_hot(place, iota((width, width), 1) + start)
        term = pick(gather, split(kept))
        total = term if total is None else total + term
    ahead[...] = total


def stage_bits(bits, stage):
    odd = lax.rem(lax.axis_index("pcol"), 2) == 1
    bit = jnp.where(odd, bits[len(bits) - 1 - stage], bits[stage])
    known = jnp.where(odd, sum(bits[len(bits) - stage :]) if stage else 0, sum(bits[:stage]))
    return bit, known


def merge(bits, stage, sent, received, owner, *refs):
    row = lax.axis_index("prow")
    bit, known = stage_bits(bits, stage)
    partner = row ^ bit
    who = owner[...]
    keep = ~known
    theirs = ((who ^ partner) & keep) == 0
    neither = ((who ^ row) & ~(known | bit)) != 0
    take = theirs | (neither & ((partner & keep) == 0))
    refs[-1][...] = jnp.where(take, received[...], sent[...])


def picked_rows(bits, sent, received, owner):
    bit, _ = stage_bits(bits, len(bits) - 1)
    mine = ((owner[...] ^ lax.axis_index("prow")) & bit) == 0
    return jnp.where(mine, sent[...], received[-1][...])


def displaced_rows(bits, received, top):
    row = lax.axis_index("prow")
    value = received[-1][...]
    for stage in reversed(range(len(bits) - 1)):
        bit, known = stage_bits(bits, stage)
        value = jnp.where((row & ~(known | bit)) == 0, received[stage][...], value)
    return jnp.where(row == 0, top, value)


def place_of(chip, core, chips, rows):
    return pl.multiple_of((lax.rem(chip + chips, chips) * 2 + core) * rows, rows)


def rows_of(ref, index, count=1):
    rows = ref.shape[0] // count
    return ref.at[pl.ds(index * rows, rows), :]


def ring_blocks(refs):
    chips = (len(refs) + 1) // 2
    mine, joint, rest = refs[:chips], refs[chips], refs[chips + 1 :]
    rows = next(ref for ref in [*mine, *rest] if ref is not None).shape[0]
    others = [joint if joint is None else rows_of(joint, half, 2) for half in range(2)] + list(rest)
    chip, core = lax.axis_index("pcol") // 2, lax.rem(lax.axis_index("pcol"), 2)
    found = []
    for order, distance in enumerate(ring_order(chips)):
        found.append((mine[order], place_of(chip - distance, core, chips, rows)))
        found.append((others[order], place_of(chip - distance, 1 - core, chips, rows)))
    return found


def pair_blocks(refs):
    own, near, far, far_back, *rest = refs
    rows = own.shape[0]
    hops = len(rest) // 2
    chips = 2 * hops + 2
    chip, core = lax.axis_index("pcol") // 2, lax.rem(lax.axis_index("pcol"), 2)
    opposite = chip + chips // 2
    found = [
        (own, place_of(chip, core, chips, rows)),
        (near, place_of(chip, 1 - core, chips, rows)),
        (far, place_of(opposite, core, chips, rows)),
        (far_back, place_of(opposite, 1 - core, chips, rows)),
    ]
    for hop in range(hops):
        along = (hop + 1) * (1 - 2 * core)
        for half in range(2):
            owner = core if half == 0 else 1 - core
            found.append((rows_of(rest[hop], half, 2), place_of(chip - along, owner, chips, rows)))
            found.append((rows_of(rest[hops + hop], half, 2), place_of(chip + along, 1 - owner, chips, rows)))
    return found


def panel_rows(places, blocks):
    high = low = None
    for block, start in blocks:
        rows = block.shape[0]
        gather = one_hot(places[:, :rows] - start, iota((places.shape[0], rows), 1))
        block_high, block_low = split(block[...])
        term_high, term_low = product(gather, block_high), product(gather, block_low)
        high = term_high if high is None else high + term_high
        low = term_low if low is None else low + term_low
    return high, low


def late_blocks(chips):
    return [chips + chips // 2 - 1, 2 * chips - 2]


def collect(late, places, *refs):
    blocks, (high, low) = list(refs[:-2]), refs[-2:]
    for position in late:
        blocks.insert(position, None)
    found_high, found_low = panel_rows(places, [pair for pair in ring_blocks(blocks) if pair[0] is not None])
    high[...] = found_high.astype(BF16)
    low[...] = found_low.astype(BF16)


def solve(bits, step, late, matrix, pivots, inverse, owner, ahead, places, sent, *refs):
    refs = list(refs)
    received = [refs.pop(0) for _ in bits]
    high, low, *found, upper_out, displaced_out, slots = refs
    rows_dev = matrix.shape[0]
    picked = picked_rows(bits, sent, received, owner)
    width = picked.shape[0]
    upper = dot(split(inverse[step]), split(picked))
    upper_out[...] = upper
    displaced = displaced_rows(bits, received, matrix[step * width : (step + 1) * width, :])
    displaced_out[...] = displaced
    moved = one_hot(places[...], local_rows(pivots, step, rows_dev))
    blocks = [None] * (rows_dev // found[0].shape[0] - 1)
    for position, block in zip(late, found):
        blocks[position] = block
    rest_high, rest_low = panel_rows(places, [pair for pair in ring_blocks(blocks) if pair[0] is not None])
    factor = ((high[...].astype(F32) + rest_high).astype(BF16), (low[...].astype(F32) + rest_low).astype(BF16))
    slots[...] = ahead[...] + (pick(moved, split(displaced)) - dot(factor, split(upper)))


def assemble(step, blocks, rows_dev, width, high, low):
    limit = (step + 1) * width - lax.axis_index("prow") * rows_dev
    for block, start in blocks:
        if block is None:
            continue
        rows = block.shape[0]
        below = start + iota(block.shape, 0) >= limit
        block_high, block_low = split(jnp.where(below, -block[...], F32(0)))
        high[pl.ds(start, rows), :] = block_high
        low[pl.ds(start, rows), :] = block_low


def halve(step, rows_dev, width, own, near, *refs):
    blocks = pair_blocks([own, near, None, None, *refs[:-2]])
    assemble(step, blocks, rows_dev, width, refs[-2], refs[-1])


def update(step, base, pivots, upper_in, displaced_in, *refs):
    blocks, (out, top_out, high, low) = refs[:-4], refs[-4:]
    rows_dev = base.shape[0]
    width = upper_in.shape[0]
    assemble(step, ring_blocks(blocks), rows_dev, width, high, low)
    offset = local_rows(pivots, step, rows_dev)
    later = local_rows(pivots, step + 1, rows_dev)
    upper = split(upper_in[...])
    displaced = split(displaced_in[...])
    for start in range(0, rows_dev, width):
        part = slice(start, start + width)
        rows = iota((width, width), 0) + start
        value = base[part, :] + dot((high[part, :], low[part, :]), upper, one_hot(rows, offset), displaced)
        if start == step * width:
            value = jnp.where(lax.axis_index("prow") == 0, upper_in[...], value)
        if start == (step + 1) * width:
            top_out[...] = value
        hit = jnp.where(later == rows, F32(1), F32(0))
        out[part, :] = jnp.where(jnp.sum(hit, axis=1, keepdims=True) == 0, value, F32(0))


def opposite_chip(chips):
    return lax.rem(lax.axis_index("pcol") // 2 + chips // 2, chips)


def with_top(step, start, value, upper):
    part, width = value.shape[0], upper.shape[0]
    inside = start - step * width
    chosen = (lax.axis_index("prow") == 0) & (inside >= 0) & (inside < width)
    place = pl.multiple_of(jnp.clip(inside, 0, width - part), part)
    return jnp.where(chosen, upper[pl.ds(place, part), :], value)


def finish(bits, step, base, pivots, inverse, owner, top, high, low, far, far_back, sent, *refs):
    received, (out, panel, upper_ref, result, sems) = refs[:-5], refs[-5:]
    rows_dev, chips = base.shape[0], sems.shape[0] - 1
    part = rows_dev // chips
    picked = picked_rows(bits, sent, received, owner)
    width = picked.shape[0]
    upper_ref[...] = dot(split(inverse[step]), split(picked))
    offset = local_rows(pivots, step, rows_dev)
    upper = split(upper_ref[...])
    displaced = split(displaced_rows(bits, received, top[...]))
    rows = far.shape[0]
    core = lax.rem(lax.axis_index("pcol"), 2)
    panel[pl.ds(pl.multiple_of(core * rows, rows), rows), :] = far[...]
    panel[pl.ds(pl.multiple_of((1 - core) * rows, rows), rows), :] = far_back[...]
    limit = (step + 1) * width - lax.axis_index("prow") * rows_dev
    copies = []
    pieces = [(turn, 0, part) for turn in range(1, chips)] + [(chips, 0, part // 2), (chips, part // 2, part // 2)]
    for turn, skip, size in pieces:
        start = pl.multiple_of(lax.rem(opposite_chip(chips) + turn, chips) * part + skip, size)
        rows = pl.ds(start, size)
        if turn < chips:
            factor = (high[rows, :], low[rows, :])
        else:
            block = panel[skip : skip + size, :]
            factor = split(jnp.where(start + iota(block.shape, 0) >= limit, -block, F32(0)))
        gather = one_hot(iota((size, width), 0) + start, offset)
        value = base[rows, :] + dot(factor, upper, gather, displaced)
        result[rows, :] = with_top(step, start, value, upper_ref)
        copies.append(pltpu.make_async_copy(result.at[rows, :], out.at[rows, :], sems.at[len(copies)]))
        copies[-1].start()
    for copy in copies:
        copy.wait()


def stack(one, other, out):
    rows = one.shape[0]
    out[:rows, :] = one[...]
    out[rows:, :] = other[...]


def pack(own, near, before, out):
    rows = own.shape[0]
    out[:rows, :] = own[...]
    out[rows:, :] = near[...]


def ring_order(chips):
    return [0] + list(range(1, chips // 2 + 1)) + list(range(chips - 1, chips // 2, -1))


def release(panel, before, out):
    out[...] = panel[...]


def shift(block, distance, count):
    return lax.ppermute(block, "pcol", [(i, (i + 2 * distance) % count) for i in range(count)])


def across(block, count):
    return lax.ppermute(block, "pcol", [(i, i ^ 1) for i in range(count)])


def forwarded(block, down, count):
    chips = count // 2
    own = [block]
    for distance in ring_order(chips)[1:]:
        if distance <= chips // 2:
            own.append(shift(own[-1], 1, count))
        else:
            own.append(shift(down if distance == chips - 1 else own[-1], -1, count))
    return own


def passed(pair, count):
    onward = [(i, (i + (2 if i % 2 == 0 else -2)) % count) for i in range(count)]
    pairs = [pair]
    for _ in range(count // 4 - 1):
        pairs.append(lax.ppermute(pairs[-1], "pcol", onward))
    return pairs[1:]


def per_device(mesh, matrix, l_panels, l_inverse, pivots):
    rows_dev, columns = matrix.shape
    steps, width = pivots.shape
    process_rows, process_columns = mesh.shape["prow"], mesh.shape["pcol"]
    bits = [1 << b for b in range(process_rows.bit_length() - 1)]
    shape = jax.ShapeDtypeStruct
    square = shape((width, columns), F32)
    full = shape((rows_dev, columns), F32)

    def call(kernel, name, operands, outs, specs=None, out_specs=None, scratch=()):
        return pl.pallas_call(
            kernel,
            out_shape=outs,
            in_specs=specs or [VMEM] * len(operands),
            out_specs=out_specs or jax.tree.map(lambda _: VMEM, outs),
            scratch_shapes=scratch,
            compiler_params=GRANT,
            cost_estimate=pl.CostEstimate(COST[name], 0, 0) if name in COST else None,
            name=name,
        )(*operands)

    def exchange(sent, step, before=()):
        received = []
        for stage in range(len(bits)):
            if stage:
                operands = [sent, received[-1], owner[step], *before]
                specs = [VMEM] * 3 + [ANY] * len(before)
                sent = call(functools.partial(merge, bits, stage - 1), "merge", operands, square, specs=specs)
            pairs = []
            for i in range(process_rows):
                for j in range(process_columns):
                    bit = bits[len(bits) - 1 - stage] if j % 2 else bits[stage]
                    pairs.append((i * process_columns + j, (i ^ bit) * process_columns + j))
            received.append(lax.ppermute(sent, ("prow", "pcol"), pairs))
        return sent, received

    chunks = rows_dev // width
    halves = [pltpu.VMEM((rows_dev, l_panels.shape[2]), BF16)] * 2
    block = shape(l_panels.shape[1:], F32)
    matrix, pivots, *own = call(
        load,
        "load",
        [pltpu.with_memory_space_constraint(x, pltpu.HBM) for x in (matrix, pivots, l_panels)],
        [full, shape(pivots.shape, pivots.dtype)] + [block] * steps,
        specs=[HBM] * 3,
        scratch=[pltpu.SemaphoreType.DMA((1 + steps + PARTS,))],
    )
    slots = call(first_slots, "first_slots", [matrix, pivots], square)

    near = across(own[1], process_columns)

    def after(panel, before, name="release"):
        return call(release, name, [panel, before], shape(panel.shape, F32), specs=[VMEM, ANY])

    indices = shape((width, columns), jnp.int32)
    owner = call(functools.partial(holders, rows_dev), "holders", [pivots], [indices] * steps)
    base, ahead, places = call(
        prepare, "prepare", [matrix, pivots], [full, square, shape((width, width), jnp.int32)]
    )
    first = forwarded(own[0], after(own[0], places, "down_block"), process_columns)
    joint = call(stack, "stack", first[:2], shape((2 * block.shape[0], block.shape[1]), F32))
    joint = across(joint, process_columns)
    first += [joint] + [across(piece, process_columns) for piece in first[2:]]
    sent, received = exchange(slots, 0, [joint])
    two = shape((2 * block.shape[0], block.shape[1]), F32)
    pair = call(pack, "pack", [own[1], near, sent], two, specs=[VMEM, VMEM, ANY])
    late = late_blocks(process_columns // 2)
    early = [piece for position, piece in enumerate(first) if position not in late]
    factor = call(functools.partial(collect, late), "collect", [places, *early], [shape((width, width), BF16)] * 2)
    operands = [matrix, pivots, l_inverse, owner[0], ahead, places, sent, *received, *factor, *[first[position] for position in late]]
    upper, displaced, slots = call(functools.partial(solve, bits, 0, late), "solve", operands, [square] * 3)
    far = shift(after(own[1], slots, "far_block"), process_columns // 4, process_columns)
    pairs = passed(pair, process_columns)
    base, top = call(
        functools.partial(update, 0),
        "update",
        [base, pivots, upper, displaced, *first],
        [full, square],
        scratch=halves,
    )
    sent, received = exchange(slots, 1, [top])
    second = [own[1], near, far, across(after(far, own[1], "far_piece"), process_columns)]
    second += pairs + [across(after(piece, sent, "pair_piece"), process_columns) for piece in pairs]
    part, depth = 2 * block.shape[0], block.shape[1]
    high, low = call(
        functools.partial(halve, 1, rows_dev, width),
        "halve",
        second[:2] + second[4:],
        [shape((rows_dev, depth), BF16)] * 2,
    )
    return call(
        functools.partial(finish, bits, 1),
        "finish",
        [base, pivots, l_inverse, owner[1], top, high, low, *second[2:4], sent, *received],
        full,
        out_specs=HBM,
        scratch=[
            pltpu.VMEM((part, depth), F32),
            pltpu.VMEM((width, columns), F32),
            pltpu.VMEM((rows_dev, columns), F32),
            pltpu.SemaphoreType.DMA((rows_dev // part + 1,)),
        ],
    )


def solution(mesh):
    placed = (P("prow", "pcol"), P(None, ("prow", "pcol"), None), P(), P())
    return jax.shard_map(
        functools.partial(per_device, mesh), mesh=mesh, in_specs=placed, out_specs=P("prow", "pcol"), check_vma=False
    )
```
